256 devices in a mesh: cal: 4 (over x_lo, core), row: 8 (over x_hi, y), col: 8 (over z).
Axes of the slice: x: 4 (x_hi: 2, x_lo: 2; x = x_hi * 2 + x_lo), y: 4, z: 8, core: 2. Of those that a mesh axis runs over, the one named last changes fastest.
Arguments:
- acts_one: bfloat16 [3072, 16384], P('cal', ('row', 'col')), may hold values from -40 to 40, as said below
- acts_two: bfloat16 [3072, 16384], P('cal', ('row', 'col')), may hold values from -40 to 40, as said below
Outputs:
- gram_reg: float32 [8, 2048, 8, 8, 256], P('row', 'cal', None, 'col')
- lead_panel: float32 [8, 2048, 512], P('row', 'cal', 'col')
The draws below stay inside these ranges and needn't reach their ends.
Inputs may be any that keep to these rules, and one draw needn't show every extreme that they name: `acts_one`: calibration activations. `acts_two`: calibration activations.
All inputs are finite; a program needn't handle non-finite values.
Results may differ from the reference program's by a relative error of at most 0.0003.
Values may be sent and summed in bfloat16 or wider, within the bound.
No kernel may reach another device: no remote copies, remote signals or barrier semaphores. Data moves between devices by JAX's collectives and lax.ppermute only.
A program may use at most 128 MiB of HBM per device.

```python
import jax
import jax.numpy as jnp
from jax import lax

W = 16384
PANEL = 512
TOKENS = 3072
PIECE = 256
N_ROW = 8
N_COL = 8


def column_scales(key):
    level = jax.random.uniform(jax.random.fold_in(key, 11), (W,), jnp.float32)
    return 0.3 * 10.0 ** level


def blend(base, scales):
    mixed = base + 0.6 * jnp.roll(base, 1, axis=1) - 0.4 * jnp.roll(base, 7, axis=1)
    return (mixed * scales[None, :]).astype(jnp.bfloat16)


def draw_acts_one(key, part):
    scales = column_scales(key)
    key = jax.random.fold_in(key, 3)
    base = jnp.clip(jax.random.normal(key, (TOKENS, W), jnp.float32), -6.0, 6.0)
    return blend(base, scales)


def draw_acts_two(key, part):
    scales = column_scales(key)
    key = jax.random.fold_in(key, 4)
    base = jnp.clip(jax.random.normal(key, (TOKENS, W), jnp.float32), -6.0, 6.0)
    return blend(base, scales)


def setup_inputs(seed: int = 0) -> dict:
    key_of = jax.random.split(jax.random.key(seed), 3)
    return {
        "acts_one": draw_acts_one(jax.random.fold_in(key_of[2], 71), 0),
        "acts_two": draw_acts_two(jax.random.fold_in(key_of[2], 71), 0),
    }


reg_alpha = 0.9

def reference(acts_one, acts_two):
    stacked = jnp.concatenate([acts_one, acts_two], axis=0).astype(jnp.float32)
    gram = jnp.dot(stacked.T, stacked, precision=lax.Precision.HIGHEST) / (2.0 * TOKENS)
    indices = jnp.arange(W, dtype=jnp.int32)
    reg = jnp.where(indices[:, None] == indices[None, :], gram, reg_alpha * gram)
    factor = jnp.linalg.cholesky(reg[:PANEL, :PANEL])
    solved = lax.linalg.triangular_solve(factor, reg[:, :PANEL], left_side=False, lower=True, transpose_a=True)
    lead = solved.at[:PANEL].set(factor)
    gram_reg = reg.reshape(N_ROW, W // N_ROW, N_ROW, N_COL, PIECE)
    return (gram_reg, lead.reshape(N_ROW, W // N_ROW, PANEL))
```

```python
import functools

import jax
import jax.numpy as jnp
import numpy as np
from jax import lax
from jax.experimental import pallas as pl
from jax.experimental.pallas import tpu as pltpu
from jax.sharding import PartitionSpec as P

PANEL = 512
reg_alpha = 0.9
AXES = ("cal", "row", "col")
NX, NY, NZ = 4, 4, 8
HIGHEST = lax.Precision.HIGHEST


def flat(x, y, z, core):
    return (((x % 2) * 2 + core) * 8 + (x // 2) * 4 + y) * 8 + z


def devices():
    for x in range(NX):
        for y in range(NY):
            for z in range(NZ):
                for core in range(2):
                    yield x, y, z, core


def move(value, target):
    pairs = []
    for device in devices():
        to = target(*device)
        if to is not None:
            pairs.append((flat(*device), flat(*to)))
    return lax.ppermute(value, AXES, sorted(pairs))


def near(i, size, phase):
    return i ^ 1 if phase == 0 else (i + 1 if i % 2 else i - 1) % size


def x_step(s):
    return lambda x, y, z, c: (near(x, NX, (s + c) % 2), y, z, c)


def y_step(s):
    return lambda x, y, z, c: (x, near(y, NY, (s + c) % 2), z, c)


def z_step(s):
    return lambda x, y, z, c: (x, y, near(z, NZ, (s + c) % 2), c)


def core_swap(x, y, z, c):
    return x, y, z, 1 - c


def row_home(x, y, z, c):
    return (x, y, z, c) if z // 4 == x % 2 else (x ^ 1, y, 7 - z, c)


def tables():
    table = np.zeros((256, 32), np.int32)
    for x, y, z, c in devices():
        def ring4(i):
            p1 = lambda v: near(v, 4, c % 2)
            p2 = lambda v: near(v, 4, (1 + c) % 2)
            return [i, p1(i), p2(i), p1(p2(i))]

        step = lambda v, s: near(v, NZ, (s + c) % 2)
        first = lambda v: [v, step(v, 0)]
        third = lambda v: first(step(step(v, 2), 1))
        slots = first(z) + first(step(z, 1)) + third(z) + third(step(z, 3))
        assert sorted(slots) == list(range(8))
        low = x % 2
        blocks = [(p if p // 4 == low else 7 - p) - 4 * low for p in slots]
        halves = [low if p // 4 == low else 1 - low for p in slots]
        table[flat(x, y, z, c)] = ring4(x) + ring4(y) + blocks + halves + [c, low] + [0] * 6
    return table


TABLE = tables()


def gram_kernel(own, meta, *refs):
    row_refs, first_refs, second_refs = refs[:5], refs[5:9], refs[9:13]
    out_ref, rows, cols, acc, row_sem, col_sem, out_sem = refs[13:]
    tokens = row_refs[0].shape[2]
    half = tokens // 2
    core = meta[24]
    wanted = core if own else 1 - core
    sizes = [r.shape[0] for r in row_refs]
    row_copies = []
    slot = 0
    for ref, size in zip(row_refs, sizes):
        for i in range(size):
            block, side = meta[8 + slot], meta[16 + slot]
            dst = rows.at[
                pl.ds(pl.multiple_of((block % 2) * 256, 256), 256),
                pl.ds(pl.multiple_of(side * tokens, tokens), tokens),
            ]
            row_copies.append(
                (block // 2 == wanted, pltpu.make_async_copy(ref.at[i], dst, row_sem.at[slot]))
            )
            slot += 1
    for want, copy in row_copies:
        pl.when(want)(copy.start)
    col_copies = []
    for j in range(4):
        group = []
        for i in range(4):
            pair = jnp.where(core == 0, i // 2, i % 2)
            side = meta[i] % 2
            for which, ref in ((0, first_refs[j].at[i]), (1, second_refs[i].at[j])):
                dst = cols.at[
                    2 * j + pair,
                    pl.ds(pl.multiple_of(side * tokens + which * half, half), half),
                ]
                copy = pltpu.make_async_copy(ref, dst, col_sem.at[j, i, which])
                copy.start()
                group.append(copy)
        col_copies.append(group)
    for want, copy in row_copies:
        pl.when(want)(copy.wait)
    out_copies = []
    for j in range(4):
        for copy in col_copies[j]:
            copy.wait()
        for pair in range(2):
            x = jnp.where(core == 0, meta[2 * pair], meta[pair])
            a = (x // 2) * 4 + meta[4 + j]
            k = 2 * j + pair
            acc[k] = jnp.dot(rows[...], cols[k], preferred_element_type=jnp.float32)
            copy = pltpu.make_async_copy(acc.at[k], out_ref.at[a], out_sem.at[k])
            copy.start()
            out_copies.append(copy)
    for copy in out_copies:
        copy.wait()


def gram_part(own, meta, row_bufs, first_bufs, second_bufs):
    tokens = row_bufs[0].shape[2]
    any_spec = pl.BlockSpec(memory_space=pl.ANY)
    return pl.pallas_call(
        functools.partial(gram_kernel, own),
        out_shape=jax.ShapeDtypeStruct((8, 512, 256), jnp.float32),
        in_specs=[pl.BlockSpec(memory_space=pltpu.SMEM)] + [any_spec] * 13,
        out_specs=any_spec,
        scratch_shapes=[
            pltpu.VMEM((512, 2 * tokens), jnp.bfloat16),
            pltpu.VMEM((8, 2 * tokens, 256), jnp.bfloat16),
            pltpu.VMEM((8, 512, 256), jnp.float32),
            pltpu.SemaphoreType.DMA((8,)),
            pltpu.SemaphoreType.DMA((4, 4, 2)),
            pltpu.SemaphoreType.DMA((8,)),
        ],
        compiler_params=pltpu.CompilerParams(vmem_limit_bytes=40 * 2**20),
        cost_estimate=pl.CostEstimate(
            flops=2 * 512 * 2048 * 2 * tokens, bytes_accessed=24 * 2**20, transcendentals=0
        ),
    )(meta, *row_bufs, *first_bufs, *second_bufs)


def finish_kernel(scale, rows, where_ref, a_ref, b_ref, out_ref):
    start = where_ref[0] + pl.program_id(0) * rows
    row_ids = start + lax.broadcasted_iota(jnp.int32, (rows, 128), 0)
    lane = lax.broadcasted_iota(jnp.int32, (rows, 128), 1)
    for a in range(8):
        for h in range(2):
            total = a_ref[a, :, h * 128:(h + 1) * 128] + b_ref[a, :, h * 128:(h + 1) * 128]
            total = total * scale
            col_ids = a * 2048 + where_ref[1] + h * 128 + lane
            value = jnp.where(row_ids == col_ids, total, reg_alpha * total)
            out_ref[pl.ds(2 * a + h, rows, stride=16), :] = value


def finish(where, mine, theirs, scale):
    rows = 128
    block = pl.BlockSpec((8, rows, 256), lambda i: (0, i, 0))
    return pl.pallas_call(
        functools.partial(finish_kernel, scale, rows),
        grid=(512 // rows,),
        out_shape=jax.ShapeDtypeStruct((512 * 16, 128), jnp.float32),
        in_specs=[pl.BlockSpec(memory_space=pltpu.SMEM), block, block],
        out_specs=pl.BlockSpec((rows * 16, 128), lambda i: (i, 0)),
        compiler_params=pltpu.CompilerParams(vmem_limit_bytes=32 * 2**20),
        cost_estimate=pl.CostEstimate(flops=2**22, bytes_accessed=12 * 2**20, transcendentals=0),
    )(where, mine, theirs)


def dot_t(a, b):
    return lax.dot_general(
        a, b, (((0,), (0,)), ((), ())), precision=HIGHEST, preferred_element_type=jnp.float32
    )


def dot_n(a, b):
    return lax.dot_general(
        a, b, (((1,), (0,)), ((), ())), precision=HIGHEST, preferred_element_type=jnp.float32
    )


def factor_kernel(scale, g_ref, u_ref, inv_ref, work, block, inv):
    n, nb, np_ = 512, 128, 8
    rid = lax.broadcasted_iota(jnp.int32, (n, n), 0)
    cid = lax.broadcasted_iota(jnp.int32, (n, n), 1)
    total = g_ref[...] * scale
    work[...] = jnp.where(rid == cid, total, reg_alpha * total)
    u_ref[...] = jnp.zeros((n, n), jnp.float32)
    inv_ref[...] = jnp.zeros((n, n), jnp.float32)
    sub = lax.broadcasted_iota(jnp.int32, (np_, nb), 0)
    lane = lax.broadcasted_iota(jnp.int32, (np_, nb), 1)
    eye = (
        lax.broadcasted_iota(jnp.int32, (nb, nb), 0) == lax.broadcasted_iota(jnp.int32, (nb, nb), 1)
    ).astype(jnp.float32)
    for k in range(n // nb):
        lo, hi = k * nb, (k + 1) * nb
        block[...] = work[lo:hi, lo:hi]
        inv[...] = eye

        def panel(p, _):
            base = pl.multiple_of(p * np_, np_)
            v = block[pl.ds(base, np_), :]
            xv = inv[pl.ds(base, np_), :]
            rolled = pltpu.roll(v, lax.rem(nb - base, nb), 1)
            pc = [jnp.broadcast_to(rolled[:, i:i + 1], (np_, nb)) for i in range(np_)]
            for i in range(np_):
                s = lax.rsqrt(pc[i][i:i + 1, :])
                u = v[i:i + 1, :] * s
                xu = xv[i:i + 1, :] * s
                below = jnp.where(sub > i, pc[i] * s, 0.0)
                here = sub == i
                for j in range(i + 1, np_):
                    pc[j] = pc[j] - below * (pc[j][i:i + 1, :] * s)
                v = jnp.where(here, u, v - below * u)
                xv = jnp.where(here, xu, xv - below * xu)
            v = jnp.where(lane >= base + sub, v, 0.0)
            block[pl.ds(base, np_), :] = v
            inv[pl.ds(base, np_), :] = xv
            later = jnp.where(lane >= base + np_, v, 0.0)
            block[...] -= dot_t(later, v)
            inv[...] -= dot_t(later, xv)
            return 0

        lax.fori_loop(0, nb // np_, panel, 0)
        x = inv[...]
        u_ref[lo:hi, lo:hi] = block[...]
        inv_ref[lo:hi, lo:hi] = x
        if k:
            inner = dot_t(u_ref[0:lo, lo:hi], inv_ref[0:lo, 0:lo])
            inv_ref[lo:hi, 0:lo] = -dot_n(x, inner)
        if hi < n:
            right = dot_n(x, work[lo:hi, hi:n])
            u_ref[lo:hi, hi:n] = right
            work[hi:n, hi:n] -= dot_t(right, right)


def factor(g, scale):
    full = pl.BlockSpec(memory_space=pltpu.VMEM)
    shape = jax.ShapeDtypeStruct((512, 512), jnp.float32)
    return pl.pallas_call(
        functools.partial(factor_kernel, scale),
        out_shape=(shape, shape),
        in_specs=[full],
        out_specs=(full, full),
        scratch_shapes=[
            pltpu.VMEM((512, 512), jnp.float32),
            pltpu.VMEM((128, 128), jnp.float32),
            pltpu.VMEM((128, 128), jnp.float32),
        ],
        compiler_params=pltpu.CompilerParams(vmem_limit_bytes=32 * 2**20),
        cost_estimate=pl.CostEstimate(flops=2**30, bytes_accessed=4 * 2**20, transcendentals=512),
    )(g)


def lead_gram(cols, z, core, row):
    other = move(cols, lambda x, y, z, c: (x, y, 1 - z, c) if (x // 2, y) == (0, 0) and z < 2 else None)
    both = jnp.where(z == 0, jnp.concatenate([cols, other], 1), jnp.concatenate([other, cols], 1))
    part = lax.dot_general(
        both, both, (((0,), (0,)), ((), ())), preferred_element_type=jnp.float32
    )
    part = part.reshape(2, 256, 512)
    mine = lax.dynamic_index_in_dim(part, core, 0, keepdims=False)
    away = lax.dynamic_index_in_dim(part, 1 - core, 0, keepdims=False)
    lead = lambda x, y, z: (x // 2, y) == (0, 0) and z < 2
    mine = mine + move(away, lambda x, y, z, c: (x, y, z, 1 - c) if lead(x, y, z) else None)
    mine = mine + move(mine, lambda x, y, z, c: (x ^ 1, y, z, c) if lead(x, y, z) else None)
    mine = jnp.where(row == 0, mine, 0.0)
    mine = mine + move(mine, lambda x, y, z, c: (x + 2, y, z, c) if lead(x, y, z) else None)
    edge = lambda y, z: y == 0 and z < 2
    sent = [
        move(mine, lambda x, y, z, c, to=to: (x, to, z, c) if edge(y, z) else None) for to in (1, 3, 2)
    ]
    mine = mine + (sent[0] + sent[1] + sent[2])
    theirs = move(mine, lambda x, y, z, c: (x, y, z, 1 - c) if z < 2 else None)
    return jnp.where(
        core == 0, jnp.concatenate([mine, theirs], 0), jnp.concatenate([theirs, mine], 0)
    )


def per_device(acts_one, acts_two):
    cal, row, z = (lax.axis_index(a) for a in AXES)
    core = cal % 2
    total_tokens = 8 * acts_one.shape[0]
    scale = 1.0 / total_tokens
    device = (cal * 8 + row) * 8 + z
    meta = lax.dynamic_index_in_dim(jnp.asarray(TABLE), device, 0, keepdims=False)

    lead = lead_gram(jnp.concatenate([acts_one, acts_two], 0), z, core, row)
    upper, inverse = factor(lead, scale)

    piece = jnp.concatenate([acts_one.T, acts_two.T], 1)[None]
    r0 = move(piece, row_home)
    r1 = move(r0, z_step(0))
    r2 = move(jnp.concatenate([r0, r1], 0), z_step(1))
    r3 = move(r2, z_step(2))
    r4 = move(r3, z_step(3))
    row_bufs = (r0, r1, r2, r3, r4)

    def ring(value, step):
        one = move(value, step(0))
        return value, one, move(value, step(1)), move(one, step(1))

    first = jnp.concatenate(ring(acts_one[None], x_step), 0)
    second = jnp.concatenate(ring(acts_two[None], y_step), 0)
    first_bufs = ring(first, y_step)
    second_bufs = ring(second, x_step)

    theirs = gram_part(False, meta, row_bufs, first_bufs, second_bufs)
    mine = gram_part(True, meta, row_bufs, first_bufs, second_bufs)
    theirs = move(theirs, core_swap)

    row_start = row * 2048 + cal * 512
    where = jnp.stack([row_start, z * 256]).astype(jnp.int32)
    gram_reg = finish(where, mine, theirs, scale)

    block = (mine[0] + theirs[0]) * scale
    row_ids = row_start + jnp.arange(512, dtype=jnp.int32)[:, None]
    col_ids = z * 256 + jnp.arange(256, dtype=jnp.int32)[None, :]
    block = jnp.where(row_ids == col_ids, block, reg_alpha * block)
    weights = jnp.where(z == 0, inverse[:, :256], inverse[:, 256:])
    solved = lax.dot_general(
        weights, block, (((1,), (1,)), ((), ())), precision=HIGHEST,
        preferred_element_type=jnp.float32,
    )
    head = jnp.where(z == 0, upper, 0.0)
    solved = jnp.where((row == 0) & (cal == 0), head, solved).reshape(8, 64, 512)
    share = jnp.where(z == 0, solved[0], 0.0)
    for to in range(1, 8):
        extra = to + 3 if to < 5 else None

        def target(x, y, z, c, to=to, extra=extra):
            if z == 0:
                return x, y, to, c
            return (x, y, extra, c) if z == 1 and extra is not None else None

        value = solved[to] if extra is None else jnp.where(z == 0, solved[to], solved[extra])
        share = share + move(value, target)
    return gram_reg.reshape(1, 512, 8, 1, 256), share.T.reshape(1, 512, 64)


def solution(mesh):
    return jax.shard_map(
        per_device,
        mesh=mesh,
        in_specs=(P("cal", ("row", "col")), P("cal", ("row", "col"))),
        out_specs=(P("row", "cal", None, "col", None), P("row", "cal", "col")),
        check_vma=False,
    )
```

```python
import functools

import jax
import jax.numpy as jnp
import numpy as np
from jax import lax
from jax.experimental import pallas as pl
from jax.experimental.pallas import tpu as pltpu
from jax.sharding import PartitionSpec as P

PANEL = 512
reg_alpha = 0.9
AXES = ("cal", "row", "col")
NX, NY, NZ = 4, 4, 8
HIGHEST = lax.Precision.HIGHEST


def flat(x, y, z, core):
    return (((x % 2) * 2 + core) * 8 + (x // 2) * 4 + y) * 8 + z


def devices():
    for x in range(NX):
        for y in range(NY):
            for z in range(NZ):
                for core in range(2):
                    yield x, y, z, core


def move(value, target):
    pairs = []
    for device in devices():
        to = target(*device)
        if to is not None:
            pairs.append((flat(*device), flat(*to)))
    return lax.ppermute(value, AXES, sorted(pairs))


def near(i, size, phase):
    return i ^ 1 if phase == 0 else (i + 1 if i % 2 else i - 1) % size


def x_step(s):
    return lambda x, y, z, c: (near(x, NX, (s + c) % 2), y, z, c)


def y_step(s):
    return lambda x, y, z, c: (x, near(y, NY, (s + c) % 2), z, c)


def z_step(s):
    return lambda x, y, z, c: (x, y, near(z, NZ, (s + c) % 2), c)


def core_swap(x, y, z, c):
    return x, y, z, 1 - c


def row_home(x, y, z, c):
    return (x, y, z, c) if z // 4 == x % 2 else (x ^ 1, y, 7 - z, c)


def tables():
    table = np.zeros((256, 32), np.int32)
    for x, y, z, c in devices():
        def ring4(i):
            p1 = lambda v: near(v, 4, c % 2)
            p2 = lambda v: near(v, 4, (1 + c) % 2)
            return [i, p1(i), p2(i), p1(p2(i))]

        step = lambda v, s: near(v, NZ, (s + c) % 2)
        first = lambda v: [v, step(v, 0)]
        third = lambda v: first(step(step(v, 2), 1))
        slots = first(z) + first(step(z, 1)) + third(z) + third(step(z, 3))
        assert sorted(slots) == list(range(8))
        low = x % 2
        blocks = [(p if p // 4 == low else 7 - p) - 4 * low for p in slots]
        halves = [low if p // 4 == low else 1 - low for p in slots]
        table[flat(x, y, z, c)] = ring4(x) + ring4(y) + blocks + halves + [c, low] + [0] * 6
    return table


TABLE = tables()


def start_rows(meta, wanted, row_refs, rows, sem):
    tokens = row_refs[0].shape[2]
    copies = []
    for ref in row_refs:
        for i in range(ref.shape[0]):
            slot = len(copies)
            block, side = meta[8 + slot], meta[16 + slot]
            dst = rows.at[
                pl.ds(pl.multiple_of((block % 2) * 256, 256), 256),
                pl.ds(pl.multiple_of(side * tokens, tokens), tokens),
            ]
            copy = pltpu.make_async_copy(ref.at[i], dst, sem.at[slot])
            copies.append((block // 2 == wanted, copy))
    for want, copy in copies:
        pl.when(want)(copy.start)

    def wait():
        for want, copy in copies:
            pl.when(want)(copy.wait)

    return wait


def gram_kernel(own, scale, *refs):
    meta, refs = refs[0], refs[1:]
    row_refs, first_refs, second_refs, refs = refs[:5], refs[5:9], refs[9:13], refs[13:]
    if own:
        other_ref, out_ref, rows, cols, other, row_sem, col_sem, sem = refs
    else:
        out_ref, rows, cols, other, row_sem, col_sem, sem = refs
    tokens = row_refs[0].shape[2]
    half = tokens // 2
    core = meta[24]
    wait_rows = start_rows(meta, core if own else 1 - core, row_refs, rows, row_sem)

    def column(j, pair):
        x = jnp.where(core == 0, meta[2 * pair], meta[pair])
        return (x // 2) * 4 + meta[4 + j]

    col_copies = []
    for j in range(4):
        group = []
        for i in range(4):
            pair = jnp.where(core == 0, i // 2, i % 2)
            side = meta[i] % 2
            for which, ref in ((0, first_refs[j].at[i]), (1, second_refs[i].at[j])):
                dst = cols.at[
                    2 * j + pair,
                    pl.ds(pl.multiple_of(side * tokens + which * half, half), half),
                ]
                copy = pltpu.make_async_copy(ref, dst, col_sem.at[j, i, which])
                copy.start()
                group.append(copy)
        if own:
            for pair in range(2):
                k = 2 * j + pair
                copy = pltpu.make_async_copy(other_ref.at[column(j, pair)], other.at[k], sem.at[k])
                copy.start()
                group.append(copy)
        col_copies.append(group)
    wait_rows()
    out_copies = []
    row_ids = meta[25] + lax.broadcasted_iota(jnp.int32, (512, 128), 0)
    lane = meta[26] + lax.broadcasted_iota(jnp.int32, (512, 128), 1)
    for j in range(4):
        for copy in col_copies[j]:
            copy.wait()
        for pair in range(2):
            a = column(j, pair)
            k = 2 * j + pair
            total = jnp.dot(rows[...], cols[k], preferred_element_type=jnp.float32)
            if own:
                for h in range(2):
                    part = total[:, h * 128:(h + 1) * 128] + other[k, :, h * 128:(h + 1) * 128]
                    part = part * scale
                    same = row_ids == lane + (a * 2048 + h * 128)
                    out_ref[pl.ds(2 * a + h, 512, stride=16), :] = jnp.where(
                        same, part, reg_alpha * part
                    )
            else:
                other[k] = total
                copy = pltpu.make_async_copy(other.at[k], out_ref.at[a], sem.at[k])
                copy.start()
                out_copies.append(copy)
    for copy in out_copies:
        copy.wait()


def gram_part(scale, meta, row_bufs, first_bufs, second_bufs, other=None):
    own = other is not None
    tokens = row_bufs[0].shape[2]
    any_spec = pl.BlockSpec(memory_space=pl.ANY)
    shape = (512 * 16, 128) if own else (8, 512, 256)
    return pl.pallas_call(
        functools.partial(gram_kernel, own, scale),
        out_shape=jax.ShapeDtypeStruct(shape, jnp.float32),
        in_specs=[pl.BlockSpec(memory_space=pltpu.SMEM)] + [any_spec] * (13 + own),
        out_specs=pl.BlockSpec(memory_space=pltpu.VMEM) if own else any_spec,
        scratch_shapes=[
            pltpu.VMEM((512, 2 * tokens), jnp.bfloat16),
            pltpu.VMEM((8, 2 * tokens, 256), jnp.bfloat16),
            pltpu.VMEM((8, 512, 256), jnp.float32),
            pltpu.SemaphoreType.DMA((8,)),
            pltpu.SemaphoreType.DMA((4, 4, 2)),
            pltpu.SemaphoreType.DMA((8,)),
        ],
        compiler_params=pltpu.CompilerParams(vmem_limit_bytes=40 * 2**20),
        cost_estimate=pl.CostEstimate(
            flops=2 * 512 * 2048 * 2 * tokens, bytes_accessed=24 * 2**20, transcendentals=0
        ),
    )(meta, *row_bufs, *first_bufs, *second_bufs, *([other] if own else []))


def lead_kernel(*refs):
    meta, refs = refs[0], refs[1:]
    row_refs, first_refs, second_refs = refs[:5], refs[5:9], refs[9:13]
    out_ref, rows, cols, row_sem, col_sem = refs[13:]
    tokens = row_refs[0].shape[2]
    half = tokens // 2
    wait_rows = start_rows(meta, meta[24], row_refs, rows, row_sem)
    copies = []
    for j in range(4):
        for i in range(4):
            want = (meta[i] // 2 == 0) & (meta[4 + j] == 0)
            side = meta[i] % 2
            for which, ref in ((0, first_refs[j].at[i]), (1, second_refs[i].at[j])):
                dst = cols.at[pl.ds(pl.multiple_of(side * tokens + which * half, half), half)]
                copies.append((want, pltpu.make_async_copy(ref, dst, col_sem.at[j, i, which])))
    for want, copy in copies:
        pl.when(want)(copy.start)
    wait_rows()
    for want, copy in copies:
        pl.when(want)(copy.wait)
    out_ref[...] = jnp.dot(rows[...], cols[...], preferred_element_type=jnp.float32)


def lead_part(meta, row_bufs, first_bufs, second_bufs):
    tokens = row_bufs[0].shape[2]
    any_spec = pl.BlockSpec(memory_space=pl.ANY)
    return pl.pallas_call(
        lead_kernel,
        out_shape=jax.ShapeDtypeStruct((512, 256), jnp.float32),
        in_specs=[pl.BlockSpec(memory_space=pltpu.SMEM)] + [any_spec] * 13,
        out_specs=pl.BlockSpec(memory_space=pltpu.VMEM),
        scratch_shapes=[
            pltpu.VMEM((512, 2 * tokens), jnp.bfloat16),
            pltpu.VMEM((2 * tokens, 256), jnp.bfloat16),
            pltpu.SemaphoreType.DMA((8,)),
            pltpu.SemaphoreType.DMA((4, 4, 2)),
        ],
        compiler_params=pltpu.CompilerParams(vmem_limit_bytes=40 * 2**20),
        cost_estimate=pl.CostEstimate(
            flops=2 * 512 * 256 * 2 * tokens, bytes_accessed=5 * 2**20, transcendentals=0
        ),
    )(meta, *row_bufs, *first_bufs, *second_bufs)


def dot_t(a, b):
    return lax.dot_general(
        a, b, (((0,), (0,)), ((), ())), precision=HIGHEST, preferred_element_type=jnp.float32
    )


def dot_n(a, b):
    return lax.dot_general(
        a, b, (((1,), (0,)), ((), ())), precision=HIGHEST, preferred_element_type=jnp.float32
    )


def factor_kernel(k, work_ref, u_in, inv_in, work, u_ref, inv_ref, block, inv):
    n, nb, np_ = 512, 128, 8
    sub = lax.broadcasted_iota(jnp.int32, (np_, nb), 0)
    lane = lax.broadcasted_iota(jnp.int32, (np_, nb), 1)
    eye = (
        lax.broadcasted_iota(jnp.int32, (nb, nb), 0) == lax.broadcasted_iota(jnp.int32, (nb, nb), 1)
    ).astype(jnp.float32)
    lo, hi = k * nb, (k + 1) * nb
    work[...] = work_ref[...]
    u_ref[...] = u_in[...]
    inv_ref[...] = inv_in[...]
    block[...] = work[lo:hi, lo:hi]
    inv[...] = eye

    def panel(p, _):
        base = pl.multiple_of(p * np_, np_)
        v = block[pl.ds(base, np_), :]
        xv = inv[pl.ds(base, np_), :]
        rolled = pltpu.roll(v, lax.rem(nb - base, nb), 1)
        pc = [jnp.broadcast_to(rolled[:, i:i + 1], (np_, nb)) for i in range(np_)]
        for i in range(np_):
            s = lax.rsqrt(pc[i][i:i + 1, :])
            u = v[i:i + 1, :] * s
            xu = xv[i:i + 1, :] * s
            below = jnp.where(sub > i, pc[i] * s, 0.0)
            here = sub == i
            for j in range(i + 1, np_):
                pc[j] = pc[j] - below * (pc[j][i:i + 1, :] * s)
            v = jnp.where(here, u, v - below * u)
            xv = jnp.where(here, xu, xv - below * xu)
        v = jnp.where(lane >= base + sub, v, 0.0)
        block[pl.ds(base, np_), :] = v
        inv[pl.ds(base, np_), :] = xv
        later = jnp.where(lane >= base + np_, v, 0.0)
        block[...] -= dot_t(later, v)
        inv[...] -= dot_t(later, xv)
        return 0

    lax.fori_loop(0, nb // np_, panel, 0)
    x = inv[...]
    u_ref[lo:hi, lo:hi] = block[...]
    inv_ref[lo:hi, lo:hi] = x
    if k:
        inner = dot_t(u_ref[0:lo, lo:hi], inv_ref[0:lo, 0:lo])
        inv_ref[lo:hi, 0:lo] = -dot_n(x, inner)
    if hi < n:
        right = dot_n(x, work[lo:hi, hi:n])
        u_ref[lo:hi, hi:n] = right
        work[hi:n, hi:n] -= dot_t(right, right)


def factor_part(k, work, upper, inverse):
    full = pl.BlockSpec(memory_space=pltpu.VMEM)
    shape = jax.ShapeDtypeStruct((512, 512), jnp.float32)
    return pl.pallas_call(
        functools.partial(factor_kernel, k),
        out_shape=(shape,) * 3,
        in_specs=[full] * 3,
        out_specs=(full,) * 3,
        scratch_shapes=[
            pltpu.VMEM((128, 128), jnp.float32),
            pltpu.VMEM((128, 128), jnp.float32),
        ],
        compiler_params=pltpu.CompilerParams(vmem_limit_bytes=32 * 2**20),
        cost_estimate=pl.CostEstimate(flops=2**33, bytes_accessed=6 * 2**20, transcendentals=512),
    )(work, upper, inverse)


def per_device(acts_one, acts_two):
    cal, row, z = (lax.axis_index(a) for a in AXES)
    core = cal % 2
    total_tokens = 8 * acts_one.shape[0]
    scale = 1.0 / total_tokens
    device = (cal * 8 + row) * 8 + z
    meta = lax.dynamic_index_in_dim(jnp.asarray(TABLE), device, 0, keepdims=False)
    after = lax.optimization_barrier
    root = lambda x, y, z: (x // 2, y) == (0, 0) and z < 2

    cols = jnp.concatenate([acts_one, acts_two], 0)
    one_t, two_t = acts_one.T, acts_two.T
    a0, b0 = acts_one[None], acts_two[None]
    one_t = move(one_t, row_home)
    a1 = move(a0, x_step(0))
    b1 = move(b0, y_step(0))
    other = move(cols, lambda x, y, z, c: (x, y, 1 - z, c) if root(x, y, z) else None)
    one_t, a1, b1, other, two_t = after((one_t, a1, b1, other, two_t))

    middle = two_t.shape[1] // 2
    q3 = move(two_t[:, :middle], row_home)
    left, right = jnp.where(z == 0, cols, other), jnp.where(z == 0, other, cols)
    part = [
        lax.dot_general(p, q, (((0,), (0,)), ((), ())), preferred_element_type=jnp.float32)
        for p, q in ((left, left), (left, right), (right, right))
    ]
    part = jnp.concatenate(part, 0).reshape(2, 384, 256)
    lead = lax.dynamic_index_in_dim(part, core, 0, keepdims=False)
    away = lax.dynamic_index_in_dim(part, 1 - core, 0, keepdims=False)
    lead = lead + move(away, lambda x, y, z, c: (x, y, z, 1 - c) if root(x, y, z) else None)
    q3, lead, one_t, two_t, a1, b1 = after((q3, lead, one_t, two_t, a1, b1))

    q4 = move(two_t[:, middle:], row_home)
    a01 = jnp.concatenate([a0, a1], 0)
    b01 = jnp.concatenate([b0, b1], 0)
    a23 = move(a01, x_step(1))
    b23 = move(b01, y_step(1))
    lead = lead + move(lead, lambda x, y, z, c: (x ^ 1, y, z, c) if root(x, y, z) else None)
    lead = jnp.where(row == 0, lead, 0.0)
    q3, q4, lead, one_t, a01, a23, b01, b23 = after((q3, q4, lead, one_t, a01, a23, b01, b23))

    r0 = jnp.concatenate([one_t, q3, q4], 1)[None]
    r1 = move(r0, z_step(0))
    first = jnp.concatenate([a01, a23], 0)
    second = jnp.concatenate([b01, b23], 0)
    lead = lead + move(lead, lambda x, y, z, c: (x + 2, y, z, c) if root(x, y, z) else None)
    lead = lead + move(lead, lambda x, y, z, c: (x, 1, z, c) if y == 0 and z < 2 else None)
    r0, r1, first, second, lead = after((r0, r1, first, second, lead))

    r2 = move(jnp.concatenate([r0, r1], 0), z_step(1))
    first1 = move(first, y_step(0))
    second1 = move(second, x_step(0))
    lead = lead + move(lead, lambda x, y, z, c: (x, 3 - y, z, c) if y < 2 and z < 2 else None)
    theirs = move(lead, lambda x, y, z, c: (x, y, z, 1 - c) if z < 2 else None)
    r0, r1, r2, first, first1, second, second1, lead, theirs = after(
        (r0, r1, r2, first, first1, second, second1, lead, theirs)
    )

    r3 = move(r2, z_step(2))
    first2 = move(first, y_step(1))
    second2 = move(second, x_step(1))
    low = jnp.where(core == 0, lead, theirs)
    high = jnp.where(core == 0, theirs, lead)
    corner = jnp.concatenate([low[256:], high[:128]], 0)
    gram = jnp.concatenate(
        [
            jnp.concatenate([low[:256], corner], 1),
            jnp.concatenate([corner.T, high[128:]], 1),
        ],
        0,
    ) * scale
    ids = jnp.arange(512, dtype=jnp.int32)
    work = jnp.where(ids[:, None] == ids[None, :], gram, reg_alpha * gram)
    zeros = jnp.zeros((512, 512), jnp.float32)
    state = factor_part(0, work, zeros, zeros)
    state = factor_part(1, *state)
    r0, r1, r2, r3, first, first1, first2, second, second1, second2, state = after(
        (r0, r1, r2, r3, first, first1, first2, second, second1, second2, state)
    )

    r4 = move(r3, z_step(3))
    first3 = move(first1, y_step(1))
    second3 = move(second1, x_step(1))
    state = factor_part(2, *state)
    _, upper, inverse = factor_part(3, *state)
    r0, r1, r2, r3, r4, first, first1, first2, first3, second, second1, second2, second3, upper, inverse = after(
        (r0, r1, r2, r3, r4, first, first1, first2, first3, second, second1, second2, second3, upper, inverse)
    )

    pieces = (
        (r0, r1, r2, r3, r4),
        (first, first1, first2, first3),
        (second, second1, second2, second3),
    )
    row_start = row * 2048 + cal * 512
    meta = meta.at[25].set(row_start).at[26].set(z * 256)
    theirs = gram_part(scale, meta, *pieces)
    theirs_lead = move(theirs[0], core_swap)
    theirs = move(theirs, core_swap)

    block = (lead_part(meta, *pieces) + theirs_lead) * scale
    row_ids = row_start + jnp.arange(512, dtype=jnp.int32)[:, None]
    col_ids = z * 256 + jnp.arange(256, dtype=jnp.int32)[None, :]
    block = jnp.where(row_ids == col_ids, block, reg_alpha * block)
    weights = jnp.where(z == 0, inverse[:, :256], inverse[:, 256:])
    solved = lax.dot_general(
        weights, block, (((1,), (1,)), ((), ())), precision=HIGHEST,
        preferred_element_type=jnp.float32,
    )
    head = jnp.where(z == 0, upper, 0.0)
    solved = jnp.where((row == 0) & (cal == 0), head, solved).reshape(8, 64, 512)
    share = jnp.where(z == 0, solved[0], 0.0)
    for to in range(1, 8):
        extra = to + 3 if to < 5 else None

        def target(x, y, z, c, to=to, extra=extra):
            if z == 0:
                return x, y, to, c
            return (x, y, extra, c) if z == 1 and extra is not None else None

        value = solved[to] if extra is None else jnp.where(z == 0, solved[to], solved[extra])
        share = share + move(value, target)

    gram_reg = gram_part(scale, meta, *pieces, other=theirs)
    return gram_reg.reshape(1, 512, 8, 1, 256), share.T.reshape(1, 512, 64)


def solution(mesh):
    return jax.shard_map(
        per_device,
        mesh=mesh,
        in_specs=(P("cal", ("row", "col")), P("cal", ("row", "col"))),
        out_specs=(P("row", "cal", None, "col", None), P("row", "cal", "col")),
        check_vma=False,
    )
```

```python
import functools

import jax
import jax.numpy as jnp
import numpy as np
from jax import lax
from jax.experimental import pallas as pl
from jax.experimental.pallas import tpu as pltpu
from jax.sharding import PartitionSpec as P

PANEL = 512
reg_alpha = 0.9
AXES = ("cal", "row", "col")
NX, NY, NZ = 4, 4, 8
HIGHEST = lax.Precision.HIGHEST


def flat(x, y, z, core):
    return (((x % 2) * 2 + core) * 8 + (x // 2) * 4 + y) * 8 + z


def devices():
    for x in range(NX):
        for y in range(NY):
            for z in range(NZ):
                for core in range(2):
                    yield x, y, z, core


def move(value, target):
    pairs = []
    for device in devices():
        to = target(*device)
        if to is not None:
            pairs.append((flat(*device), flat(*to)))
    return lax.ppermute(value, AXES, sorted(pairs))


def near(i, size, phase):
    return i ^ 1 if phase == 0 else (i + 1 if i % 2 else i - 1) % size


def x_step(s):
    return lambda x, y, z, c: (near(x, NX, (s + c) % 2), y, z, c)


def y_step(s):
    return lambda x, y, z, c: (x, near(y, NY, (s + c) % 2), z, c)


def z_step(s):
    return lambda x, y, z, c: (x, y, near(z, NZ, (s + c) % 2), c)


def core_swap(x, y, z, c):
    return x, y, z, 1 - c


def row_home(x, y, z, c):
    return (x, y, z, c) if z // 4 == x % 2 else (x ^ 1, y, 7 - z, c)


def tables():
    table = np.zeros((256, 32), np.int32)
    for x, y, z, c in devices():
        def ring4(i):
            p1 = lambda v: near(v, 4, c % 2)
            p2 = lambda v: near(v, 4, (1 + c) % 2)
            return [i, p1(i), p2(i), p1(p2(i))]

        step = lambda v, s: near(v, NZ, (s + c) % 2)
        first = lambda v: [v, step(v, 0)]
        third = lambda v: first(step(step(v, 2), 1))
        slots = first(z) + first(step(z, 1)) + third(z) + third(step(z, 3))
        assert sorted(slots) == list(range(8))
        low = x % 2
        blocks = [(p if p // 4 == low else 7 - p) - 4 * low for p in slots]
        halves = [low if p // 4 == low else 1 - low for p in slots]
        table[flat(x, y, z, c)] = ring4(x) + ring4(y) + blocks + halves + [c, low] + [0] * 6
    return table


TABLE = tables()


def start_rows(meta, wanted, row_refs, rows, sem):
    tokens = row_refs[0].shape[2]
    copies = []
    for ref in row_refs:
        for i in range(ref.shape[0]):
            slot = len(copies)
            block, side = meta[8 + slot], meta[16 + slot]
            dst = rows.at[
                pl.ds(pl.multiple_of((block % 2) * 256, 256), 256),
                pl.ds(pl.multiple_of(side * tokens, tokens), tokens),
            ]
            copy = pltpu.make_async_copy(ref.at[i], dst, sem.at[slot])
            copies.append((block // 2 == wanted, copy))
    for want, copy in copies:
        pl.when(want)(copy.start)

    def wait():
        for want, copy in copies:
            pl.when(want)(copy.wait)

    return wait


def gram_kernel(own, scale, *refs):
    meta, refs = refs[0], refs[1:]
    row_refs, first_refs, second_refs, refs = refs[:4], refs[4:8], refs[8:12], refs[12:]
    if own:
        other_ref, out_ref, rows, cols, other, row_sem, col_sem, sem = refs
    else:
        out_ref, rows, cols, other, row_sem, col_sem, sem = refs
    tokens = row_refs[0].shape[2]
    half = tokens // 2
    core = meta[24]
    wait_rows = start_rows(meta, core if own else 1 - core, row_refs, rows, row_sem)

    def column(j, pair):
        x = jnp.where(core == 0, meta[2 * pair], meta[pair])
        return (x // 2) * 4 + meta[4 + j]

    col_copies = []
    for j in range(4):
        group = []
        for i in range(4):
            pair = jnp.where(core == 0, i // 2, i % 2)
            side = meta[i] % 2
            for which, ref in ((0, first_refs[j].at[i]), (1, second_refs[i].at[j])):
                dst = cols.at[
                    2 * j + pair,
                    pl.ds(pl.multiple_of(side * tokens + which * half, half), half),
                ]
                copy = pltpu.make_async_copy(ref, dst, col_sem.at[j, i, which])
                copy.start()
                group.append(copy)
        if own:
            for pair in range(2):
                k = 2 * j + pair
                copy = pltpu.make_async_copy(other_ref.at[column(j, pair)], other.at[k], sem.at[k])
                copy.start()
                group.append(copy)
        col_copies.append(group)
    wait_rows()
    out_copies = []
    row_ids = meta[25] + lax.broadcasted_iota(jnp.int32, (512, 128), 0)
    lane = meta[26] + lax.broadcasted_iota(jnp.int32, (512, 128), 1)
    for j in range(4):
        for copy in col_copies[j]:
            copy.wait()
        for pair in range(2):
            a = column(j, pair)
            k = 2 * j + pair
            total = jnp.dot(rows[...], cols[k], preferred_element_type=jnp.float32)
            if own:
                for h in range(2):
                    part = total[:, h * 128:(h + 1) * 128] + other[k, :, h * 128:(h + 1) * 128]
                    part = part * scale
                    same = row_ids == lane + (a * 2048 + h * 128)
                    out_ref[pl.ds(2 * a + h, 512, stride=16), :] = jnp.where(
                        same, part, reg_alpha * part
                    )
            else:
                other[k] = total
                copy = pltpu.make_async_copy(other.at[k], out_ref.at[a], sem.at[k])
                copy.start()
                out_copies.append(copy)
    for copy in out_copies:
        copy.wait()


def gram_part(scale, meta, row_bufs, first_bufs, second_bufs, other=None):
    own = other is not None
    tokens = row_bufs[0].shape[2]
    any_spec = pl.BlockSpec(memory_space=pl.ANY)
    shape = (512 * 16, 128) if own else (8, 512, 256)
    return pl.pallas_call(
        functools.partial(gram_kernel, own, scale),
        out_shape=jax.ShapeDtypeStruct(shape, jnp.float32),
        in_specs=[pl.BlockSpec(memory_space=pltpu.SMEM)] + [any_spec] * (12 + own),
        out_specs=pl.BlockSpec(memory_space=pltpu.VMEM) if own else any_spec,
        scratch_shapes=[
            pltpu.VMEM((512, 2 * tokens), jnp.bfloat16),
            pltpu.VMEM((8, 2 * tokens, 256), jnp.bfloat16),
            pltpu.VMEM((8, 512, 256), jnp.float32),
            pltpu.SemaphoreType.DMA((8,)),
            pltpu.SemaphoreType.DMA((4, 4, 2)),
            pltpu.SemaphoreType.DMA((8,)),
        ],
        compiler_params=pltpu.CompilerParams(vmem_limit_bytes=62 * 2**20),
        cost_estimate=pl.CostEstimate(
            flops=2 * 512 * 2048 * 2 * tokens, bytes_accessed=24 * 2**20, transcendentals=0
        ),
    )(meta, *row_bufs, *first_bufs, *second_bufs, *([other] if own else []))


def lead_kernel(*refs):
    meta, refs = refs[0], refs[1:]
    row_refs, first_refs, second_refs = refs[:4], refs[4:8], refs[8:12]
    own_ref, away_ref, rows, cols, row_sem, col_sem = refs[12:]
    tokens = row_refs[0].shape[2]
    half = tokens // 2
    copies = []
    for ref in row_refs:
        for i in range(ref.shape[0]):
            slot = len(copies)
            block, side = meta[8 + slot], meta[16 + slot]
            at = jnp.where(block // 2 == meta[24], 0, 512) + (block % 2) * 256
            dst = rows.at[
                pl.ds(pl.multiple_of(at, 256), 256),
                pl.ds(pl.multiple_of(side * tokens, tokens), tokens),
            ]
            copies.append((True, pltpu.make_async_copy(ref.at[i], dst, row_sem.at[slot])))
    for j in range(4):
        for i in range(4):
            want = (meta[i] // 2 == 0) & (meta[4 + j] == 0)
            side = meta[i] % 2
            for which, ref in ((0, first_refs[j].at[i]), (1, second_refs[i].at[j])):
                dst = cols.at[pl.ds(pl.multiple_of(side * tokens + which * half, half), half)]
                copies.append((want, pltpu.make_async_copy(ref, dst, col_sem.at[j, i, which])))
    for want, copy in copies:
        pl.when(want)(copy.start)
    for want, copy in copies:
        pl.when(want)(copy.wait)
    own_ref[...] = jnp.dot(rows[:512], cols[...], preferred_element_type=jnp.float32)
    away_ref[...] = jnp.dot(rows[512:], cols[...], preferred_element_type=jnp.float32)


def lead_part(meta, row_bufs, first_bufs, second_bufs):
    tokens = row_bufs[0].shape[2]
    any_spec = pl.BlockSpec(memory_space=pl.ANY)
    vmem = pl.BlockSpec(memory_space=pltpu.VMEM)
    return pl.pallas_call(
        lead_kernel,
        out_shape=(jax.ShapeDtypeStruct((512, 256), jnp.float32),) * 2,
        in_specs=[pl.BlockSpec(memory_space=pltpu.SMEM)] + [any_spec] * 12,
        out_specs=(vmem, vmem),
        scratch_shapes=[
            pltpu.VMEM((1024, 2 * tokens), jnp.bfloat16),
            pltpu.VMEM((2 * tokens, 256), jnp.bfloat16),
            pltpu.SemaphoreType.DMA((8,)),
            pltpu.SemaphoreType.DMA((4, 4, 2)),
        ],
        compiler_params=pltpu.CompilerParams(vmem_limit_bytes=62 * 2**20),
        cost_estimate=pl.CostEstimate(
            flops=4 * 512 * 256 * 2 * tokens, bytes_accessed=9 * 2**20, transcendentals=0
        ),
    )(meta, *row_bufs, *first_bufs, *second_bufs)


def dot_t(a, b):
    return lax.dot_general(
        a, b, (((0,), (0,)), ((), ())), precision=HIGHEST, preferred_element_type=jnp.float32
    )


def dot_n(a, b):
    return lax.dot_general(
        a, b, (((1,), (0,)), ((), ())), precision=HIGHEST, preferred_element_type=jnp.float32
    )


def factor_kernel(k, work_ref, u_in, inv_in, work, u_ref, inv_ref, block, inv):
    n, nb, np_ = 512, 128, 8
    sub = lax.broadcasted_iota(jnp.int32, (np_, nb), 0)
    lane = lax.broadcasted_iota(jnp.int32, (np_, nb), 1)
    eye = (
        lax.broadcasted_iota(jnp.int32, (nb, nb), 0) == lax.broadcasted_iota(jnp.int32, (nb, nb), 1)
    ).astype(jnp.float32)
    lo, hi = k * nb, (k + 1) * nb
    work[...] = work_ref[...]
    u_ref[...] = u_in[...]
    inv_ref[...] = inv_in[...]
    block[...] = work[lo:hi, lo:hi]
    inv[...] = eye

    def panel(p, _):
        base = pl.multiple_of(p * np_, np_)
        v = block[pl.ds(base, np_), :]
        xv = inv[pl.ds(base, np_), :]
        rolled = pltpu.roll(v, lax.rem(nb - base, nb), 1)
        pc = [jnp.broadcast_to(rolled[:, i:i + 1], (np_, nb)) for i in range(np_)]
        for i in range(np_):
            s = lax.rsqrt(pc[i][i:i + 1, :])
            u = v[i:i + 1, :] * s
            xu = xv[i:i + 1, :] * s
            below = jnp.where(sub > i, pc[i] * s, 0.0)
            here = sub == i
            for j in range(i + 1, np_):
                pc[j] = pc[j] - below * (pc[j][i:i + 1, :] * s)
            v = jnp.where(here, u, v - below * u)
            xv = jnp.where(here, xu, xv - below * xu)
        v = jnp.where(lane >= base + sub, v, 0.0)
        block[pl.ds(base, np_), :] = v
        inv[pl.ds(base, np_), :] = xv
        later = jnp.where(lane >= base + np_, v, 0.0)
        block[...] -= dot_t(later, v)
        inv[...] -= dot_t(later, xv)
        return 0

    lax.fori_loop(0, nb // np_, panel, 0)
    x = inv[...]
    u_ref[lo:hi, lo:hi] = block[...]
    inv_ref[lo:hi, lo:hi] = x
    if k:
        inner = dot_t(u_ref[0:lo, lo:hi], inv_ref[0:lo, 0:lo])
        inv_ref[lo:hi, 0:lo] = -dot_n(x, inner)
    if hi < n:
        right = dot_n(x, work[lo:hi, hi:n])
        u_ref[lo:hi, hi:n] = right
        work[hi:n, hi:n] -= dot_t(right, right)


def factor_part(k, work, upper, inverse):
    full = pl.BlockSpec(memory_space=pltpu.VMEM)
    shape = jax.ShapeDtypeStruct((512, 512), jnp.float32)
    return pl.pallas_call(
        functools.partial(factor_kernel, k),
        out_shape=(shape,) * 3,
        in_specs=[full] * 3,
        out_specs=(full,) * 3,
        scratch_shapes=[
            pltpu.VMEM((128, 128), jnp.float32),
            pltpu.VMEM((128, 128), jnp.float32),
        ],
        compiler_params=pltpu.CompilerParams(vmem_limit_bytes=32 * 2**20),
        cost_estimate=pl.CostEstimate(flops=2**20, bytes_accessed=2**20, transcendentals=512),
    )(work, upper, inverse)


def per_device(acts_one, acts_two):
    cal, row, z = (lax.axis_index(a) for a in AXES)
    core = cal % 2
    total_tokens = 8 * acts_one.shape[0]
    scale = 1.0 / total_tokens
    device = (cal * 8 + row) * 8 + z
    meta = lax.dynamic_index_in_dim(jnp.asarray(TABLE), device, 0, keepdims=False)
    after = lax.optimization_barrier
    root = lambda x, y, z: (x // 2, y) == (0, 0) and z < 2

    cols = jnp.concatenate([acts_one, acts_two], 0)
    piece = jnp.concatenate([acts_one.T, acts_two.T], 1)[None]
    a0, b0 = acts_one[None], acts_two[None]
    a1 = move(a0, x_step(0))
    b1 = move(b0, y_step(0))
    other = move(cols, lambda x, y, z, c: (x, y, 1 - z, c) if root(x, y, z) else None)
    a1, b1, other, piece = after((a1, b1, other, piece))

    r0 = move(piece, row_home)
    a01 = jnp.concatenate([a0, a1], 0)
    b01 = jnp.concatenate([b0, b1], 0)
    a23 = move(a01, x_step(1))
    b23 = move(b01, y_step(1))
    left, right = jnp.where(z == 0, cols, other), jnp.where(z == 0, other, cols)
    part = [
        lax.dot_general(p, q, (((0,), (0,)), ((), ())), preferred_element_type=jnp.float32)
        for p, q in ((left, left), (left, right), (right, right))
    ]
    part = jnp.concatenate(part, 0).reshape(2, 384, 256)
    lead = lax.dynamic_index_in_dim(part, core, 0, keepdims=False)
    away = lax.dynamic_index_in_dim(part, 1 - core, 0, keepdims=False)
    lead = lead + move(away, lambda x, y, z, c: (x, y, z, 1 - c) if root(x, y, z) else None)
    lead = lead + move(lead, lambda x, y, z, c: (x ^ 1, y, z, c) if root(x, y, z) else None)
    r0, lead, a01, a23, b01, b23 = after((r0, lead, a01, a23, b01, b23))

    r1 = move(r0, z_step(0))
    first = jnp.concatenate([a01, a23], 0)
    second = jnp.concatenate([b01, b23], 0)
    lead = jnp.where(row == 0, lead, 0.0)
    lead = lead + move(lead, lambda x, y, z, c: (x + 2, y, z, c) if root(x, y, z) else None)
    sent = [
        move(lead, lambda x, y, z, c, to=to: (x, to, z, c) if y == 0 and z < 2 else None)
        for to in (1, 3, 2)
    ]
    lead = lead + (sent[0] + sent[1] + sent[2])
    r0, r1, first, second, lead = after((r0, r1, first, second, lead))

    r01 = jnp.concatenate([r0, r1], 0)
    r2 = move(r01, z_step(1))
    first1 = move(first, y_step(0))
    second1 = move(second, x_step(0))
    theirs = move(lead, lambda x, y, z, c: (x, y, z, 1 - c) if z < 2 else None)
    low = jnp.where(core == 0, lead, theirs)
    high = jnp.where(core == 0, theirs, lead)
    corner = jnp.concatenate([low[256:], high[:128]], 0)
    gram = jnp.concatenate(
        [
            jnp.concatenate([low[:256], corner], 1),
            jnp.concatenate([corner.T, high[128:]], 1),
        ],
        0,
    ) * scale
    ids = jnp.arange(512, dtype=jnp.int32)
    work = jnp.where(ids[:, None] == ids[None, :], gram, reg_alpha * gram)
    zeros = jnp.zeros((512, 512), jnp.float32)
    state = factor_part(0, work, zeros, zeros)
    r01, r2, first, first1, second, second1, state = after(
        (r01, r2, first, first1, second, second1, state)
    )

    r3 = move(r2, z_step(2))
    first2 = move(first, y_step(1))
    second2 = move(second, x_step(1))
    state = factor_part(1, *state)
    state = factor_part(2, *state)
    r01, r2, r3, first, first1, first2, second, second1, second2, state = after(
        (r01, r2, r3, first, first1, first2, second, second1, second2, state)
    )

    r4 = move(r3, z_step(3))
    first3 = move(first1, y_step(1))
    second3 = move(second1, x_step(1))
    _, upper, inverse = factor_part(3, *state)
    r01, r2, r3, r4, first, first1, first2, first3, second, second1, second2, second3, upper, inverse = after(
        (r01, r2, r3, r4, first, first1, first2, first3, second, second1, second2, second3, upper, inverse)
    )

    pieces = (
        (r01, r2, r3, r4),
        (first, first1, first2, first3),
        (second, second1, second2, second3),
    )
    row_start = row * 2048 + cal * 512
    meta = meta.at[25].set(row_start).at[26].set(z * 256)

    block, away = lead_part(meta, *pieces)
    block = block + move(away, lambda x, y, z, c: (x, y, z, 1 - c) if z < 2 else None)
    block = block * scale
    row_ids = row_start + jnp.arange(512, dtype=jnp.int32)[:, None]
    col_ids = z * 256 + jnp.arange(256, dtype=jnp.int32)[None, :]
    block = jnp.where(row_ids == col_ids, block, reg_alpha * block)
    block, pieces = after((block, pieces))
    left = move(block, lambda x, y, z, c: (x, y, 1, c) if z == 0 else None)

    theirs = gram_part(scale, meta, *pieces)
    theirs = move(theirs, core_swap)

    def times(weights, rows):
        return lax.dot_general(
            weights, rows, (((1,), (1,)), ((), ())), precision=HIGHEST,
            preferred_element_type=jnp.float32,
        )

    low = z == 0
    solved = times(jnp.where(low, inverse[:256, :256], inverse[256:, 256:]), block)
    solved = solved + times(jnp.where(low, 0.0, inverse[256:, :256]), left)
    head = jnp.where(low, upper[:256], upper[256:])
    solved = jnp.where((row == 0) & (cal == 0), head, solved).reshape(4, 64, 512)
    share = jnp.where(low, solved[0], 0.0)
    for i in range(4):
        def target(x, y, z, c, i=i):
            if z == 0 and i < 3:
                return x, y, i + 1, c
            return (x, y, i + 4, c) if z == 1 else None

        value = jnp.where(low, solved[i + 1], solved[i]) if i < 3 else solved[i]
        share = share + move(value, target)

    gram_reg = gram_part(scale, meta, *pieces, other=theirs)
    return gram_reg.reshape(1, 512, 8, 1, 256), share.T.reshape(1, 512, 64)


def solution(mesh):
    return jax.shard_map(
        per_device,
        mesh=mesh,
        in_specs=(P("cal", ("row", "col")), P("cal", ("row", "col"))),
        out_specs=(P("row", "cal", None, "col", None), P("row", "cal", "col")),
        check_vma=False,
    )
```

```python
import functools

import jax
import jax.numpy as jnp
import numpy as np
from jax import lax
from jax.experimental import pallas as pl
from jax.experimental.pallas import tpu as pltpu
from jax.sharding import PartitionSpec as P

PANEL = 512
reg_alpha = 0.9
AXES = ("cal", "row", "col")
NX, NY, NZ = 4, 4, 8
HIGHEST = lax.Precision.HIGHEST


def flat(x, y, z, core):
    return (((x % 2) * 2 + core) * 8 + (x // 2) * 4 + y) * 8 + z


def devices():
    for x in range(NX):
        for y in range(NY):
            for z in range(NZ):
                for core in range(2):
                    yield x, y, z, core


def move(value, target):
    pairs = []
    for device in devices():
        to = target(*device)
        if to is not None:
            pairs.append((flat(*device), flat(*to)))
    return lax.ppermute(value, AXES, sorted(pairs))


def near(i, size, phase):
    return i ^ 1 if phase == 0 else (i + 1 if i % 2 else i - 1) % size


def x_step(s):
    return lambda x, y, z, c: (near(x, NX, (s + c) % 2), y, z, c)


def y_step(s):
    return lambda x, y, z, c: (x, near(y, NY, (s + c) % 2), z, c)


def z_step(s):
    return lambda x, y, z, c: (x, y, near(z, NZ, (s + c) % 2), c)


def core_swap(x, y, z, c):
    return x, y, z, 1 - c


def row_home(x, y, z, c):
    return (x, y, z, c) if z // 4 == x % 2 else (x ^ 1, y, 7 - z, c)


def tables():
    table = np.zeros((256, 32), np.int32)
    for x, y, z, c in devices():
        def ring4(i):
            p1 = lambda v: near(v, 4, c % 2)
            p2 = lambda v: near(v, 4, (1 + c) % 2)
            return [i, p1(i), p2(i), p1(p2(i))]

        step = lambda v, s: near(v, NZ, (s + c) % 2)
        first = lambda v: [v, step(v, 0)]
        third = lambda v: first(step(step(v, 2), 1))
        slots = first(z) + first(step(z, 1)) + third(z) + third(step(z, 3))
        assert sorted(slots) == list(range(8))
        low = x % 2
        blocks = [(p if p // 4 == low else 7 - p) - 4 * low for p in slots]
        halves = [low if p // 4 == low else 1 - low for p in slots]
        table[flat(x, y, z, c)] = ring4(x) + ring4(y) + blocks + halves + [c, low] + [0] * 6
    return table


TABLE = tables()


def join_kernel(*refs):
    n = len(refs) - 2
    out_ref, sem = refs[n], refs[n + 1]
    copies, at = [], 0
    for i in range(n):
        size = refs[i].shape[0]
        copy = pltpu.make_async_copy(refs[i], out_ref.at[pl.ds(at, size)], sem.at[i])
        copy.start()
        copies.append(copy)
        at += size
    for copy in copies:
        copy.wait()


def join(*parts):
    any_spec = pl.BlockSpec(memory_space=pl.ANY)
    rows = sum(p.shape[0] for p in parts)
    return pl.pallas_call(
        join_kernel,
        out_shape=jax.ShapeDtypeStruct((rows,) + parts[0].shape[1:], parts[0].dtype),
        in_specs=[any_spec] * len(parts),
        out_specs=any_spec,
        scratch_shapes=[pltpu.SemaphoreType.DMA((len(parts),))],
        cost_estimate=pl.CostEstimate(flops=0, bytes_accessed=2**20, transcendentals=0),
    )(*parts)


def transpose_kernel(one_ref, two_ref, out_ref):
    tokens = one_ref.shape[0]
    out_ref[0, :, :tokens] = one_ref[...].T
    out_ref[0, :, tokens:] = two_ref[...].T


def transposed(one, two):
    full = pl.BlockSpec(memory_space=pltpu.VMEM)
    return pl.pallas_call(
        transpose_kernel,
        out_shape=jax.ShapeDtypeStruct((1, one.shape[1], 2 * one.shape[0]), one.dtype),
        in_specs=[full, full],
        out_specs=full,
        cost_estimate=pl.CostEstimate(flops=0, bytes_accessed=2**20, transcendentals=0),
    )(one, two)


def column(meta, j, pair):
    x = jnp.where(meta[24] == 0, meta[2 * pair], meta[pair])
    return (x // 2) * 4 + meta[4 + j]


def column_copies(meta, first_refs, second_refs, cols, sem, j, needed=None):
    half = first_refs[0].shape[1]
    copies = []
    for i in range(4):
        pair = jnp.where(meta[24] == 0, i // 2, i % 2)
        side = meta[i] % 2
        for which, ref in ((0, first_refs[j].at[i]), (1, second_refs[i].at[j])):
            dst = cols.at[
                2 * j + pair,
                pl.ds(pl.multiple_of(side * 2 * half + which * half, half), half),
            ]
            want = True if needed is None else needed(side)
            copies.append((want, pltpu.make_async_copy(ref, dst, sem.at[j, i, which])))
    return copies


def start_all(copies):
    for want, copy in copies:
        pl.when(want)(copy.start)


def wait_all(copies):
    for want, copy in copies:
        pl.when(want)(copy.wait)


def early_kernel(own, *refs):
    meta, row_refs, first_refs, second_refs = refs[0], refs[1:4], refs[4:8], refs[8:12]
    out_ref, rows, cols, acc, row_sem, col_sem, sem = refs[12:]
    tokens = row_refs[0].shape[2]
    wanted = meta[24] if own else 1 - meta[24]

    def place(slot):
        return rows.at[
            pl.ds(pl.multiple_of((meta[8 + slot] % 2) * 256, 256), 256),
            pl.ds(pl.multiple_of(meta[16 + slot] * tokens, tokens), tokens),
        ]

    row_copies = []
    for slot in range(6):
        copy = pltpu.make_async_copy(row_refs[slot // 2].at[slot % 2], place(slot), row_sem.at[slot])
        row_copies.append((meta[8 + slot] // 2 == wanted, copy))
    col_copies = [column_copies(meta, first_refs, second_refs, cols, col_sem, j) for j in range(4)]
    start_all(row_copies)
    start_all(col_copies[0])
    start_all(col_copies[1])
    for slot in (6, 7):
        @pl.when(meta[8 + slot] // 2 == wanted)
        def _(slot=slot):
            place(slot)[...] = jnp.zeros((256, tokens), rows.dtype)
    wait_all(row_copies)
    out_copies = []
    for j in range(4):
        wait_all(col_copies[j])
        if j + 2 < 4:
            start_all(col_copies[j + 2])
        for pair in range(2):
            k = 2 * j + pair
            acc[k] = jnp.dot(rows[...], cols[k], preferred_element_type=jnp.float32)
            copy = pltpu.make_async_copy(acc.at[k], out_ref.at[column(meta, j, pair)], sem.at[k])
            copy.start()
            out_copies.append(copy)
    for copy in out_copies:
        copy.wait()


def early_part(own, meta, rows, first_bufs, second_bufs):
    tokens = rows[0].shape[2]
    any_spec = pl.BlockSpec(memory_space=pl.ANY)
    return pl.pallas_call(
        functools.partial(early_kernel, own),
        out_shape=jax.ShapeDtypeStruct((8, 512, 256), jnp.float32),
        in_specs=[pl.BlockSpec(memory_space=pltpu.SMEM)] + [any_spec] * 11,
        out_specs=any_spec,
        scratch_shapes=[
            pltpu.VMEM((512, 2 * tokens), jnp.bfloat16),
            pltpu.VMEM((8, 2 * tokens, 256), jnp.bfloat16),
            pltpu.VMEM((8, 512, 256), jnp.float32),
            pltpu.SemaphoreType.DMA((6,)),
            pltpu.SemaphoreType.DMA((4, 4, 2)),
            pltpu.SemaphoreType.DMA((8,)),
        ],
        compiler_params=pltpu.CompilerParams(vmem_limit_bytes=62 * 2**20),
        cost_estimate=pl.CostEstimate(flops=2**20, bytes_accessed=2**20, transcendentals=0),
    )(meta, *rows, *first_bufs, *second_bufs)


def late_kernel(own, scale, *refs):
    meta, row_ref, first_refs, second_refs, early_ref = refs[0], refs[1], refs[2:6], refs[6:10], refs[10]
    refs = refs[11:]
    if own:
        other_ref, out_ref, rows, cols, acc, other, row_sem, col_sem, sem, other_sem = refs
    else:
        out_ref, rows, cols, acc, row_sem, col_sem, sem = refs
    tokens = row_ref.shape[2]
    wanted = meta[24] if own else 1 - meta[24]
    mine = [meta[8 + slot] // 2 == wanted for slot in (6, 7)]
    needed = lambda side: (mine[0] & (meta[22] == side)) | (mine[1] & (meta[23] == side))
    row_copies = [
        (mine[i], pltpu.make_async_copy(row_ref.at[i], rows.at[i], row_sem.at[i])) for i in range(2)
    ]
    groups = []
    for j in range(4):
        group = column_copies(meta, first_refs, second_refs, cols, col_sem, j, needed)
        for pair in range(2):
            k, a = 2 * j + pair, column(meta, j, pair)
            group.append((True, pltpu.make_async_copy(early_ref.at[a], acc.at[k], sem.at[k])))
            if own:
                copy = pltpu.make_async_copy(other_ref.at[a], other.at[k], other_sem.at[k])
                group.append((True, copy))
        groups.append(group)
    start_all(row_copies)
    start_all(groups[0])
    start_all(groups[1])
    wait_all(row_copies)
    row_ids = meta[25] + lax.broadcasted_iota(jnp.int32, (512, 128), 0)
    lane = meta[26] + lax.broadcasted_iota(jnp.int32, (512, 128), 1)
    out_copies = []
    for j in range(4):
        wait_all(groups[j])
        if j + 2 < 4:
            start_all(groups[j + 2])
        for i in range(2):
            @pl.when(mine[i])
            def _(i=i):
                at = pl.ds(pl.multiple_of((meta[14 + i] % 2) * 256, 256), 256)
                side = pl.ds(pl.multiple_of(meta[22 + i] * tokens, tokens), tokens)
                for pair in range(2):
                    k = 2 * j + pair
                    acc[k, at, :] += jnp.dot(
                        rows[i], cols[k, side, :], preferred_element_type=jnp.float32
                    )
        for pair in range(2):
            k, a = 2 * j + pair, column(meta, j, pair)
            if own:
                for h in range(2):
                    at = slice(h * 128, (h + 1) * 128)
                    part = (acc[k, :, at] + other[k, :, at]) * scale
                    same = row_ids == lane + (a * 2048 + h * 128)
                    out_ref[pl.ds(2 * a + h, 512, stride=16), :] = jnp.where(
                        same, part, reg_alpha * part
                    )
            else:
                copy = pltpu.make_async_copy(acc.at[k], out_ref.at[a], sem.at[k])
                copy.start()
                out_copies.append(copy)
    for copy in out_copies:
        copy.wait()


def late_part(scale, meta, row, first_bufs, second_bufs, early, other=None):
    own = other is not None
    tokens = row.shape[2]
    any_spec = pl.BlockSpec(memory_space=pl.ANY)
    shape = (512 * 16, 128) if own else (8, 512, 256)
    half = pltpu.VMEM((8, 512, 256), jnp.float32)
    return pl.pallas_call(
        functools.partial(late_kernel, own, scale),
        out_shape=jax.ShapeDtypeStruct(shape, jnp.float32),
        in_specs=[pl.BlockSpec(memory_space=pltpu.SMEM)] + [any_spec] * (10 + own),
        out_specs=pl.BlockSpec(memory_space=pltpu.VMEM) if own else any_spec,
        scratch_shapes=[
            pltpu.VMEM((2, 256, tokens), jnp.bfloat16),
            pltpu.VMEM((8, 2 * tokens, 256), jnp.bfloat16),
        ]
        + [half] * (1 + own)
        + [
            pltpu.SemaphoreType.DMA((2,)),
            pltpu.SemaphoreType.DMA((4, 4, 2)),
            pltpu.SemaphoreType.DMA((8,)),
        ]
        + [pltpu.SemaphoreType.DMA((8,))] * own,
        compiler_params=pltpu.CompilerParams(vmem_limit_bytes=62 * 2**20),
        cost_estimate=pl.CostEstimate(
            flops=2 * 512 * 2048 * 2 * tokens, bytes_accessed=24 * 2**20, transcendentals=0
        ),
    )(meta, row, *first_bufs, *second_bufs, early, *([other] if own else []))


def lead_kernel(*refs):
    meta, row_ref, first_refs, second_refs = refs[0], refs[1], refs[2:6], refs[6:10]
    early_refs, out_refs = refs[10:12], refs[12:14]
    rows, cols, row_sem, col_sem, sem = refs[14:]
    tokens = row_ref.shape[2]
    half = tokens // 2
    copies = [
        (True, pltpu.make_async_copy(row_ref.at[i], rows.at[i], row_sem.at[i])) for i in range(2)
    ]
    for h in range(2):
        copies.append((True, pltpu.make_async_copy(early_refs[h].at[0], out_refs[h], sem.at[h])))
    for j in range(4):
        for i in range(4):
            side = meta[i] % 2
            want = (meta[i] // 2 == 0) & (meta[4 + j] == 0)
            for which, ref in ((0, first_refs[j].at[i]), (1, second_refs[i].at[j])):
                dst = cols.at[pl.ds(pl.multiple_of(side * tokens + which * half, half), half)]
                copies.append((want, pltpu.make_async_copy(ref, dst, col_sem.at[j, i, which])))
    start_all(copies)
    wait_all(copies)
    for i in range(2):
        at = pl.ds(pl.multiple_of((meta[14 + i] % 2) * 256, 256), 256)
        side = pl.ds(pl.multiple_of(meta[22 + i] * tokens, tokens), tokens)
        part = jnp.dot(rows[i], cols[side, :], preferred_element_type=jnp.float32)
        for h in range(2):
            @pl.when((meta[14 + i] // 2 == meta[24]) == (h == 0))
            def _(h=h, at=at, part=part):
                out_refs[h][at, :] += part


def lead_part(meta, row, first_bufs, second_bufs, early_own, early_away):
    tokens = row.shape[2]
    any_spec = pl.BlockSpec(memory_space=pl.ANY)
    vmem = pl.BlockSpec(memory_space=pltpu.VMEM)
    return pl.pallas_call(
        lead_kernel,
        out_shape=(jax.ShapeDtypeStruct((512, 256), jnp.float32),) * 2,
        in_specs=[pl.BlockSpec(memory_space=pltpu.SMEM)] + [any_spec] * 11,
        out_specs=(vmem, vmem),
        scratch_shapes=[
            pltpu.VMEM((2, 256, tokens), jnp.bfloat16),
            pltpu.VMEM((2 * tokens, 256), jnp.bfloat16),
            pltpu.SemaphoreType.DMA((2,)),
            pltpu.SemaphoreType.DMA((4, 4, 2)),
            pltpu.SemaphoreType.DMA((2,)),
        ],
        compiler_params=pltpu.CompilerParams(vmem_limit_bytes=62 * 2**20),
        cost_estimate=pl.CostEstimate(flops=2**30, bytes_accessed=4 * 2**20, transcendentals=0),
    )(meta, row, *first_bufs, *second_bufs, early_own, early_away)


def dot_t(a, b):
    return lax.dot_general(
        a, b, (((0,), (0,)), ((), ())), precision=HIGHEST, preferred_element_type=jnp.float32
    )


def dot_n(a, b):
    return lax.dot_general(
        a, b, (((1,), (0,)), ((), ())), precision=HIGHEST, preferred_element_type=jnp.float32
    )


def factor_block(k, work, u_ref, inv_ref, block, inv):
    n, nb, np_ = 512, 128, 8
    sub = lax.broadcasted_iota(jnp.int32, (np_, nb), 0)
    lane = lax.broadcasted_iota(jnp.int32, (np_, nb), 1)
    lo, hi = k * nb, (k + 1) * nb
    block[...] = work[lo:hi, lo:hi]
    inv[...] = (
        lax.broadcasted_iota(jnp.int32, (nb, nb), 0) == lax.broadcasted_iota(jnp.int32, (nb, nb), 1)
    ).astype(jnp.float32)

    def panel(p, _):
        base = pl.multiple_of(p * np_, np_)
        v = block[pl.ds(base, np_), :]
        xv = inv[pl.ds(base, np_), :]
        rolled = pltpu.roll(v, lax.rem(nb - base, nb), 1)
        pc = [jnp.broadcast_to(rolled[:, i:i + 1], (np_, nb)) for i in range(np_)]
        for i in range(np_):
            s = lax.rsqrt(pc[i][i:i + 1, :])
            u = v[i:i + 1, :] * s
            xu = xv[i:i + 1, :] * s
            below = jnp.where(sub > i, pc[i] * s, 0.0)
            here = sub == i
            for j in range(i + 1, np_):
                pc[j] = pc[j] - below * (pc[j][i:i + 1, :] * s)
            v = jnp.where(here, u, v - below * u)
            xv = jnp.where(here, xu, xv - below * xu)
        v = jnp.where(lane >= base + sub, v, 0.0)
        block[pl.ds(base, np_), :] = v
        inv[pl.ds(base, np_), :] = xv
        later = jnp.where(lane >= base + np_, v, 0.0)
        block[...] -= dot_t(later, v)
        inv[...] -= dot_t(later, xv)
        return 0

    lax.fori_loop(0, nb // np_, panel, 0)
    x = inv[...]
    u_ref[lo:hi, lo:hi] = block[...]
    inv_ref[lo:hi, lo:hi] = x
    if k:
        inner = dot_t(u_ref[0:lo, lo:hi], inv_ref[0:lo, 0:lo])
        inv_ref[lo:hi, 0:lo] = -dot_n(x, inner)
    if hi < n:
        right = dot_n(x, work[lo:hi, hi:n])
        u_ref[lo:hi, hi:n] = right
        work[hi:n, hi:n] -= dot_t(right, right)


def factor_first(scale, sums, work, u_ref, inv_ref, block, inv):
    rid = lax.broadcasted_iota(jnp.int32, (256, 256), 0)
    cid = lax.broadcasted_iota(jnp.int32, (256, 256), 1)

    def regular(part):
        return jnp.where(rid == cid, part * scale, reg_alpha * (part * scale))

    work[...] = jnp.zeros((512, 512), jnp.float32)
    work[:256, :256] = regular(sums[:256])
    work[:256, 256:] = reg_alpha * (sums[256:512] * scale)
    work[256:, 256:] = regular(sums[512:])
    u_ref[...] = jnp.zeros((512, 512), jnp.float32)
    inv_ref[...] = jnp.zeros((512, 512), jnp.float32)
    for k in (0, 1):
        factor_block(k, work, u_ref, inv_ref, block, inv)


def factor_second(work_ref, u_in, inv_in, u_ref, inv_ref, work, block, inv):
    work[...] = work_ref[...]
    u_ref[...] = u_in[...]
    inv_ref[...] = inv_in[...]
    for k in (2, 3):
        factor_block(k, work, u_ref, inv_ref, block, inv)


def factor_part(kernel, n_out, args):
    full = pl.BlockSpec(memory_space=pltpu.VMEM)
    shape = jax.ShapeDtypeStruct((512, 512), jnp.float32)
    small = pltpu.VMEM((128, 128), jnp.float32)
    return pl.pallas_call(
        kernel,
        out_shape=(shape,) * n_out,
        in_specs=[full] * len(args),
        out_specs=(full,) * n_out,
        scratch_shapes=[pltpu.VMEM((512, 512), jnp.float32)] * (3 - n_out) + [small] * 2,
        compiler_params=pltpu.CompilerParams(vmem_limit_bytes=32 * 2**20),
        cost_estimate=pl.CostEstimate(flops=2**20, bytes_accessed=2**20, transcendentals=512),
    )(*args)


def per_device(acts_one, acts_two):
    cal, row, z = (lax.axis_index(a) for a in AXES)
    low, core = cal // 2, cal % 2
    total_tokens = 8 * acts_one.shape[0]
    scale = 1.0 / total_tokens
    device = (cal * 8 + row) * 8 + z
    meta = lax.dynamic_index_in_dim(jnp.asarray(TABLE), device, 0, keepdims=False)
    after = lax.optimization_barrier
    root = lambda x, y, z: (x // 2, y) == (0, 0) and z < 2

    cols = join(acts_one, acts_two)
    piece = transposed(acts_one, acts_two)
    other = move(cols, lambda x, y, z, c: (x, y, 1 - z, c) if root(x, y, z) else None)
    a0, b0 = acts_one[None], acts_two[None]
    a01 = join(a0, move(a0, x_step(0)))
    b01 = join(b0, move(b0, y_step(0)))
    first = join(a01, move(a01, x_step(1)))
    second = join(b01, move(b01, y_step(1)))
    first, second, other, piece = after((first, second, other, piece))

    r0 = move(piece, row_home)
    first1 = move(first, y_step(0))
    second1 = move(second, x_step(0))
    left, right = jnp.where(z == 0, cols, other), jnp.where(z == 0, other, cols)
    part = [
        lax.dot_general(p, q, (((0,), (0,)), ((), ())), preferred_element_type=jnp.float32)
        for p, q in ((left, left), (left, right), (right, right))
    ]
    part = jnp.concatenate(part, 0).reshape(2, 2, 192, 256)
    pick = lambda value, at: lax.dynamic_index_in_dim(value, at, 0, keepdims=False)
    away = move(pick(part, 1 - core), lambda x, y, z, c: (x, y, z, 1 - c) if root(x, y, z) else None)
    lead = pick(part, core) + away
    away = move(pick(lead, 1 - low), lambda x, y, z, c: (x ^ 1, y, z, c) if root(x, y, z) else None)
    lead = jnp.where(row == 0, pick(lead, low) + away, 0.0)
    lead = lead + move(lead, lambda x, y, z, c: (x + 2, y, z, c) if root(x, y, z) else None)
    lead = lead + move(lead, lambda x, y, z, c: (x, 1, z, c) if y == 0 and z < 2 else None)
    lead = lead + move(lead, lambda x, y, z, c: (x, 3 - y, z, c) if y < 2 and z < 2 else None)
    r0, first, first1, second, second1, lead = after((r0, first, first1, second, second1, lead))

    r01 = join(r0, move(r0, z_step(0)))
    theirs = move(lead, lambda x, y, z, c: (x ^ 1, y, z, c) if z < 2 else None)
    lead = jnp.where(low == 0, jnp.stack([lead, theirs]), jnp.stack([theirs, lead]))
    theirs = move(lead, lambda x, y, z, c: (x, y, z, 1 - c) if z < 2 else None)
    lead = jnp.where(core == 0, jnp.stack([lead, theirs]), jnp.stack([theirs, lead]))
    r01, lead, first, first1, second, second1 = after((r01, lead, first, first1, second, second1))

    r2 = move(r01, z_step(1))
    first2 = move(first, y_step(1))
    second2 = move(second, x_step(1))
    state = factor_part(functools.partial(factor_first, scale), 3, (lead.reshape(768, 256),))
    r01, r2, first, first1, first2, second, second1, second2, state = after(
        (r01, r2, first, first1, first2, second, second1, second2, state)
    )

    r3 = move(r2, z_step(2))
    first3 = move(first1, y_step(1))
    second3 = move(second1, x_step(1))
    upper, inverse = factor_part(factor_second, 2, state)
    rows, firsts, seconds, upper, inverse = after(
        (
            (r01, r2, r3),
            (first, first1, first2, first3),
            (second, second1, second2, second3),
            upper,
            inverse,
        )
    )

    row_start = row * 2048 + cal * 512
    meta = meta.at[25].set(row_start).at[26].set(z * 256)
    r4 = move(rows[2], z_step(3))
    early_away = early_part(False, meta, rows, firsts, seconds)
    early_own = early_part(True, meta, rows, firsts, seconds)
    r4, early_away, early_own, firsts, seconds = after((r4, early_away, early_own, firsts, seconds))

    block, away = lead_part(meta, r4, firsts, seconds, early_own, early_away)
    block = block + move(away, lambda x, y, z, c: (x, y, z, 1 - c) if z < 2 else None)
    block = block * scale
    row_ids = row_start + jnp.arange(512, dtype=jnp.int32)[:, None]
    col_ids = z * 256 + jnp.arange(256, dtype=jnp.int32)[None, :]
    block = jnp.where(row_ids == col_ids, block, reg_alpha * block)
    block, r4, early_away, firsts, seconds = after((block, r4, early_away, firsts, seconds))
    left = move(block, lambda x, y, z, c: (x, y, 1, c) if z == 0 else None)
    theirs = late_part(scale, meta, r4, firsts, seconds, early_away)
    left, theirs = after((left, theirs))
    theirs = move(theirs, core_swap)

    def times(weights, rows):
        return lax.dot_general(
            weights, rows, (((1,), (1,)), ((), ())), precision=HIGHEST,
            preferred_element_type=jnp.float32,
        )

    edge = z == 0
    solved = times(jnp.where(edge, inverse[:256, :256], inverse[256:, 256:]), block)
    solved = solved + times(jnp.where(edge, 0.0, inverse[256:, :256]), left)
    head = jnp.where(edge, upper[:256], upper[256:])
    solved = jnp.where((row == 0) & (cal == 0), head, solved).reshape(4, 64, 512)
    share = [jnp.where(edge, solved[0], 0.0)]
    for i in range(4):
        def target(x, y, z, c, i=i):
            if z == 0 and i < 3:
                return x, y, i + 1, c
            return (x, y, i + 4, c) if z == 1 else None

        value = jnp.where(edge, solved[i + 1], solved[i]) if i < 3 else solved[i]
        share.append(move(value, target))

    gram_reg = late_part(scale, meta, r4, firsts, seconds, early_own, other=theirs)
    gram_reg, share = after((gram_reg, share))
    share = functools.reduce(jnp.add, share)
    return gram_reg.reshape(1, 512, 8, 1, 256), share.T.reshape(1, 512, 64)


def solution(mesh):
    return jax.shard_map(
        per_device,
        mesh=mesh,
        in_specs=(P("cal", ("row", "col")), P("cal", ("row", "col"))),
        out_specs=(P("row", "cal", None, "col", None), P("row", "cal", "col")),
        check_vma=False,
    )
```

```python
import functools

import jax
import jax.numpy as jnp
import numpy as np
from jax import lax
from jax.experimental import pallas as pl
from jax.experimental.pallas import tpu as pltpu
from jax.sharding import PartitionSpec as P

PANEL = 512
reg_alpha = 0.9
AXES = ("cal", "row", "col")
NX, NY, NZ = 4, 4, 8
HIGHEST = lax.Precision.HIGHEST


def flat(x, y, z, core):
    return (((x % 2) * 2 + core) * 8 + (x // 2) * 4 + y) * 8 + z


def devices():
    for x in range(NX):
        for y in range(NY):
            for z in range(NZ):
                for core in range(2):
                    yield x, y, z, core


def move(value, target):
    pairs = []
    for device in devices():
        to = target(*device)
        if to is not None:
            pairs.append((flat(*device), flat(*to)))
    return lax.ppermute(value, AXES, sorted(pairs))


def near(i, size, phase):
    return i ^ 1 if phase == 0 else (i + 1 if i % 2 else i - 1) % size


def x_step(s):
    return lambda x, y, z, c: (near(x, NX, (s + c) % 2), y, z, c)


def y_step(s):
    return lambda x, y, z, c: (x, near(y, NY, (s + c) % 2), z, c)


def z_step(s):
    return lambda x, y, z, c: (x, y, near(z, NZ, (s + c) % 2), c)


def core_swap(x, y, z, c):
    return x, y, z, 1 - c


def row_home(x, y, z, c):
    return (x, y, z, c) if z // 4 == x % 2 else (x ^ 1, y, 7 - z, c)


def tables():
    table = np.zeros((256, 32), np.int32)
    for x, y, z, c in devices():
        def ring4(i):
            p1 = lambda v: near(v, 4, c % 2)
            p2 = lambda v: near(v, 4, (1 + c) % 2)
            return [i, p1(i), p2(i), p1(p2(i))]

        step = lambda v, s: near(v, NZ, (s + c) % 2)
        first = lambda v: [v, step(v, 0)]
        third = lambda v: first(step(step(v, 2), 1))
        slots = first(z) + first(step(z, 1)) + third(z) + third(step(z, 3))
        assert sorted(slots) == list(range(8))
        low = x % 2
        blocks = [(p if p // 4 == low else 7 - p) - 4 * low for p in slots]
        halves = [low if p // 4 == low else 1 - low for p in slots]
        table[flat(x, y, z, c)] = ring4(x) + ring4(y) + blocks + halves + [c, low] + [0] * 6
    return table


TABLE = tables()


def column(meta, j, pair):
    x = jnp.where(meta[24] == 0, meta[2 * pair], meta[pair])
    return (x // 2) * 4 + meta[4 + j]


def column_copies(meta, first_refs, second_refs, cols, sem, j, needed=None):
    half = first_refs[0].shape[1]
    copies = []
    for i in range(4):
        pair = jnp.where(meta[24] == 0, i // 2, i % 2)
        side = meta[i] % 2
        for which, ref in ((0, first_refs[j].at[i]), (1, second_refs[i].at[j])):
            dst = cols.at[
                2 * j + pair,
                pl.ds(pl.multiple_of(side * 2 * half + which * half, half), half),
            ]
            want = True if needed is None else needed(side)
            copies.append((want, pltpu.make_async_copy(ref, dst, sem.at[j, i, which])))
    return copies


def start_all(copies):
    for want, copy in copies:
        pl.when(want)(copy.start)


def wait_all(copies):
    for want, copy in copies:
        pl.when(want)(copy.wait)


def early_kernel(*refs):
    meta, row_refs, first_refs, second_refs = refs[0], refs[1:4], refs[4:8], refs[8:12]
    own_ref, away_ref, rows, cols, acc, row_sem, col_sem, sem = refs[12:]
    tokens = row_refs[0].shape[2]

    def place(slot):
        at = jnp.where(meta[8 + slot] // 2 == meta[24], 0, 512) + (meta[8 + slot] % 2) * 256
        return rows.at[
            pl.ds(pl.multiple_of(at, 256), 256),
            pl.ds(pl.multiple_of(meta[16 + slot] * tokens, tokens), tokens),
        ]

    row_copies = [
        (True, pltpu.make_async_copy(row_refs[i // 2].at[i % 2], place(i), row_sem.at[i]))
        for i in range(6)
    ]
    col_copies = [column_copies(meta, first_refs, second_refs, cols, col_sem, j) for j in range(4)]
    start_all(row_copies)
    start_all(col_copies[0])
    start_all(col_copies[1])
    for slot in (6, 7):
        place(slot)[...] = jnp.zeros((256, tokens), rows.dtype)
    wait_all(row_copies)
    out_copies = []
    for j in range(4):
        wait_all(col_copies[j])
        if j + 2 < 4:
            start_all(col_copies[j + 2])

        def part(i, _, j=j):
            at = pl.ds(pl.multiple_of((i % 2) * 512, 512), 512)
            k = 2 * j + i // 2
            acc[k, at, :] = jnp.dot(rows[at, :], cols[k], preferred_element_type=jnp.float32)
            return 0

        lax.fori_loop(0, 4, part, 0)
        for pair in range(2):
            k = 2 * j + pair
            for h, ref in ((0, own_ref), (1, away_ref)):
                copy = pltpu.make_async_copy(
                    acc.at[k, pl.ds(h * 512, 512)], ref.at[column(meta, j, pair)], sem.at[h, k]
                )
                copy.start()
                out_copies.append(copy)
    for copy in out_copies:
        copy.wait()


def early_part(meta, rows, first_bufs, second_bufs):
    tokens = rows[0].shape[2]
    any_spec = pl.BlockSpec(memory_space=pl.ANY)
    return pl.pallas_call(
        early_kernel,
        out_shape=(jax.ShapeDtypeStruct((8, 512, 256), jnp.float32),) * 2,
        in_specs=[pl.BlockSpec(memory_space=pltpu.SMEM)] + [any_spec] * 11,
        out_specs=(any_spec, any_spec),
        scratch_shapes=[
            pltpu.VMEM((1024, 2 * tokens), jnp.bfloat16),
            pltpu.VMEM((8, 2 * tokens, 256), jnp.bfloat16),
            pltpu.VMEM((8, 1024, 256), jnp.float32),
            pltpu.SemaphoreType.DMA((6,)),
            pltpu.SemaphoreType.DMA((4, 4, 2)),
            pltpu.SemaphoreType.DMA((2, 8)),
        ],
        compiler_params=pltpu.CompilerParams(vmem_limit_bytes=62 * 2**20),
        cost_estimate=pl.CostEstimate(flops=2**20, bytes_accessed=2**20, transcendentals=0),
    )(meta, *rows, *first_bufs, *second_bufs)


def late_kernel(own, scale, *refs):
    meta, row_ref, first_refs, second_refs, early_ref = refs[0], refs[1], refs[2:6], refs[6:10], refs[10]
    refs = refs[11:]
    if own:
        other_ref, out_ref, rows, cols, acc, other, row_sem, col_sem, sem, other_sem = refs
    else:
        out_ref, rows, cols, acc, row_sem, col_sem, sem = refs
    tokens = row_ref.shape[2]
    wanted = meta[24] if own else 1 - meta[24]
    mine = [meta[8 + slot] // 2 == wanted for slot in (6, 7)]
    needed = lambda side: (mine[0] & (meta[22] == side)) | (mine[1] & (meta[23] == side))
    row_copies = [
        (mine[i], pltpu.make_async_copy(row_ref.at[i], rows.at[i], row_sem.at[i])) for i in range(2)
    ]
    groups = []
    for j in range(4):
        group = column_copies(meta, first_refs, second_refs, cols, col_sem, j, needed)
        for pair in range(2):
            k, a = 2 * j + pair, column(meta, j, pair)
            group.append((True, pltpu.make_async_copy(early_ref.at[a], acc.at[k], sem.at[k])))
            if own:
                copy = pltpu.make_async_copy(other_ref.at[a], other.at[k], other_sem.at[k])
                group.append((True, copy))
        groups.append(group)
    start_all(row_copies)
    start_all(groups[0])
    start_all(groups[1])
    wait_all(row_copies)
    row_ids = meta[25] + lax.broadcasted_iota(jnp.int32, (512, 128), 0)
    lane = meta[26] + lax.broadcasted_iota(jnp.int32, (512, 128), 1)
    out_copies = []
    for j in range(4):
        wait_all(groups[j])
        if j + 2 < 4:
            start_all(groups[j + 2])
        for i in range(2):
            @pl.when(mine[i])
            def _(i=i):
                at = pl.ds(pl.multiple_of((meta[14 + i] % 2) * 256, 256), 256)
                side = pl.ds(pl.multiple_of(meta[22 + i] * tokens, tokens), tokens)
                for pair in range(2):
                    k = 2 * j + pair
                    acc[k, at, :] += jnp.dot(
                        rows[i], cols[k, side, :], preferred_element_type=jnp.float32
                    )
        for pair in range(2):
            k, a = 2 * j + pair, column(meta, j, pair)
            if own:
                for h in range(2):
                    at = slice(h * 128, (h + 1) * 128)
                    part = (acc[k, :, at] + other[k, :, at]) * scale
                    same = row_ids == lane + (a * 2048 + h * 128)
                    out_ref[pl.ds(2 * a + h, 512, stride=16), :] = jnp.where(
                        same, part, reg_alpha * part
                    )
            else:
                copy = pltpu.make_async_copy(acc.at[k], out_ref.at[a], sem.at[k])
                copy.start()
                out_copies.append(copy)
    for copy in out_copies:
        copy.wait()


def late_part(scale, meta, row, first_bufs, second_bufs, early, other=None):
    own = other is not None
    tokens = row.shape[2]
    any_spec = pl.BlockSpec(memory_space=pl.ANY)
    shape = (512 * 16, 128) if own else (8, 512, 256)
    half = pltpu.VMEM((8, 512, 256), jnp.float32)
    return pl.pallas_call(
        functools.partial(late_kernel, own, scale),
        out_shape=jax.ShapeDtypeStruct(shape, jnp.float32),
        in_specs=[pl.BlockSpec(memory_space=pltpu.SMEM)] + [any_spec] * (10 + own),
        out_specs=pl.BlockSpec(memory_space=pltpu.VMEM) if own else any_spec,
        scratch_shapes=[
            pltpu.VMEM((2, 256, tokens), jnp.bfloat16),
            pltpu.VMEM((8, 2 * tokens, 256), jnp.bfloat16),
        ]
        + [half] * (1 + own)
        + [
            pltpu.SemaphoreType.DMA((2,)),
            pltpu.SemaphoreType.DMA((4, 4, 2)),
            pltpu.SemaphoreType.DMA((8,)),
        ]
        + [pltpu.SemaphoreType.DMA((8,))] * own,
        compiler_params=pltpu.CompilerParams(vmem_limit_bytes=62 * 2**20),
        cost_estimate=pl.CostEstimate(
            flops=2 * 512 * 2048 * 2 * tokens, bytes_accessed=24 * 2**20, transcendentals=0
        ),
    )(meta, row, *first_bufs, *second_bufs, early, *([other] if own else []))


def lead_kernel(*refs):
    meta, row_ref, first_refs, second_refs = refs[0], refs[1], refs[2:6], refs[6:10]
    early_refs, out_refs = refs[10:12], refs[12:14]
    rows, cols, row_sem, col_sem, sem = refs[14:]
    tokens = row_ref.shape[2]
    half = tokens // 2
    copies = [
        (True, pltpu.make_async_copy(row_ref.at[i], rows.at[i], row_sem.at[i])) for i in range(2)
    ]
    for h in range(2):
        copies.append((True, pltpu.make_async_copy(early_refs[h].at[0], out_refs[h], sem.at[h])))
    for j in range(4):
        for i in range(4):
            side = meta[i] % 2
            want = (meta[i] // 2 == 0) & (meta[4 + j] == 0)
            for which, ref in ((0, first_refs[j].at[i]), (1, second_refs[i].at[j])):
                dst = cols.at[pl.ds(pl.multiple_of(side * tokens + which * half, half), half)]
                copies.append((want, pltpu.make_async_copy(ref, dst, col_sem.at[j, i, which])))
    start_all(copies)
    wait_all(copies)
    for i in range(2):
        at = pl.ds(pl.multiple_of((meta[14 + i] % 2) * 256, 256), 256)
        side = pl.ds(pl.multiple_of(meta[22 + i] * tokens, tokens), tokens)
        part = jnp.dot(rows[i], cols[side, :], preferred_element_type=jnp.float32)
        for h in range(2):
            @pl.when((meta[14 + i] // 2 == meta[24]) == (h == 0))
            def _(h=h, at=at, part=part):
                out_refs[h][at, :] += part


def lead_part(meta, row, first_bufs, second_bufs, early_own, early_away):
    tokens = row.shape[2]
    any_spec = pl.BlockSpec(memory_space=pl.ANY)
    vmem = pl.BlockSpec(memory_space=pltpu.VMEM)
    return pl.pallas_call(
        lead_kernel,
        out_shape=(jax.ShapeDtypeStruct((512, 256), jnp.float32),) * 2,
        in_specs=[pl.BlockSpec(memory_space=pltpu.SMEM)] + [any_spec] * 11,
        out_specs=(vmem, vmem),
        scratch_shapes=[
            pltpu.VMEM((2, 256, tokens), jnp.bfloat16),
            pltpu.VMEM((2 * tokens, 256), jnp.bfloat16),
            pltpu.SemaphoreType.DMA((2,)),
            pltpu.SemaphoreType.DMA((4, 4, 2)),
            pltpu.SemaphoreType.DMA((2,)),
        ],
        compiler_params=pltpu.CompilerParams(vmem_limit_bytes=62 * 2**20),
        cost_estimate=pl.CostEstimate(flops=2**30, bytes_accessed=4 * 2**20, transcendentals=0),
    )(meta, row, *first_bufs, *second_bufs, early_own, early_away)


def dot_t(a, b):
    return lax.dot_general(
        a, b, (((0,), (0,)), ((), ())), precision=HIGHEST, preferred_element_type=jnp.float32
    )


def dot_n(a, b):
    return lax.dot_general(
        a, b, (((1,), (0,)), ((), ())), precision=HIGHEST, preferred_element_type=jnp.float32
    )


def factor_block(k, work, u_ref, inv_ref, block):
    n, nb, np_ = 512, 128, 16
    lo, hi = k * nb, (k + 1) * nb
    sub = lax.broadcasted_iota(jnp.int32, (np_, nb), 0)
    sub2 = lax.broadcasted_iota(jnp.int32, (np_, 2 * nb), 0)
    lane2 = lax.broadcasted_iota(jnp.int32, (np_, 2 * nb), 1)
    block[:, :nb] = work[lo:hi, lo:hi]
    block[:, nb:] = (
        lax.broadcasted_iota(jnp.int32, (nb, nb), 0) == lax.broadcasted_iota(jnp.int32, (nb, nb), 1)
    ).astype(jnp.float32)
    for base in range(0, nb, np_):
        end = base + np_
        v = block[base:end, :]
        pc = [jnp.broadcast_to(v[:, base + i:base + i + 1], (np_, nb)) for i in range(np_)]
        for i in range(np_):
            s = lax.rsqrt(pc[i][i:i + 1, :])
            below = jnp.where(sub > i, pc[i] * s, 0.0)
            for j in range(i + 1, np_):
                pc[j] = pc[j] - below * (pc[j][i:i + 1, :] * s)
            u = v[i:i + 1, :] * jnp.concatenate([s, s], 1)
            v = jnp.where(sub2 == i, u, v - jnp.concatenate([below, below], 1) * u)
        v = jnp.where(lane2 >= base + sub2, v, 0.0)
        block[base:end, :] = v
        if end < nb:
            block[end:, :] -= dot_t(v[:, :nb], v)[end:]
    x = block[:, nb:]
    u_ref[lo:hi, lo:hi] = block[:, :nb]
    inv_ref[lo:hi, lo:hi] = x
    if k:
        inner = dot_t(u_ref[0:lo, lo:hi], inv_ref[0:lo, 0:lo])
        inv_ref[lo:hi, 0:lo] = -dot_n(x, inner)
    if hi < n:
        right = dot_n(x, work[lo:hi, hi:n])
        u_ref[lo:hi, hi:n] = right
        work[hi:n, hi:n] -= dot_t(right, right)


def factor_first(scale, sums, work, u_ref, inv_ref, block):
    rid = lax.broadcasted_iota(jnp.int32, (256, 256), 0)
    cid = lax.broadcasted_iota(jnp.int32, (256, 256), 1)

    def regular(part):
        return jnp.where(rid == cid, part * scale, reg_alpha * (part * scale))

    work[...] = jnp.zeros((512, 512), jnp.float32)
    work[:256, :256] = regular(sums[:256])
    work[:256, 256:] = reg_alpha * (sums[256:512] * scale)
    work[256:, 256:] = regular(sums[512:])
    u_ref[...] = jnp.zeros((512, 512), jnp.float32)
    inv_ref[...] = jnp.zeros((512, 512), jnp.float32)
    for k in (0, 1):
        factor_block(k, work, u_ref, inv_ref, block)


def factor_second(work_ref, u_in, inv_in, u_ref, inv_ref, work, block):
    work[...] = work_ref[...]
    u_ref[...] = u_in[...]
    inv_ref[...] = inv_in[...]
    for k in (2, 3):
        factor_block(k, work, u_ref, inv_ref, block)


def factor_part(kernel, n_out, args):
    full = pl.BlockSpec(memory_space=pltpu.VMEM)
    shape = jax.ShapeDtypeStruct((512, 512), jnp.float32)
    small = pltpu.VMEM((128, 256), jnp.float32)
    return pl.pallas_call(
        kernel,
        out_shape=(shape,) * n_out,
        in_specs=[full] * len(args),
        out_specs=(full,) * n_out,
        scratch_shapes=[pltpu.VMEM((512, 512), jnp.float32)] * (3 - n_out) + [small],
        compiler_params=pltpu.CompilerParams(vmem_limit_bytes=32 * 2**20),
        cost_estimate=pl.CostEstimate(flops=2**20, bytes_accessed=2**20, transcendentals=512),
    )(*args)


def per_device(acts_one, acts_two):
    cal, row, z = (lax.axis_index(a) for a in AXES)
    low, core = cal // 2, cal % 2
    total_tokens = 8 * acts_one.shape[0]
    scale = 1.0 / total_tokens
    device = (cal * 8 + row) * 8 + z
    meta = lax.dynamic_index_in_dim(jnp.asarray(TABLE), device, 0, keepdims=False)
    after = lax.optimization_barrier
    root = lambda x, y, z: (x // 2, y) == (0, 0) and z < 2

    cols = jnp.concatenate([acts_one, acts_two], 0)
    other = move(cols, lambda x, y, z, c: (x, y, 1 - z, c) if root(x, y, z) else None)
    a0, b0 = acts_one[None], acts_two[None]
    a01 = jnp.concatenate([a0, move(a0, x_step(0))], 0)
    b01 = jnp.concatenate([b0, move(b0, y_step(0))], 0)
    a23 = move(a01, x_step(1))
    b23 = move(b01, y_step(1))
    one_t = move(acts_one.T, row_home)
    two_t = acts_two.T
    a01, a23, b01, b23, other, one_t, two_t = after((a01, a23, b01, b23, other, one_t, two_t))

    two_t = move(two_t, row_home)
    left, right = jnp.where(z == 0, cols, other), jnp.where(z == 0, other, cols)
    part = [
        lax.dot_general(p, q, (((0,), (0,)), ((), ())), preferred_element_type=jnp.float32)
        for p, q in ((left, left), (left, right), (right, right))
    ]
    part = jnp.concatenate(part, 0).reshape(2, 2, 192, 256)
    pick = lambda value, at: lax.dynamic_index_in_dim(value, at, 0, keepdims=False)
    away = move(pick(part, 1 - core), lambda x, y, z, c: (x, y, z, 1 - c) if root(x, y, z) else None)
    lead = pick(part, core) + away
    away = move(pick(lead, 1 - low), lambda x, y, z, c: (x ^ 1, y, z, c) if root(x, y, z) else None)
    lead = jnp.where(row == 0, pick(lead, low) + away, 0.0)
    first = jnp.concatenate([a01, a23], 0)
    second = jnp.concatenate([b01, b23], 0)
    r0 = jnp.concatenate([one_t, two_t], 1)[None]
    r0, first, second, lead = after((r0, first, second, lead))

    r01 = jnp.concatenate([r0, move(r0, z_step(0))], 0)
    first1 = move(first, y_step(0))
    second1 = move(second, x_step(0))
    lead = lead + move(lead, lambda x, y, z, c: (x + 2, y, z, c) if root(x, y, z) else None)
    lead = lead + move(lead, lambda x, y, z, c: (x, 1, z, c) if y == 0 and z < 2 else None)
    lead = lead + move(lead, lambda x, y, z, c: (x, 3 - y, z, c) if y < 2 and z < 2 else None)
    r01, lead, first, first1, second, second1 = after((r01, lead, first, first1, second, second1))

    r2 = move(r01, z_step(1))
    first2 = move(first, y_step(1))
    second2 = move(second, x_step(1))
    theirs = move(lead, lambda x, y, z, c: (x ^ 1, y, z, c) if z < 2 else None)
    lead = jnp.where(low == 0, jnp.stack([lead, theirs]), jnp.stack([theirs, lead]))
    theirs = move(lead, lambda x, y, z, c: (x, y, z, 1 - c) if z < 2 else None)
    lead = jnp.where(core == 0, jnp.stack([lead, theirs]), jnp.stack([theirs, lead]))
    state = factor_part(functools.partial(factor_first, scale), 3, (lead.reshape(768, 256),))
    r01, r2, first, first1, first2, second, second1, second2, state = after(
        (r01, r2, first, first1, first2, second, second1, second2, state)
    )

    r3 = move(r2, z_step(2))
    first3 = move(first1, y_step(1))
    second3 = move(second1, x_step(1))
    upper, inverse = factor_part(factor_second, 2, state)
    rows, firsts, seconds, upper, inverse = after(
        (
            (r01, r2, r3),
            (first, first1, first2, first3),
            (second, second1, second2, second3),
            upper,
            inverse,
        )
    )

    row_start = row * 2048 + cal * 512
    meta = meta.at[25].set(row_start).at[26].set(z * 256)
    r4 = move(rows[2], z_step(3))
    early_own, early_away = early_part(meta, rows, firsts, seconds)
    r4, early_away, early_own, firsts, seconds = after((r4, early_away, early_own, firsts, seconds))

    block, away = lead_part(meta, r4, firsts, seconds, early_own, early_away)
    away, r4, early_away, firsts, seconds = after((away, r4, early_away, firsts, seconds))
    block = block + move(away, lambda x, y, z, c: (x, y, z, 1 - c) if z < 2 else None)
    block = block * scale
    row_ids = row_start + jnp.arange(512, dtype=jnp.int32)[:, None]
    col_ids = z * 256 + jnp.arange(256, dtype=jnp.int32)[None, :]
    block = jnp.where(row_ids == col_ids, block, reg_alpha * block)
    theirs = late_part(scale, meta, r4, firsts, seconds, early_away)
    block, theirs = after((block, theirs))
    theirs = move(theirs, core_swap)

    edge = z == 0
    solved = lax.dot_general(
        jnp.where(edge, inverse[:, :256], inverse[:, 256:]), block, (((1,), (1,)), ((), ())),
        precision=HIGHEST, preferred_element_type=jnp.float32,
    )
    head = jnp.where(edge, upper, 0.0)
    solved = jnp.where((row == 0) & (cal == 0), head, solved).reshape(8, 64, 512)
    share = [jnp.where(edge, solved[0], 0.0)]
    for i in range(1, 8):
        extra = i + 3 if i < 5 else None

        def target(x, y, z, c, i=i, extra=extra):
            if z == 0:
                return x, y, i, c
            return (x, y, extra, c) if z == 1 and extra is not None else None

        value = solved[i] if extra is None else jnp.where(edge, solved[i], solved[extra])
        share.append(move(value, target))

    gram_reg = late_part(scale, meta, r4, firsts, seconds, early_own, other=theirs)
    gram_reg, share = after((gram_reg, share))
    share = functools.reduce(jnp.add, share)
    return gram_reg.reshape(1, 512, 8, 1, 256), share.T.reshape(1, 512, 64)


def solution(mesh):
    return jax.shard_map(
        per_device,
        mesh=mesh,
        in_specs=(P("cal", ("row", "col")), P("cal", ("row", "col"))),
        out_specs=(P("row", "cal", None, "col", None), P("row", "cal", "col")),
        check_vma=False,
    )
```

```python
import functools

import jax
import jax.numpy as jnp
import numpy as np
from jax import lax
from jax.experimental import pallas as pl
from jax.experimental.pallas import tpu as pltpu
from jax.sharding import PartitionSpec as P

PANEL = 512
reg_alpha = 0.9
AXES = ("cal", "row", "col")
NX, NY, NZ = 4, 4, 8
HIGHEST = lax.Precision.HIGHEST


def flat(x, y, z, core):
    return (((x % 2) * 2 + core) * 8 + (x // 2) * 4 + y) * 8 + z


def devices():
    for x in range(NX):
        for y in range(NY):
            for z in range(NZ):
                for core in range(2):
                    yield x, y, z, core


def move(value, target):
    pairs = []
    for device in devices():
        to = target(*device)
        if to is not None:
            pairs.append((flat(*device), flat(*to)))
    return lax.ppermute(value, AXES, sorted(pairs))


def near(i, size, phase):
    return i ^ 1 if phase == 0 else (i + 1 if i % 2 else i - 1) % size


def x_step(s):
    return lambda x, y, z, c: (near(x, NX, (s + c) % 2), y, z, c)


def y_step(s):
    return lambda x, y, z, c: (x, near(y, NY, (s + c) % 2), z, c)


def z_step(s):
    return lambda x, y, z, c: (x, y, near(z, NZ, (s + c) % 2), c)


def core_swap(x, y, z, c):
    return x, y, z, 1 - c


def row_home(x, y, z, c):
    return (x, y, z, c) if z // 4 == x % 2 else (x ^ 1, y, 7 - z, c)


def tables():
    table = np.zeros((256, 32), np.int32)
    for x, y, z, c in devices():
        def ring4(i):
            p1 = lambda v: near(v, 4, c % 2)
            p2 = lambda v: near(v, 4, (1 + c) % 2)
            return [i, p1(i), p2(i), p1(p2(i))]

        step = lambda v, s: near(v, NZ, (s + c) % 2)
        first = lambda v: [v, step(v, 0)]
        third = lambda v: first(step(step(v, 2), 1))
        slots = first(z) + first(step(z, 1)) + third(z) + third(step(z, 3))
        assert sorted(slots) == list(range(8))
        low = x % 2
        blocks = [(p if p // 4 == low else 7 - p) - 4 * low for p in slots]
        halves = [low if p // 4 == low else 1 - low for p in slots]
        table[flat(x, y, z, c)] = ring4(x) + ring4(y) + blocks + halves + [c, low] + [0] * 6
    return table


TABLE = tables()


def column(meta, j, pair):
    x = jnp.where(meta[24] == 0, meta[2 * pair], meta[pair])
    return (x // 2) * 4 + meta[4 + j]


def column_copies(meta, first_refs, second_refs, cols, sem, j, needed=None):
    half = first_refs[0].shape[1]
    copies = []
    for i in range(4):
        pair = jnp.where(meta[24] == 0, i // 2, i % 2)
        side = meta[i] % 2
        for which, ref in ((0, first_refs[j].at[i]), (1, second_refs[i].at[j])):
            dst = cols.at[
                2 * j + pair,
                pl.ds(pl.multiple_of(side * 2 * half + which * half, half), half),
            ]
            want = True if needed is None else needed(side)
            copies.append((want, pltpu.make_async_copy(ref, dst, sem.at[j, i, which])))
    return copies


def start_all(copies):
    for want, copy in copies:
        pl.when(want)(copy.start)


def wait_all(copies):
    for want, copy in copies:
        pl.when(want)(copy.wait)


def early_kernel(*refs):
    meta, row_refs, first_refs, second_refs = refs[0], refs[1:4], refs[4:8], refs[8:12]
    own_ref, away_ref, rows, cols, acc, row_sem, col_sem, sem = refs[12:]
    tokens = row_refs[0].shape[2]

    def place(slot):
        at = jnp.where(meta[8 + slot] // 2 == meta[24], 0, 512) + (meta[8 + slot] % 2) * 256
        return rows.at[
            pl.ds(pl.multiple_of(at, 256), 256),
            pl.ds(pl.multiple_of(meta[16 + slot] * tokens, tokens), tokens),
        ]

    row_copies = [
        (True, pltpu.make_async_copy(row_refs[i // 2].at[i % 2], place(i), row_sem.at[i]))
        for i in range(6)
    ]
    col_copies = [column_copies(meta, first_refs, second_refs, cols, col_sem, j) for j in range(4)]
    start_all(row_copies)
    start_all(col_copies[0])
    start_all(col_copies[1])
    for slot in (6, 7):
        place(slot)[...] = jnp.zeros((256, tokens), rows.dtype)
    wait_all(row_copies)
    out_copies = []
    for j in range(4):
        wait_all(col_copies[j])
        if j + 2 < 4:
            start_all(col_copies[j + 2])

        def part(i, _, j=j):
            at = pl.ds(pl.multiple_of((i % 2) * 512, 512), 512)
            k = 2 * j + i // 2
            acc[k, at, :] = jnp.dot(rows[at, :], cols[k], preferred_element_type=jnp.float32)
            return 0

        lax.fori_loop(0, 4, part, 0)
        for pair in range(2):
            k = 2 * j + pair
            for h, ref in ((0, own_ref), (1, away_ref)):
                copy = pltpu.make_async_copy(
                    acc.at[k, pl.ds(h * 512, 512)], ref.at[column(meta, j, pair)], sem.at[h, k]
                )
                copy.start()
                out_copies.append(copy)
    for copy in out_copies:
        copy.wait()


def early_part(meta, rows, first_bufs, second_bufs):
    tokens = rows[0].shape[2]
    any_spec = pl.BlockSpec(memory_space=pl.ANY)
    return pl.pallas_call(
        early_kernel,
        out_shape=(jax.ShapeDtypeStruct((8, 512, 256), jnp.float32),) * 2,
        in_specs=[pl.BlockSpec(memory_space=pltpu.SMEM)] + [any_spec] * 11,
        out_specs=(any_spec, any_spec),
        scratch_shapes=[
            pltpu.VMEM((1024, 2 * tokens), jnp.bfloat16),
            pltpu.VMEM((8, 2 * tokens, 256), jnp.bfloat16),
            pltpu.VMEM((8, 1024, 256), jnp.float32),
            pltpu.SemaphoreType.DMA((6,)),
            pltpu.SemaphoreType.DMA((4, 4, 2)),
            pltpu.SemaphoreType.DMA((2, 8)),
        ],
        compiler_params=pltpu.CompilerParams(vmem_limit_bytes=62 * 2**20),
        cost_estimate=pl.CostEstimate(flops=2**20, bytes_accessed=2**20, transcendentals=0),
    )(meta, *rows, *first_bufs, *second_bufs)


def late_kernel(own, scale, *refs):
    meta, row_ref, first_refs, second_refs, early_ref = refs[0], refs[1], refs[2:6], refs[6:10], refs[10]
    refs = refs[11:]
    if own:
        other_ref, out_ref, rows, cols, acc, other, row_sem, col_sem, sem, other_sem = refs
    else:
        out_ref, rows, cols, acc, row_sem, col_sem, sem = refs
    tokens = row_ref.shape[2]
    wanted = meta[24] if own else 1 - meta[24]
    mine = [meta[8 + slot] // 2 == wanted for slot in (6, 7)]
    needed = lambda side: (mine[0] & (meta[22] == side)) | (mine[1] & (meta[23] == side))
    row_copies = [
        (mine[i], pltpu.make_async_copy(row_ref.at[i], rows.at[i], row_sem.at[i])) for i in range(2)
    ]
    groups = []
    for j in range(4):
        group = column_copies(meta, first_refs, second_refs, cols, col_sem, j, needed)
        for pair in range(2):
            k, a = 2 * j + pair, column(meta, j, pair)
            group.append((True, pltpu.make_async_copy(early_ref.at[a], acc.at[k], sem.at[k])))
            if own:
                copy = pltpu.make_async_copy(other_ref.at[a], other.at[k], other_sem.at[k])
                group.append((True, copy))
        groups.append(group)
    start_all(row_copies)
    start_all(groups[0])
    start_all(groups[1])
    wait_all(row_copies)
    row_ids = meta[25] + lax.broadcasted_iota(jnp.int32, (512, 128), 0)
    lane = meta[26] + lax.broadcasted_iota(jnp.int32, (512, 128), 1)
    out_copies = []
    for j in range(4):
        wait_all(groups[j])
        if j + 2 < 4:
            start_all(groups[j + 2])
        for i in range(2):
            @pl.when(mine[i])
            def _(i=i):
                at = pl.ds(pl.multiple_of((meta[14 + i] % 2) * 256, 256), 256)
                side = pl.ds(pl.multiple_of(meta[22 + i] * tokens, tokens), tokens)
                for pair in range(2):
                    k = 2 * j + pair
                    acc[k, at, :] += jnp.dot(
                        rows[i], cols[k, side, :], preferred_element_type=jnp.float32
                    )
        for pair in range(2):
            k, a = 2 * j + pair, column(meta, j, pair)
            if own:
                for h in range(2):
                    at = slice(h * 128, (h + 1) * 128)
                    part = (acc[k, :, at] + other[k, :, at]) * scale
                    same = row_ids == lane + (a * 2048 + h * 128)
                    out_ref[pl.ds(2 * a + h, 512, stride=16), :] = jnp.where(
                        same, part, reg_alpha * part
                    )
            else:
                copy = pltpu.make_async_copy(acc.at[k], out_ref.at[a], sem.at[k])
                copy.start()
                out_copies.append(copy)
    for copy in out_copies:
        copy.wait()


def late_part(scale, meta, row, first_bufs, second_bufs, early, other=None):
    own = other is not None
    tokens = row.shape[2]
    any_spec = pl.BlockSpec(memory_space=pl.ANY)
    shape = (512 * 16, 128) if own else (8, 512, 256)
    half = pltpu.VMEM((8, 512, 256), jnp.float32)
    return pl.pallas_call(
        functools.partial(late_kernel, own, scale),
        out_shape=jax.ShapeDtypeStruct(shape, jnp.float32),
        in_specs=[pl.BlockSpec(memory_space=pltpu.SMEM)] + [any_spec] * (10 + own),
        out_specs=pl.BlockSpec(memory_space=pltpu.VMEM) if own else any_spec,
        scratch_shapes=[
            pltpu.VMEM((2, 256, tokens), jnp.bfloat16),
            pltpu.VMEM((8, 2 * tokens, 256), jnp.bfloat16),
        ]
        + [half] * (1 + own)
        + [
            pltpu.SemaphoreType.DMA((2,)),
            pltpu.SemaphoreType.DMA((4, 4, 2)),
            pltpu.SemaphoreType.DMA((8,)),
        ]
        + [pltpu.SemaphoreType.DMA((8,))] * own,
        compiler_params=pltpu.CompilerParams(vmem_limit_bytes=62 * 2**20),
        cost_estimate=pl.CostEstimate(
            flops=2 * 512 * 2048 * 2 * tokens, bytes_accessed=24 * 2**20, transcendentals=0
        ),
    )(meta, row, *first_bufs, *second_bufs, early, *([other] if own else []))


def lead_kernel(*refs):
    meta, row_ref, first_refs, second_refs = refs[0], refs[1], refs[2:6], refs[6:10]
    early_refs, out_refs = refs[10:12], refs[12:14]
    rows, cols, row_sem, col_sem, sem = refs[14:]
    tokens = row_ref.shape[2]
    half = tokens // 2
    copies = [
        (True, pltpu.make_async_copy(row_ref.at[i], rows.at[i], row_sem.at[i])) for i in range(2)
    ]
    for h in range(2):
        copies.append((True, pltpu.make_async_copy(early_refs[h].at[0], out_refs[h], sem.at[h])))
    for j in range(4):
        for i in range(4):
            side = meta[i] % 2
            want = (meta[i] // 2 == 0) & (meta[4 + j] == 0)
            for which, ref in ((0, first_refs[j].at[i]), (1, second_refs[i].at[j])):
                dst = cols.at[pl.ds(pl.multiple_of(side * tokens + which * half, half), half)]
                copies.append((want, pltpu.make_async_copy(ref, dst, col_sem.at[j, i, which])))
    start_all(copies)
    wait_all(copies)
    for i in range(2):
        at = pl.ds(pl.multiple_of((meta[14 + i] % 2) * 256, 256), 256)
        side = pl.ds(pl.multiple_of(meta[22 + i] * tokens, tokens), tokens)
        part = jnp.dot(rows[i], cols[side, :], preferred_element_type=jnp.float32)
        for h in range(2):
            @pl.when((meta[14 + i] // 2 == meta[24]) == (h == 0))
            def _(h=h, at=at, part=part):
                out_refs[h][at, :] += part


def lead_part(meta, row, first_bufs, second_bufs, early_own, early_away):
    tokens = row.shape[2]
    any_spec = pl.BlockSpec(memory_space=pl.ANY)
    vmem = pl.BlockSpec(memory_space=pltpu.VMEM)
    return pl.pallas_call(
        lead_kernel,
        out_shape=(jax.ShapeDtypeStruct((512, 256), jnp.float32),) * 2,
        in_specs=[pl.BlockSpec(memory_space=pltpu.SMEM)] + [any_spec] * 11,
        out_specs=(vmem, vmem),
        scratch_shapes=[
            pltpu.VMEM((2, 256, tokens), jnp.bfloat16),
            pltpu.VMEM((2 * tokens, 256), jnp.bfloat16),
            pltpu.SemaphoreType.DMA((2,)),
            pltpu.SemaphoreType.DMA((4, 4, 2)),
            pltpu.SemaphoreType.DMA((2,)),
        ],
        compiler_params=pltpu.CompilerParams(vmem_limit_bytes=62 * 2**20),
        cost_estimate=pl.CostEstimate(flops=2**30, bytes_accessed=4 * 2**20, transcendentals=0),
    )(meta, row, *first_bufs, *second_bufs, early_own, early_away)


def dot_t(a, b):
    return lax.dot_general(
        a, b, (((0,), (0,)), ((), ())), precision=HIGHEST, preferred_element_type=jnp.float32
    )


def dot_n(a, b):
    return lax.dot_general(
        a, b, (((1,), (0,)), ((), ())), precision=HIGHEST, preferred_element_type=jnp.float32
    )


def sums_kernel(meta, own, other, mine_ref, away_ref, sums):
    def dot(p, q):
        return lax.dot_general(
            p[0], q[0], (((1,), (1,)), ((), ())), preferred_element_type=jnp.float32
        )

    @pl.when(meta[26] == 0)
    def _():
        sums[:256] = dot(own, own)
        sums[256:512] = dot(own, other)
        sums[512:] = dot(other, other)

    @pl.when(meta[26] != 0)
    def _():
        sums[:256] = dot(other, other)
        sums[256:512] = dot(other, own)
        sums[512:] = dot(own, own)

    mine_ref[...] = sums[pl.ds(pl.multiple_of(meta[24] * 384, 128), 384), :]
    away_ref[...] = sums[pl.ds(pl.multiple_of((1 - meta[24]) * 384, 128), 384), :]


def leading_sums(meta, own, other):
    full = pl.BlockSpec(memory_space=pltpu.VMEM)
    return pl.pallas_call(
        sums_kernel,
        out_shape=(jax.ShapeDtypeStruct((384, 256), jnp.float32),) * 2,
        in_specs=[pl.BlockSpec(memory_space=pltpu.SMEM), full, full],
        out_specs=(full, full),
        scratch_shapes=[pltpu.VMEM((768, 256), jnp.float32)],
        compiler_params=pltpu.CompilerParams(vmem_limit_bytes=32 * 2**20),
        cost_estimate=pl.CostEstimate(flops=2**30, bytes_accessed=2**20, transcendentals=0),
    )(meta, own, other)


def factor_block(k, work, u_ref, inv_ref, block):
    n, nb, np_ = 512, 128, 16
    lo, hi = k * nb, (k + 1) * nb
    sub = lax.broadcasted_iota(jnp.int32, (np_, nb), 0)
    sub2 = lax.broadcasted_iota(jnp.int32, (np_, 2 * nb), 0)
    lane2 = lax.broadcasted_iota(jnp.int32, (np_, 2 * nb), 1)
    block[:, :nb] = work[lo:hi, lo:hi]
    block[:, nb:] = (
        lax.broadcasted_iota(jnp.int32, (nb, nb), 0) == lax.broadcasted_iota(jnp.int32, (nb, nb), 1)
    ).astype(jnp.float32)
    for base in range(0, nb, np_):
        end = base + np_
        v = block[base:end, :]
        pc = [jnp.broadcast_to(v[:, base + i:base + i + 1], (np_, nb)) for i in range(np_)]
        for i in range(np_):
            s = lax.rsqrt(pc[i][i:i + 1, :])
            below = jnp.where(sub > i, pc[i] * s, 0.0)
            for j in range(i + 1, np_):
                pc[j] = pc[j] - below * (pc[j][i:i + 1, :] * s)
            u = v[i:i + 1, :] * jnp.concatenate([s, s], 1)
            v = jnp.where(sub2 == i, u, v - jnp.concatenate([below, below], 1) * u)
        v = jnp.where(lane2 >= base + sub2, v, 0.0)
        block[base:end, :] = v
        if end < nb:
            block[end:, :] -= dot_t(v[:, :nb], v)[end:]
    x = block[:, nb:]
    u_ref[lo:hi, lo:hi] = block[:, :nb]
    inv_ref[lo:hi, lo:hi] = x
    if k:
        inner = dot_t(u_ref[0:lo, lo:hi], inv_ref[0:lo, 0:lo])
        inv_ref[lo:hi, 0:lo] = -dot_n(x, inner)
    if hi < n:
        right = dot_n(x, work[lo:hi, hi:n])
        u_ref[lo:hi, hi:n] = right
        work[hi:n, hi:n] -= dot_t(right, right)


def factor_first(scale, sums, work, u_ref, inv_ref, block):
    rid = lax.broadcasted_iota(jnp.int32, (256, 256), 0)
    cid = lax.broadcasted_iota(jnp.int32, (256, 256), 1)

    def regular(part):
        return jnp.where(rid == cid, part * scale, reg_alpha * (part * scale))

    work[...] = jnp.zeros((512, 512), jnp.float32)
    work[:256, :256] = regular(sums[:256])
    work[:256, 256:] = reg_alpha * (sums[256:512] * scale)
    work[256:, 256:] = regular(sums[512:])
    u_ref[...] = jnp.zeros((512, 512), jnp.float32)
    inv_ref[...] = jnp.zeros((512, 512), jnp.float32)
    for k in (0, 1):
        factor_block(k, work, u_ref, inv_ref, block)


def factor_second(work_ref, u_in, inv_in, u_ref, inv_ref, work, block):
    work[...] = work_ref[...]
    u_ref[...] = u_in[...]
    inv_ref[...] = inv_in[...]
    for k in (2, 3):
        factor_block(k, work, u_ref, inv_ref, block)


def factor_part(kernel, n_out, args):
    full = pl.BlockSpec(memory_space=pltpu.VMEM)
    shape = jax.ShapeDtypeStruct((512, 512), jnp.float32)
    small = pltpu.VMEM((128, 256), jnp.float32)
    return pl.pallas_call(
        kernel,
        out_shape=(shape,) * n_out,
        in_specs=[full] * len(args),
        out_specs=(full,) * n_out,
        scratch_shapes=[pltpu.VMEM((512, 512), jnp.float32)] * (3 - n_out) + [small],
        compiler_params=pltpu.CompilerParams(vmem_limit_bytes=32 * 2**20),
        cost_estimate=pl.CostEstimate(flops=2**20, bytes_accessed=2**20, transcendentals=512),
    )(*args)


def per_device(acts_one, acts_two):
    cal, row, z = (lax.axis_index(a) for a in AXES)
    low, core = cal // 2, cal % 2
    total_tokens = 8 * acts_one.shape[0]
    scale = 1.0 / total_tokens
    device = (cal * 8 + row) * 8 + z
    meta = lax.dynamic_index_in_dim(jnp.asarray(TABLE), device, 0, keepdims=False)
    after = lax.optimization_barrier
    root = lambda x, y, z: (x // 2, y) == (0, 0) and z < 2

    row_start = row * 2048 + cal * 512
    meta = meta.at[25].set(row_start).at[26].set(z * 256)

    piece = jnp.concatenate([acts_one.T, acts_two.T], 1)[None]
    other = move(piece, lambda x, y, z, c: (x, y, 1 - z, c) if root(x, y, z) else None)
    a0, b0 = acts_one[None], acts_two[None]
    a01 = jnp.concatenate([a0, move(a0, x_step(0))], 0)
    b01 = jnp.concatenate([b0, move(b0, y_step(0))], 0)
    a23 = move(a01, x_step(1))
    b23 = move(b01, y_step(1))
    first = jnp.concatenate([a01, a23], 0)
    first, b01, b23, other, piece = after((first, b01, b23, other, piece))

    r0 = move(piece, row_home)
    first1 = move(first, y_step(0))
    lead, away = leading_sums(meta, piece, other)
    lead = lead + move(away, lambda x, y, z, c: (x, y, z, 1 - c) if root(x, y, z) else None)
    lead = lead + move(lead, lambda x, y, z, c: (x ^ 1, y, z, c) if root(x, y, z) else None)
    lead = jnp.where(row == 0, lead, 0.0)
    second = jnp.concatenate([b01, b23], 0)
    r0, first, first1, second, lead = after((r0, first, first1, second, lead))

    r01 = jnp.concatenate([r0, move(r0, z_step(0))], 0)
    lead = lead + move(lead, lambda x, y, z, c: (x + 2, y, z, c) if root(x, y, z) else None)
    lead, second = after((lead, second))
    second1 = move(second, x_step(0))
    lead = lead + move(lead, lambda x, y, z, c: (x, 1, z, c) if y == 0 and z < 2 else None)
    lead = lead + move(lead, lambda x, y, z, c: (x, 3 - y, z, c) if y < 2 and z < 2 else None)
    r01, lead, first, first1, second, second1 = after((r01, lead, first, first1, second, second1))

    r2 = move(r01, z_step(1))
    first2 = move(first, y_step(1))
    second2 = move(second, x_step(1))
    theirs = move(lead, lambda x, y, z, c: (x, y, z, 1 - c) if z < 2 else None)
    lead = jnp.where(core == 0, jnp.stack([lead, theirs]), jnp.stack([theirs, lead]))
    state = factor_part(functools.partial(factor_first, scale), 3, (lead.reshape(768, 256),))
    r01, r2, first, first1, first2, second, second1, second2, state = after(
        (r01, r2, first, first1, first2, second, second1, second2, state)
    )

    r3 = move(r2, z_step(2))
    first3 = move(first1, y_step(1))
    second3 = move(second1, x_step(1))
    upper, inverse = factor_part(factor_second, 2, state)
    rows, firsts, seconds, upper, inverse = after(
        (
            (r01, r2, r3),
            (first, first1, first2, first3),
            (second, second1, second2, second3),
            upper,
            inverse,
        )
    )

    r4 = move(rows[2], z_step(3))
    early_own, early_away = early_part(meta, rows, firsts, seconds)
    r4, early_away, early_own, firsts, seconds = after((r4, early_away, early_own, firsts, seconds))

    block, away = lead_part(meta, r4, firsts, seconds, early_own, early_away)
    away, r4, early_away, firsts, seconds = after((away, r4, early_away, firsts, seconds))
    block = block + move(away, lambda x, y, z, c: (x, y, z, 1 - c) if z < 2 else None)
    block = block * scale
    row_ids = row_start + jnp.arange(512, dtype=jnp.int32)[:, None]
    col_ids = z * 256 + jnp.arange(256, dtype=jnp.int32)[None, :]
    block = jnp.where(row_ids == col_ids, block, reg_alpha * block)
    theirs = late_part(scale, meta, r4, firsts, seconds, early_away)
    block, theirs = after((block, theirs))
    theirs = move(theirs, core_swap)

    edge = z == 0
    solved = lax.dot_general(
        jnp.where(edge, inverse[:, :256], inverse[:, 256:]), block, (((1,), (1,)), ((), ())),
        precision=HIGHEST, preferred_element_type=jnp.float32,
    )
    head = jnp.where(edge, upper, 0.0)
    solved = jnp.where((row == 0) & (cal == 0), head, solved).reshape(4, 128, 512)
    share = jnp.where(edge, solved[0], 0.0)
    for i in range(3):
        def target(x, y, z, c, i=i):
            if z == 0:
                return x, y, 2 * i + 2, c
            return (x, y, 2 * i + 4, c) if z == 1 and i < 2 else None

        value = jnp.where(edge, solved[i + 1], solved[i + 2]) if i < 2 else solved[3]
        share = share + move(value, target)
    odd = move(share[64:], lambda x, y, z, c: (x, y, z + 1, c) if z % 2 == 0 else None)

    gram_reg = late_part(scale, meta, r4, firsts, seconds, early_own, other=theirs)
    gram_reg, odd = after((gram_reg, odd))
    share = jnp.where(z % 2 == 0, share[:64], odd)
    return gram_reg.reshape(1, 512, 8, 1, 256), share.T.reshape(1, 512, 64)


def solution(mesh):
    return jax.shard_map(
        per_device,
        mesh=mesh,
        in_specs=(P("cal", ("row", "col")), P("cal", ("row", "col"))),
        out_specs=(P("row", "cal", None, "col", None), P("row", "cal", "col")),
        check_vma=False,
    )
```

```python
import functools

import jax
import jax.numpy as jnp
import numpy as np
from jax import lax
from jax.experimental import pallas as pl
from jax.experimental.pallas import tpu as pltpu
from jax.sharding import PartitionSpec as P

PANEL = 512
reg_alpha = 0.9
AXES = ("cal", "row", "col")
NX, NY, NZ = 4, 4, 8
HIGHEST = lax.Precision.HIGHEST


def flat(x, y, z, core):
    return (((x % 2) * 2 + core) * 8 + (x // 2) * 4 + y) * 8 + z


def devices():
    for x in range(NX):
        for y in range(NY):
            for z in range(NZ):
                for core in range(2):
                    yield x, y, z, core


def move(value, target):
    pairs = []
    for device in devices():
        to = target(*device)
        if to is not None:
            pairs.append((flat(*device), flat(*to)))
    return lax.ppermute(value, AXES, sorted(pairs))


def near(i, size, phase):
    return i ^ 1 if phase == 0 else (i + 1 if i % 2 else i - 1) % size


def x_step(s):
    return lambda x, y, z, c: (near(x, NX, (s + c) % 2), y, z, c)


def y_step(s):
    return lambda x, y, z, c: (x, near(y, NY, (s + c) % 2), z, c)


def z_step(s):
    return lambda x, y, z, c: (x, y, near(z, NZ, (s + c) % 2), c)


def core_swap(x, y, z, c):
    return x, y, z, 1 - c


def row_home(x, y, z, c):
    return (x, y, z, c) if z // 4 == x % 2 else (x ^ 1, y, 7 - z, c)


def tables():
    table = np.zeros((256, 32), np.int32)
    for x, y, z, c in devices():
        def ring4(i):
            p1 = lambda v: near(v, 4, c % 2)
            p2 = lambda v: near(v, 4, (1 + c) % 2)
            return [i, p1(i), p2(i), p1(p2(i))]

        step = lambda v, s: near(v, NZ, (s + c) % 2)
        first = lambda v: [v, step(v, 0)]
        third = lambda v: first(step(step(v, 2), 1))
        slots = first(z) + first(step(z, 1)) + third(z) + third(step(z, 3))
        assert sorted(slots) == list(range(8))
        low = x % 2
        blocks = [(p if p // 4 == low else 7 - p) - 4 * low for p in slots]
        halves = [low if p // 4 == low else 1 - low for p in slots]
        table[flat(x, y, z, c)] = ring4(x) + ring4(y) + blocks + halves + [c, low] + [0] * 6
    return table


TABLE = tables()


def column(meta, j, pair):
    x = jnp.where(meta[24] == 0, meta[2 * pair], meta[pair])
    return (x // 2) * 4 + meta[4 + j]


def column_copies(meta, first_refs, second_refs, cols, sem, j):
    half = first_refs[0].shape[1]
    copies = []
    for i in range(4):
        pair = jnp.where(meta[24] == 0, i // 2, i % 2)
        side = meta[i] % 2
        for which, ref in ((0, first_refs[j].at[i]), (1, second_refs[i].at[j])):
            dst = cols.at[
                2 * j + pair,
                pl.ds(pl.multiple_of(side * 2 * half + which * half, half), half),
            ]
            copies.append((True, pltpu.make_async_copy(ref, dst, sem.at[j, i, which])))
    return copies


def start_all(copies):
    for want, copy in copies:
        pl.when(want)(copy.start)


def wait_all(copies):
    for want, copy in copies:
        pl.when(want)(copy.wait)


def row_copies_of(meta, row_refs, rows, sem):
    tokens = row_refs[0].shape[2]
    wanted, refs = rows
    copies = []
    for slot in range(8):
        dst = refs.at[
            pl.ds(pl.multiple_of((meta[8 + slot] % 2) * 256, 256), 256),
            pl.ds(pl.multiple_of(meta[16 + slot] * tokens, tokens), tokens),
        ]
        copy = pltpu.make_async_copy(row_refs[slot // 2].at[slot % 2], dst, sem.at[slot])
        copies.append((meta[8 + slot] // 2 == wanted, copy))
    return copies


def gram_kernel(own, scale, *refs):
    meta, row_refs, first_refs, second_refs, refs = refs[0], refs[1:5], refs[5:9], refs[9:13], refs[13:]
    if own:
        other_ref, out_ref, rows, cols, acc, row_sem, col_sem, sem = refs
    else:
        out_ref, rows, cols, acc, row_sem, col_sem, sem = refs
    wanted = meta[24] if own else 1 - meta[24]
    row_copies = row_copies_of(meta, row_refs, (wanted, rows), row_sem)
    groups = []
    for j in range(4):
        group = column_copies(meta, first_refs, second_refs, cols, col_sem, j)
        if own:
            for pair in range(2):
                k = 2 * j + pair
                src = other_ref.at[column(meta, j, pair)]
                group.append((True, pltpu.make_async_copy(src, acc.at[k], sem.at[k])))
        groups.append(group)
    start_all(row_copies)
    start_all(groups[0])
    start_all(groups[1])
    row_ids = meta[25] + lax.broadcasted_iota(jnp.int32, (512, 128), 0)
    lane = meta[26] + lax.broadcasted_iota(jnp.int32, (512, 128), 1)
    wait_all(row_copies)
    out_copies = []
    for j in range(4):
        wait_all(groups[j])
        if j + 2 < 4:
            start_all(groups[j + 2])
        for pair in range(2):
            k, a = 2 * j + pair, column(meta, j, pair)
            total = jnp.dot(rows[...], cols[k], preferred_element_type=jnp.float32)
            if own:
                for h in range(2):
                    at = slice(h * 128, (h + 1) * 128)
                    part = (total[:, at] + acc[k, :, at]) * scale
                    same = row_ids == lane + (a * 2048 + h * 128)
                    out_ref[pl.ds(2 * a + h, 512, stride=16), :] = jnp.where(
                        same, part, reg_alpha * part
                    )
            else:
                acc[k] = total
                copy = pltpu.make_async_copy(acc.at[k], out_ref.at[a], sem.at[k])
                copy.start()
                out_copies.append(copy)
    for copy in out_copies:
        copy.wait()


def gram_part(scale, meta, row_bufs, first_bufs, second_bufs, other=None):
    own = other is not None
    tokens = row_bufs[0].shape[2]
    any_spec = pl.BlockSpec(memory_space=pl.ANY)
    shape = (512 * 16, 128) if own else (8, 512, 256)
    return pl.pallas_call(
        functools.partial(gram_kernel, own, scale),
        out_shape=jax.ShapeDtypeStruct(shape, jnp.float32),
        in_specs=[pl.BlockSpec(memory_space=pltpu.SMEM)] + [any_spec] * (12 + own),
        out_specs=pl.BlockSpec(memory_space=pltpu.VMEM) if own else any_spec,
        scratch_shapes=[
            pltpu.VMEM((512, 2 * tokens), jnp.bfloat16),
            pltpu.VMEM((8, 2 * tokens, 256), jnp.bfloat16),
            pltpu.VMEM((8, 512, 256), jnp.float32),
            pltpu.SemaphoreType.DMA((8,)),
            pltpu.SemaphoreType.DMA((4, 4, 2)),
            pltpu.SemaphoreType.DMA((8,)),
        ],
        compiler_params=pltpu.CompilerParams(vmem_limit_bytes=62 * 2**20),
        cost_estimate=pl.CostEstimate(
            flops=2 * 512 * 2048 * 2 * tokens, bytes_accessed=24 * 2**20, transcendentals=0
        ),
    )(meta, *row_bufs, *first_bufs, *second_bufs, *([other] if own else []))


def lead_kernel(*refs):
    meta, row_refs, first_refs, second_refs = refs[0], refs[1:5], refs[5:9], refs[9:13]
    out_ref, rows, cols, row_sem, col_sem = refs[13:]
    tokens = row_refs[0].shape[2]
    half = tokens // 2
    copies = row_copies_of(meta, row_refs, (meta[24], rows), row_sem)
    for j in range(4):
        for i in range(4):
            side = meta[i] % 2
            want = (meta[i] // 2 == 0) & (meta[4 + j] == 0)
            for which, ref in ((0, first_refs[j].at[i]), (1, second_refs[i].at[j])):
                dst = cols.at[pl.ds(pl.multiple_of(side * tokens + which * half, half), half)]
                copies.append((want, pltpu.make_async_copy(ref, dst, col_sem.at[j, i, which])))
    start_all(copies)
    wait_all(copies)
    out_ref[...] = jnp.dot(rows[...], cols[...], preferred_element_type=jnp.float32)


def lead_part(meta, row_bufs, first_bufs, second_bufs):
    tokens = row_bufs[0].shape[2]
    any_spec = pl.BlockSpec(memory_space=pl.ANY)
    return pl.pallas_call(
        lead_kernel,
        out_shape=jax.ShapeDtypeStruct((512, 256), jnp.float32),
        in_specs=[pl.BlockSpec(memory_space=pltpu.SMEM)] + [any_spec] * 12,
        out_specs=pl.BlockSpec(memory_space=pltpu.VMEM),
        scratch_shapes=[
            pltpu.VMEM((512, 2 * tokens), jnp.bfloat16),
            pltpu.VMEM((2 * tokens, 256), jnp.bfloat16),
            pltpu.SemaphoreType.DMA((8,)),
            pltpu.SemaphoreType.DMA((4, 4, 2)),
        ],
        compiler_params=pltpu.CompilerParams(vmem_limit_bytes=62 * 2**20),
        cost_estimate=pl.CostEstimate(flops=2**30, bytes_accessed=4 * 2**20, transcendentals=0),
    )(meta, *row_bufs, *first_bufs, *second_bufs)


def dot_t(a, b):
    return lax.dot_general(
        a, b, (((0,), (0,)), ((), ())), precision=HIGHEST, preferred_element_type=jnp.float32
    )


def dot_n(a, b):
    return lax.dot_general(
        a, b, (((1,), (0,)), ((), ())), precision=HIGHEST, preferred_element_type=jnp.float32
    )


def sums_kernel(meta, own, other, mine_ref, away_ref, sums):
    def dot(p, q):
        return lax.dot_general(
            p[0], q[0], (((1,), (1,)), ((), ())), preferred_element_type=jnp.float32
        )

    @pl.when(meta[26] == 0)
    def _():
        sums[:256] = dot(own, own)
        sums[256:512] = dot(own, other)
        sums[512:] = dot(other, other)

    @pl.when(meta[26] != 0)
    def _():
        sums[:256] = dot(other, other)
        sums[256:512] = dot(other, own)
        sums[512:] = dot(own, own)

    mine_ref[...] = sums[pl.ds(pl.multiple_of(meta[24] * 384, 128), 384), :]
    away_ref[...] = sums[pl.ds(pl.multiple_of((1 - meta[24]) * 384, 128), 384), :]


def leading_sums(meta, own, other):
    full = pl.BlockSpec(memory_space=pltpu.VMEM)
    return pl.pallas_call(
        sums_kernel,
        out_shape=(jax.ShapeDtypeStruct((384, 256), jnp.float32),) * 2,
        in_specs=[pl.BlockSpec(memory_space=pltpu.SMEM), full, full],
        out_specs=(full, full),
        scratch_shapes=[pltpu.VMEM((768, 256), jnp.float32)],
        compiler_params=pltpu.CompilerParams(vmem_limit_bytes=32 * 2**20),
        cost_estimate=pl.CostEstimate(flops=2**30, bytes_accessed=2**20, transcendentals=0),
    )(meta, own, other)


def factor_block(k, work, u_ref, inv_ref, block):
    n, nb, np_ = 512, 128, 16
    lo, hi = k * nb, (k + 1) * nb
    sub = lax.broadcasted_iota(jnp.int32, (np_, nb), 0)
    sub2 = lax.broadcasted_iota(jnp.int32, (np_, 2 * nb), 0)
    lane2 = lax.broadcasted_iota(jnp.int32, (np_, 2 * nb), 1)
    block[:, :nb] = work[lo:hi, lo:hi]
    block[:, nb:] = (
        lax.broadcasted_iota(jnp.int32, (nb, nb), 0) == lax.broadcasted_iota(jnp.int32, (nb, nb), 1)
    ).astype(jnp.float32)
    for base in range(0, nb, np_):
        end = base + np_
        v = block[base:end, :]
        pc = [jnp.broadcast_to(v[:, base + i:base + i + 1], (np_, nb)) for i in range(np_)]
        for i in range(np_):
            s = lax.rsqrt(pc[i][i:i + 1, :])
            below = jnp.where(sub > i, pc[i] * s, 0.0)
            for j in range(i + 1, np_):
                pc[j] = pc[j] - below * (pc[j][i:i + 1, :] * s)
            u = v[i:i + 1, :] * jnp.concatenate([s, s], 1)
            v = jnp.where(sub2 == i, u, v - jnp.concatenate([below, below], 1) * u)
        v = jnp.where(lane2 >= base + sub2, v, 0.0)
        block[base:end, :] = v
        if end < nb:
            block[end:, :] -= dot_t(v[:, :nb], v)[end:]
    x = block[:, nb:]
    u_ref[lo:hi, lo:hi] = block[:, :nb]
    inv_ref[lo:hi, lo:hi] = x
    if k:
        inner = dot_t(u_ref[0:lo, lo:hi], inv_ref[0:lo, 0:lo])
        inv_ref[lo:hi, 0:lo] = -dot_n(x, inner)
    if hi < n:
        right = dot_n(x, work[lo:hi, hi:n])
        u_ref[lo:hi, hi:n] = right
        work[hi:n, hi:n] -= dot_t(right, right)


def factor_first(scale, sums, work, u_ref, inv_ref, block):
    rid = lax.broadcasted_iota(jnp.int32, (256, 256), 0)
    cid = lax.broadcasted_iota(jnp.int32, (256, 256), 1)

    def regular(part):
        return jnp.where(rid == cid, part * scale, reg_alpha * (part * scale))

    work[...] = jnp.zeros((512, 512), jnp.float32)
    work[:256, :256] = regular(sums[:256])
    work[:256, 256:] = reg_alpha * (sums[256:512] * scale)
    work[256:, 256:] = regular(sums[512:])
    u_ref[...] = jnp.zeros((512, 512), jnp.float32)
    inv_ref[...] = jnp.zeros((512, 512), jnp.float32)
    for k in (0, 1):
        factor_block(k, work, u_ref, inv_ref, block)


def factor_second(work_ref, u_in, inv_in, u_ref, inv_ref, work, block):
    work[...] = work_ref[...]
    u_ref[...] = u_in[...]
    inv_ref[...] = inv_in[...]
    for k in (2, 3):
        factor_block(k, work, u_ref, inv_ref, block)


def factor_part(kernel, n_out, args):
    full = pl.BlockSpec(memory_space=pltpu.VMEM)
    shape = jax.ShapeDtypeStruct((512, 512), jnp.float32)
    small = pltpu.VMEM((128, 256), jnp.float32)
    return pl.pallas_call(
        kernel,
        out_shape=(shape,) * n_out,
        in_specs=[full] * len(args),
        out_specs=(full,) * n_out,
        scratch_shapes=[pltpu.VMEM((512, 512), jnp.float32)] * (3 - n_out) + [small],
        compiler_params=pltpu.CompilerParams(vmem_limit_bytes=32 * 2**20),
        cost_estimate=pl.CostEstimate(flops=2**20, bytes_accessed=2**20, transcendentals=512),
    )(*args)


def per_device(acts_one, acts_two):
    cal, row, z = (lax.axis_index(a) for a in AXES)
    low, core = cal // 2, cal % 2
    total_tokens = 8 * acts_one.shape[0]
    scale = 1.0 / total_tokens
    device = (cal * 8 + row) * 8 + z
    meta = lax.dynamic_index_in_dim(jnp.asarray(TABLE), device, 0, keepdims=False)
    after = lax.optimization_barrier
    root = lambda x, y, z: (x // 2, y) == (0, 0) and z < 2

    row_start = row * 2048 + cal * 512
    meta = meta.at[25].set(row_start).at[26].set(z * 256)

    piece = jnp.concatenate([acts_one.T, acts_two.T], 1)[None]
    other = move(piece, lambda x, y, z, c: (x, y, 1 - z, c) if root(x, y, z) else None)
    r0 = move(piece, row_home)
    a0, b0 = acts_one[None], acts_two[None]
    a01 = jnp.concatenate([a0, move(a0, x_step(0))], 0)
    b01 = jnp.concatenate([b0, move(b0, y_step(0))], 0)
    lead, away = leading_sums(meta, piece, other)
    lead = lead + move(away, lambda x, y, z, c: (x, y, z, 1 - c) if root(x, y, z) else None)
    r0, a01, b01, lead = after((r0, a01, b01, lead))

    r01 = jnp.concatenate([r0, move(r0, z_step(0))], 0)
    first = jnp.concatenate([a01, move(a01, x_step(1))], 0)
    second = jnp.concatenate([b01, move(b01, y_step(1))], 0)
    lead = lead + move(lead, lambda x, y, z, c: (x ^ 1, y, z, c) if root(x, y, z) else None)
    lead = jnp.where(row == 0, lead, 0.0)
    lead = lead + move(lead, lambda x, y, z, c: (x + 2, y, z, c) if root(x, y, z) else None)
    lead = lead + move(lead, lambda x, y, z, c: (x, 1, z, c) if y == 0 and z < 2 else None)
    r01, first, second, lead = after((r01, first, second, lead))

    r2 = move(r01, z_step(1))
    first1 = move(first, y_step(0))
    second1 = move(second, x_step(0))
    lead = lead + move(lead, lambda x, y, z, c: (x, 3 - y, z, c) if y < 2 and z < 2 else None)
    r01, r2, first, first1, second, second1, lead = after(
        (r01, r2, first, first1, second, second1, lead)
    )

    r3 = move(r2, z_step(2))
    first2 = move(first, y_step(1))
    second2 = move(second, x_step(1))
    theirs = move(lead, lambda x, y, z, c: (x, y, z, 1 - c) if z < 2 else None)
    lead = jnp.where(core == 0, jnp.stack([lead, theirs]), jnp.stack([theirs, lead]))
    state = factor_part(functools.partial(factor_first, scale), 3, (lead.reshape(768, 256),))
    r01, r2, r3, first, first1, first2, second, second1, second2, state = after(
        (r01, r2, r3, first, first1, first2, second, second1, second2, state)
    )

    r4 = move(r3, z_step(3))
    first3 = move(first1, y_step(1))
    second3 = move(second1, x_step(1))
    upper, inverse = factor_part(factor_second, 2, state)
    pieces, upper, inverse = after(
        (
            (
                (r01, r2, r3, r4),
                (first, first1, first2, first3),
                (second, second1, second2, second3),
            ),
            upper,
            inverse,
        )
    )

    theirs = gram_part(scale, meta, *pieces)
    theirs, pieces = after((theirs, pieces))
    away = move(theirs[0], lambda x, y, z, c: (x, y, z, 1 - c) if z < 2 else None)
    theirs = move(theirs, core_swap)
    block = (lead_part(meta, *pieces) + away) * scale
    row_ids = row_start + jnp.arange(512, dtype=jnp.int32)[:, None]
    col_ids = z * 256 + jnp.arange(256, dtype=jnp.int32)[None, :]
    block = jnp.where(row_ids == col_ids, block, reg_alpha * block)

    edge = z == 0
    solved = lax.dot_general(
        jnp.where(edge, inverse[:, :256], inverse[:, 256:]), block, (((1,), (1,)), ((), ())),
        precision=HIGHEST, preferred_element_type=jnp.float32,
    )
    head = jnp.where(edge, upper, 0.0)
    solved = jnp.where((row == 0) & (cal == 0), head, solved).reshape(4, 128, 512)
    parts = [jnp.where(edge, solved[0], 0.0)]
    for i in range(3):
        def target(x, y, z, c, i=i):
            if z == 0:
                return x, y, 2 * i + 2, c
            return (x, y, 2 * i + 4, c) if z == 1 and i < 2 else None

        value = jnp.where(edge, solved[i + 1], solved[i + 2]) if i < 2 else solved[3]
        parts.append(move(value, target))
    gram_reg = gram_part(scale, meta, *pieces, other=theirs)
    gram_reg, parts = after((gram_reg, parts))
    share = functools.reduce(jnp.add, parts)
    odd = move(share[64:], lambda x, y, z, c: (x, y, z + 1, c) if z % 2 == 0 else None)
    share = jnp.where(z % 2 == 0, share[:64], odd)
    return gram_reg.reshape(1, 512, 8, 1, 256), share.T.reshape(1, 512, 64)


def solution(mesh):
    return jax.shard_map(
        per_device,
        mesh=mesh,
        in_specs=(P("cal", ("row", "col")), P("cal", ("row", "col"))),
        out_specs=(P("row", "cal", None, "col", None), P("row", "cal", "col")),
        check_vma=False,
    )
```

```python
import functools

import jax
import jax.numpy as jnp
import numpy as np
from jax import lax
from jax.experimental import pallas as pl
from jax.experimental.pallas import tpu as pltpu
from jax.sharding import PartitionSpec as P

PANEL = 512
reg_alpha = 0.9
AXES = ("cal", "row", "col")
NX, NY, NZ = 4, 4, 8
HIGHEST = lax.Precision.HIGHEST


def flat(x, y, z, core):
    return (((x % 2) * 2 + core) * 8 + (x // 2) * 4 + y) * 8 + z


def devices():
    for x in range(NX):
        for y in range(NY):
            for z in range(NZ):
                for core in range(2):
                    yield x, y, z, core


def move(value, target):
    pairs = []
    for device in devices():
        to = target(*device)
        if to is not None:
            pairs.append((flat(*device), flat(*to)))
    return lax.ppermute(value, AXES, sorted(pairs))


def near(i, size, phase):
    return i ^ 1 if phase == 0 else (i + 1 if i % 2 else i - 1) % size


def x_step(s):
    return lambda x, y, z, c: (near(x, NX, (s + c) % 2), y, z, c)


def y_step(s):
    return lambda x, y, z, c: (x, near(y, NY, (s + c) % 2), z, c)


def z_step(s):
    return lambda x, y, z, c: (x, y, near(z, NZ, (s + c) % 2), c)


def core_swap(x, y, z, c):
    return x, y, z, 1 - c


def at_home(z, low):
    return z // 4 == low


def row_home(ends):
    def target(x, y, z, c):
        if at_home(z, x % 2) or (z % 4 in (0, 3)) != ends:
            return None
        return x ^ 1, y, 7 - z, c

    return target


def tables():
    table = np.zeros((256, 32), np.int32)
    for x, y, z, c in devices():
        def ring4(i):
            p1 = lambda v: near(v, 4, c % 2)
            p2 = lambda v: near(v, 4, (1 + c) % 2)
            return [i, p1(i), p2(i), p1(p2(i))]

        step = lambda v, s: near(v, NZ, (s + c) % 2)
        first = lambda v: [v, step(v, 0)]
        third = lambda v: first(step(step(v, 2), 1))
        slots = first(z) + first(step(z, 1)) + third(z) + third(step(z, 3))
        assert sorted(slots) == list(range(8))
        low = x % 2
        blocks = [(p if p // 4 == low else 7 - p) - 4 * low for p in slots]
        halves = [low if p // 4 == low else 1 - low for p in slots]
        table[flat(x, y, z, c)] = ring4(x) + ring4(y) + blocks + halves + [c, low] + [0] * 6
    return table


TABLE = tables()


def column(meta, j, pair):
    x = jnp.where(meta[24] == 0, meta[2 * pair], meta[pair])
    return (x // 2) * 4 + meta[4 + j]


def column_copies(meta, first_refs, second_refs, cols, sem, j):
    half = first_refs[0].shape[1]
    copies = []
    for i in range(4):
        pair = jnp.where(meta[24] == 0, i // 2, i % 2)
        side = meta[i] % 2
        for which, ref in ((0, first_refs[j].at[i]), (1, second_refs[i].at[j])):
            dst = cols.at[
                2 * j + pair,
                pl.ds(pl.multiple_of(side * 2 * half + which * half, half), half),
            ]
            copies.append((True, pltpu.make_async_copy(ref, dst, sem.at[j, i, which])))
    return copies


def start_all(copies):
    for want, copy in copies:
        pl.when(want)(copy.start)


def wait_all(copies):
    for want, copy in copies:
        pl.when(want)(copy.wait)


def row_copies_of(meta, row_refs, rows, sem):
    tokens = row_refs[0].shape[2]
    wanted, refs = rows
    copies = []
    for slot in range(8):
        dst = refs.at[
            pl.ds(pl.multiple_of((meta[8 + slot] % 2) * 256, 256), 256),
            pl.ds(pl.multiple_of(meta[16 + slot] * tokens, tokens), tokens),
        ]
        copy = pltpu.make_async_copy(row_refs[slot // 2].at[slot % 2], dst, sem.at[slot])
        copies.append((meta[8 + slot] // 2 == wanted, copy))
    return copies


def gram_kernel(own, scale, *refs):
    meta, row_refs, first_refs, second_refs, refs = refs[0], refs[1:5], refs[5:9], refs[9:13], refs[13:]
    if own:
        other_ref, out_ref, rows, cols, acc, row_sem, col_sem, sem = refs
    else:
        out_ref, lead_ref, away_ref, rows, cols, acc, row_sem, col_sem, sem, lead_rows, lead_sem = refs
    wanted = meta[24] if own else 1 - meta[24]
    row_copies = row_copies_of(meta, row_refs, (wanted, rows), row_sem)
    lead_copies = [] if own else row_copies_of(meta, row_refs, (1 - wanted, lead_rows), lead_sem)
    groups = []
    for j in range(4):
        group = column_copies(meta, first_refs, second_refs, cols, col_sem, j)
        if own:
            for pair in range(2):
                k = 2 * j + pair
                src = other_ref.at[column(meta, j, pair)]
                group.append((True, pltpu.make_async_copy(src, acc.at[k], sem.at[k])))
        groups.append(group)
    start_all(row_copies)
    start_all(groups[0])
    start_all(groups[1])
    start_all(lead_copies)
    row_ids = meta[25] + lax.broadcasted_iota(jnp.int32, (512, 128), 0)
    lane = meta[26] + lax.broadcasted_iota(jnp.int32, (512, 128), 1)
    wait_all(row_copies)
    out_copies = []
    for j in range(4):
        wait_all(groups[j])
        if j + 2 < 4:
            start_all(groups[j + 2])
        for pair in range(2):
            k, a = 2 * j + pair, column(meta, j, pair)
            total = jnp.dot(rows[...], cols[k], preferred_element_type=jnp.float32)
            if own:
                for h in range(2):
                    at = slice(h * 128, (h + 1) * 128)
                    part = (total[:, at] + acc[k, :, at]) * scale
                    same = row_ids == lane + (a * 2048 + h * 128)
                    out_ref[pl.ds(2 * a + h, 512, stride=16), :] = jnp.where(
                        same, part, reg_alpha * part
                    )
            else:
                acc[k] = total
                copy = pltpu.make_async_copy(acc.at[k], out_ref.at[a], sem.at[k])
                copy.start()
                out_copies.append(copy)
    if not own:
        at = sum((2 * j + p) * (column(meta, j, p) == 0) for j in range(4) for p in range(2))
        away_ref[...] = acc[at]
        wait_all(lead_copies)
        lead_ref[...] = jnp.dot(lead_rows[...], cols[at], preferred_element_type=jnp.float32)
    for copy in out_copies:
        copy.wait()


def gram_part(scale, meta, row_bufs, first_bufs, second_bufs, other=None):
    own = other is not None
    tokens = row_bufs[0].shape[2]
    any_spec = pl.BlockSpec(memory_space=pl.ANY)
    vmem = pl.BlockSpec(memory_space=pltpu.VMEM)
    shapes = ((512 * 16, 128),) if own else ((8, 512, 256), (512, 256), (512, 256))
    rows = pltpu.VMEM((512, 2 * tokens), jnp.bfloat16)
    return pl.pallas_call(
        functools.partial(gram_kernel, own, scale),
        out_shape=tuple(jax.ShapeDtypeStruct(shape, jnp.float32) for shape in shapes),
        in_specs=[pl.BlockSpec(memory_space=pltpu.SMEM)] + [any_spec] * (12 + own),
        out_specs=(vmem,) if own else (any_spec, vmem, vmem),
        scratch_shapes=[
            rows,
            pltpu.VMEM((8, 2 * tokens, 256), jnp.bfloat16),
            pltpu.VMEM((8, 512, 256), jnp.float32),
            pltpu.SemaphoreType.DMA((8,)),
            pltpu.SemaphoreType.DMA((4, 4, 2)),
            pltpu.SemaphoreType.DMA((8,)),
        ]
        + ([] if own else [rows, pltpu.SemaphoreType.DMA((8,))]),
        compiler_params=pltpu.CompilerParams(vmem_limit_bytes=62 * 2**20),
        cost_estimate=pl.CostEstimate(
            flops=2 * 512 * 2048 * 2 * tokens, bytes_accessed=24 * 2**20, transcendentals=0
        ),
    )(meta, *row_bufs, *first_bufs, *second_bufs, *([other] if own else []))


def dot_t(a, b):
    return lax.dot_general(
        a, b, (((0,), (0,)), ((), ())), precision=HIGHEST, preferred_element_type=jnp.float32
    )


def dot_n(a, b):
    return lax.dot_general(
        a, b, (((1,), (0,)), ((), ())), precision=HIGHEST, preferred_element_type=jnp.float32
    )


def sums_kernel(meta, own, other, mine_ref, away_ref, sums):
    def dot(p, q):
        return lax.dot_general(
            p[0], q[0], (((1,), (1,)), ((), ())), preferred_element_type=jnp.float32
        )

    @pl.when(meta[26] == 0)
    def _():
        sums[:256] = dot(own, own)
        sums[256:512] = dot(own, other)
        sums[512:] = dot(other, other)

    @pl.when(meta[26] != 0)
    def _():
        sums[:256] = dot(other, other)
        sums[256:512] = dot(other, own)
        sums[512:] = dot(own, own)

    mine_ref[...] = sums[pl.ds(pl.multiple_of(meta[24] * 384, 128), 384), :]
    away_ref[...] = sums[pl.ds(pl.multiple_of((1 - meta[24]) * 384, 128), 384), :]


def leading_sums(meta, own, other):
    full = pl.BlockSpec(memory_space=pltpu.VMEM)
    return pl.pallas_call(
        sums_kernel,
        out_shape=(jax.ShapeDtypeStruct((384, 256), jnp.float32),) * 2,
        in_specs=[pl.BlockSpec(memory_space=pltpu.SMEM), full, full],
        out_specs=(full, full),
        scratch_shapes=[pltpu.VMEM((768, 256), jnp.float32)],
        compiler_params=pltpu.CompilerParams(vmem_limit_bytes=32 * 2**20),
        cost_estimate=pl.CostEstimate(flops=2**30, bytes_accessed=2**20, transcendentals=0),
    )(meta, own, other)


def factor_block(k, work, u_ref, inv_ref, block):
    n, nb, np_ = 512, 128, 16
    lo, hi = k * nb, (k + 1) * nb
    sub = lax.broadcasted_iota(jnp.int32, (np_, nb), 0)
    sub2 = lax.broadcasted_iota(jnp.int32, (np_, 2 * nb), 0)
    lane2 = lax.broadcasted_iota(jnp.int32, (np_, 2 * nb), 1)
    block[:, :nb] = work[lo:hi, lo:hi]
    block[:, nb:] = (
        lax.broadcasted_iota(jnp.int32, (nb, nb), 0) == lax.broadcasted_iota(jnp.int32, (nb, nb), 1)
    ).astype(jnp.float32)
    for base in range(0, nb, np_):
        end = base + np_
        v = block[base:end, :]
        pc = [jnp.broadcast_to(v[:, base + i:base + i + 1], (np_, nb)) for i in range(np_)]
        for i in range(np_):
            s = lax.rsqrt(pc[i][i:i + 1, :])
            below = jnp.where(sub > i, pc[i] * s, 0.0)
            for j in range(i + 1, np_):
                pc[j] = pc[j] - below * (pc[j][i:i + 1, :] * s)
            u = v[i:i + 1, :] * jnp.concatenate([s, s], 1)
            v = jnp.where(sub2 == i, u, v - jnp.concatenate([below, below], 1) * u)
        v = jnp.where(lane2 >= base + sub2, v, 0.0)
        block[base:end, :] = v
        if end < nb:
            block[end:, :] -= dot_t(v[:, :nb], v)[end:]
    x = block[:, nb:]
    u_ref[lo:hi, lo:hi] = block[:, :nb]
    inv_ref[lo:hi, lo:hi] = x
    if k:
        inner = dot_t(u_ref[0:lo, lo:hi], inv_ref[0:lo, 0:lo])
        inv_ref[lo:hi, 0:lo] = -dot_n(x, inner)
    if hi < n:
        right = dot_n(x, work[lo:hi, hi:n])
        u_ref[lo:hi, hi:n] = right
        work[hi:n, hi:n] -= dot_t(right, right)


def factor_first(scale, sums, work, u_ref, inv_ref, block):
    rid = lax.broadcasted_iota(jnp.int32, (256, 256), 0)
    cid = lax.broadcasted_iota(jnp.int32, (256, 256), 1)

    def regular(part):
        return jnp.where(rid == cid, part * scale, reg_alpha * (part * scale))

    work[...] = jnp.zeros((512, 512), jnp.float32)
    work[:256, :256] = regular(sums[:256])
    work[:256, 256:] = reg_alpha * (sums[256:512] * scale)
    work[256:, 256:] = regular(sums[512:])
    u_ref[...] = jnp.zeros((512, 512), jnp.float32)
    inv_ref[...] = jnp.zeros((512, 512), jnp.float32)
    for k in (0, 1):
        factor_block(k, work, u_ref, inv_ref, block)


def factor_second(work_ref, u_in, inv_in, u_ref, inv_ref, work, block):
    work[...] = work_ref[...]
    u_ref[...] = u_in[...]
    inv_ref[...] = inv_in[...]
    for k in (2, 3):
        factor_block(k, work, u_ref, inv_ref, block)


def factor_part(kernel, n_out, args):
    full = pl.BlockSpec(memory_space=pltpu.VMEM)
    shape = jax.ShapeDtypeStruct((512, 512), jnp.float32)
    small = pltpu.VMEM((128, 256), jnp.float32)
    return pl.pallas_call(
        kernel,
        out_shape=(shape,) * n_out,
        in_specs=[full] * len(args),
        out_specs=(full,) * n_out,
        scratch_shapes=[pltpu.VMEM((512, 512), jnp.float32)] * (3 - n_out) + [small],
        compiler_params=pltpu.CompilerParams(vmem_limit_bytes=32 * 2**20),
        cost_estimate=pl.CostEstimate(flops=2**20, bytes_accessed=2**20, transcendentals=512),
    )(*args)


def per_device(acts_one, acts_two):
    cal, row, z = (lax.axis_index(a) for a in AXES)
    low, core = cal // 2, cal % 2
    total_tokens = 8 * acts_one.shape[0]
    scale = 1.0 / total_tokens
    device = (cal * 8 + row) * 8 + z
    meta = lax.dynamic_index_in_dim(jnp.asarray(TABLE), device, 0, keepdims=False)
    after = lax.optimization_barrier
    root = lambda x, y, z: (x // 2, y) == (0, 0) and z < 2

    row_start = row * 2048 + cal * 512
    meta = meta.at[25].set(row_start).at[26].set(z * 256)

    piece = jnp.concatenate([acts_one.T, acts_two.T], 1)[None]
    other = move(piece, lambda x, y, z, c: (x, y, 1 - z, c) if root(x, y, z) else None)
    ends = move(piece, row_home(True))
    a0, b0 = acts_one[None], acts_two[None]
    a01 = jnp.concatenate([a0, move(a0, x_step(0))], 0)
    b01 = jnp.concatenate([b0, move(b0, y_step(0))], 0)
    piece, other, ends, a01, b01 = after((piece, other, ends, a01, b01))

    inner = move(piece, row_home(False))
    first = jnp.concatenate([a01, move(a01, x_step(1))], 0)
    second = jnp.concatenate([b01, move(b01, y_step(1))], 0)
    lead, away = leading_sums(meta, piece, other)
    lead = lead + move(away, lambda x, y, z, c: (x, y, z, 1 - c) if root(x, y, z) else None)
    r0 = jnp.where(at_home(z, low), piece, ends + inner)
    r0, first, second, lead = after((r0, first, second, lead))

    r01 = jnp.concatenate([r0, move(r0, z_step(0))], 0)
    first1 = move(first, y_step(0))
    lead = lead + move(lead, lambda x, y, z, c: (x ^ 1, y, z, c) if root(x, y, z) else None)
    lead = jnp.where(row == 0, lead, 0.0)
    lead = lead + move(lead, lambda x, y, z, c: (x + 2, y, z, c) if root(x, y, z) else None)
    r01, first, first1, second, lead = after((r01, first, first1, second, lead))

    r2 = move(r01, z_step(1))
    second1 = move(second, x_step(0))
    lead = lead + move(lead, lambda x, y, z, c: (x, 1, z, c) if y == 0 and z < 2 else None)
    lead = lead + move(lead, lambda x, y, z, c: (x, 3 - y, z, c) if y < 2 and z < 2 else None)
    r01, r2, first, first1, second, second1, lead = after(
        (r01, r2, first, first1, second, second1, lead)
    )

    r3 = move(r2, z_step(2))
    first2 = move(first, y_step(1))
    second2 = move(second, x_step(1))
    theirs = move(lead, lambda x, y, z, c: (x, y, z, 1 - c) if z < 2 else None)
    lead = jnp.where(core == 0, jnp.stack([lead, theirs]), jnp.stack([theirs, lead]))
    state = factor_part(functools.partial(factor_first, scale), 3, (lead.reshape(768, 256),))
    r01, r2, r3, first, first1, first2, second, second1, second2, state = after(
        (r01, r2, r3, first, first1, first2, second, second1, second2, state)
    )

    r4 = move(r3, z_step(3))
    first3 = move(first1, y_step(1))
    second3 = move(second1, x_step(1))
    upper, inverse = factor_part(factor_second, 2, state)
    pieces, upper, inverse = after(
        (
            (
                (r01, r2, r3, r4),
                (first, first1, first2, first3),
                (second, second1, second2, second3),
            ),
            upper,
            inverse,
        )
    )

    theirs, block, away = gram_part(scale, meta, *pieces)
    away = move(away, lambda x, y, z, c: (x, y, z, 1 - c) if z < 2 else None)
    away, theirs = after((away, theirs))
    theirs = move(theirs, core_swap)
    block = (block + away) * scale
    row_ids = row_start + jnp.arange(512, dtype=jnp.int32)[:, None]
    col_ids = z * 256 + jnp.arange(256, dtype=jnp.int32)[None, :]
    block = jnp.where(row_ids == col_ids, block, reg_alpha * block)

    edge = z == 0
    solved = lax.dot_general(
        jnp.where(edge, inverse[:, :256], inverse[:, 256:]), block, (((1,), (1,)), ((), ())),
        precision=HIGHEST, preferred_element_type=jnp.float32,
    )
    head = jnp.where(edge, upper, 0.0)
    solved = jnp.where((row == 0) & (cal == 0), head, solved).reshape(4, 128, 512)
    parts = [jnp.where(edge, solved[0], 0.0)]
    for i in range(3):
        def target(x, y, z, c, i=i):
            if z == 0:
                return x, y, 2 * i + 2, c
            return (x, y, 2 * i + 4, c) if z == 1 and i < 2 else None

        value = jnp.where(edge, solved[i + 1], solved[i + 2]) if i < 2 else solved[3]
        parts.append(move(value, target))
    (gram_reg,) = gram_part(scale, meta, *pieces, other=theirs)
    gram_reg, parts = after((gram_reg, parts))
    share = functools.reduce(jnp.add, parts)
    odd = move(share[64:], lambda x, y, z, c: (x, y, z + 1, c) if z % 2 == 0 else None)
    share = jnp.where(z % 2 == 0, share[:64], odd)
    return gram_reg.reshape(1, 512, 8, 1, 256), share.T.reshape(1, 512, 64)


def solution(mesh):
    return jax.shard_map(
        per_device,
        mesh=mesh,
        in_specs=(P("cal", ("row", "col")), P("cal", ("row", "col"))),
        out_specs=(P("row", "cal", None, "col", None), P("row", "cal", "col")),
        check_vma=False,
    )
```

```python
import functools

import jax
import jax.numpy as jnp
import numpy as np
from jax import lax
from jax.experimental import pallas as pl
from jax.experimental.pallas import tpu as pltpu
from jax.sharding import PartitionSpec as P

PANEL = 512
reg_alpha = 0.9
AXES = ("cal", "row", "col")
NX, NY, NZ = 4, 4, 8
HIGHEST = lax.Precision.HIGHEST


def flat(x, y, z, core):
    return (((x % 2) * 2 + core) * 8 + (x // 2) * 4 + y) * 8 + z


def devices():
    for x in range(NX):
        for y in range(NY):
            for z in range(NZ):
                for core in range(2):
                    yield x, y, z, core


def move(value, target):
    pairs = []
    for device in devices():
        to = target(*device)
        if to is not None:
            pairs.append((flat(*device), flat(*to)))
    return lax.ppermute(value, AXES, sorted(pairs))


def near(i, size, phase):
    return i ^ 1 if phase == 0 else (i + 1 if i % 2 else i - 1) % size


def x_step(s):
    return lambda x, y, z, c: (near(x, NX, (s + c) % 2), y, z, c)


def y_step(s):
    return lambda x, y, z, c: (x, near(y, NY, (s + c) % 2), z, c)


def z_step(s):
    return lambda x, y, z, c: (x, y, near(z, NZ, (s + c) % 2), c)


def core_swap(x, y, z, c):
    return x, y, z, 1 - c


def row_home(x, y, z, c):
    return (x, y, z, c) if z // 4 == x % 2 else (x ^ 1, y, 7 - z, c)


def tables():
    table = np.zeros((256, 32), np.int32)
    for x, y, z, c in devices():
        def ring4(i):
            p1 = lambda v: near(v, 4, c % 2)
            p2 = lambda v: near(v, 4, (1 + c) % 2)
            return [i, p1(i), p2(i), p1(p2(i))]

        step = lambda v, s: near(v, NZ, (s + c) % 2)
        first = lambda v: [v, step(v, 0)]
        third = lambda v: first(step(step(v, 2), 1))
        slots = first(z) + first(step(z, 1)) + third(z) + third(step(z, 3))
        assert sorted(slots) == list(range(8))
        low = x % 2
        blocks = [(p if p // 4 == low else 7 - p) - 4 * low for p in slots]
        halves = [low if p // 4 == low else 1 - low for p in slots]
        table[flat(x, y, z, c)] = ring4(x) + ring4(y) + blocks + halves + [c, low] + [0] * 6
    return table


TABLE = tables()


def column(meta, j, pair):
    x = jnp.where(meta[24] == 0, meta[2 * pair], meta[pair])
    return (x // 2) * 4 + meta[4 + j]


def column_copies(meta, first_refs, second_refs, cols, sem, j):
    half = first_refs[0].shape[1]
    copies = []
    for i in range(4):
        pair = jnp.where(meta[24] == 0, i // 2, i % 2)
        side = meta[i] % 2
        for which, ref in ((0, first_refs[j].at[i]), (1, second_refs[i].at[j])):
            dst = cols.at[
                2 * j + pair,
                pl.ds(pl.multiple_of(side * 2 * half + which * half, half), half),
            ]
            copies.append((True, pltpu.make_async_copy(ref, dst, sem.at[j, i, which])))
    return copies


def start_all(copies):
    for want, copy in copies:
        pl.when(want)(copy.start)


def wait_all(copies):
    for want, copy in copies:
        pl.when(want)(copy.wait)


def row_copies_of(meta, row_refs, rows, sem):
    tokens = row_refs[0].shape[2]
    wanted, refs = rows
    copies = []
    for slot in range(8):
        dst = refs.at[
            pl.ds(pl.multiple_of((meta[8 + slot] % 2) * 256, 256), 256),
            pl.ds(pl.multiple_of(meta[16 + slot] * tokens, tokens), tokens),
        ]
        copy = pltpu.make_async_copy(row_refs[slot // 2].at[slot % 2], dst, sem.at[slot])
        copies.append((meta[8 + slot] // 2 == wanted, copy))
    return copies


def gram_kernel(own, scale, *refs):
    meta, row_refs, first_refs, second_refs, refs = refs[0], refs[1:5], refs[5:9], refs[9:13], refs[13:]
    if own:
        other_ref, out_ref, rows, cols, acc, row_sem, col_sem, sem = refs
    else:
        out_ref, lead_ref, away_ref, rows, cols, acc, row_sem, col_sem, sem, lead_rows, lead_sem = refs
    wanted = meta[24] if own else 1 - meta[24]
    row_copies = row_copies_of(meta, row_refs, (wanted, rows), row_sem)
    lead_copies = [] if own else row_copies_of(meta, row_refs, (1 - wanted, lead_rows), lead_sem)
    groups = []
    for j in range(4):
        group = column_copies(meta, first_refs, second_refs, cols, col_sem, j)
        if own:
            for pair in range(2):
                k = 2 * j + pair
                src = other_ref.at[column(meta, j, pair)]
                group.append((True, pltpu.make_async_copy(src, acc.at[k], sem.at[k])))
        groups.append(group)
    start_all(row_copies)
    start_all(groups[0])
    start_all(groups[1])
    start_all(lead_copies)
    row_ids = meta[25] + lax.broadcasted_iota(jnp.int32, (512, 128), 0)
    lane = meta[26] + lax.broadcasted_iota(jnp.int32, (512, 128), 1)
    wait_all(row_copies)
    out_copies = []
    for j in range(4):
        wait_all(groups[j])
        if j + 2 < 4:
            start_all(groups[j + 2])
        for pair in range(2):
            k, a = 2 * j + pair, column(meta, j, pair)
            total = jnp.dot(rows[...], cols[k], preferred_element_type=jnp.float32)
            if own:
                for h in range(2):
                    at = slice(h * 128, (h + 1) * 128)
                    part = (total[:, at] + acc[k, :, at]) * scale
                    same = row_ids == lane + (a * 2048 + h * 128)
                    out_ref[pl.ds(2 * a + h, 512, stride=16), :] = jnp.where(
                        same, part, reg_alpha * part
                    )
            else:
                acc[k] = total
                copy = pltpu.make_async_copy(acc.at[k], out_ref.at[a], sem.at[k])
                copy.start()
                out_copies.append(copy)
    if not own:
        at = sum((2 * j + p) * (column(meta, j, p) == 0) for j in range(4) for p in range(2))
        away_ref[...] = acc[at]
        wait_all(lead_copies)
        lead_ref[...] = jnp.dot(lead_rows[...], cols[at], preferred_element_type=jnp.float32)
    for copy in out_copies:
        copy.wait()


def gram_part(scale, meta, row_bufs, first_bufs, second_bufs, other=None):
    own = other is not None
    tokens = row_bufs[0].shape[2]
    any_spec = pl.BlockSpec(memory_space=pl.ANY)
    vmem = pl.BlockSpec(memory_space=pltpu.VMEM)
    shapes = ((512 * 16, 128),) if own else ((8, 512, 256), (512, 256), (512, 256))
    rows = pltpu.VMEM((512, 2 * tokens), jnp.bfloat16)
    return pl.pallas_call(
        functools.partial(gram_kernel, own, scale),
        out_shape=tuple(jax.ShapeDtypeStruct(shape, jnp.float32) for shape in shapes),
        in_specs=[pl.BlockSpec(memory_space=pltpu.SMEM)] + [any_spec] * (12 + own),
        out_specs=(vmem,) if own else (any_spec, vmem, vmem),
        scratch_shapes=[
            rows,
            pltpu.VMEM((8, 2 * tokens, 256), jnp.bfloat16),
            pltpu.VMEM((8, 512, 256), jnp.float32),
            pltpu.SemaphoreType.DMA((8,)),
            pltpu.SemaphoreType.DMA((4, 4, 2)),
            pltpu.SemaphoreType.DMA((8,)),
        ]
        + ([] if own else [rows, pltpu.SemaphoreType.DMA((8,))]),
        compiler_params=pltpu.CompilerParams(vmem_limit_bytes=62 * 2**20),
        cost_estimate=pl.CostEstimate(
            flops=2 * 512 * 2048 * 2 * tokens, bytes_accessed=24 * 2**20, transcendentals=0
        ),
    )(meta, *row_bufs, *first_bufs, *second_bufs, *([other] if own else []))


def dot_t(a, b):
    return lax.dot_general(
        a, b, (((0,), (0,)), ((), ())), precision=HIGHEST, preferred_element_type=jnp.float32
    )


def dot_n(a, b):
    return lax.dot_general(
        a, b, (((1,), (0,)), ((), ())), precision=HIGHEST, preferred_element_type=jnp.float32
    )


def sums_kernel(meta, own, other, mine_ref, away_ref, sums):
    def dot(p, q):
        return lax.dot_general(
            p[0], q[0], (((1,), (1,)), ((), ())), preferred_element_type=jnp.float32
        )

    @pl.when(meta[26] == 0)
    def _():
        sums[:256] = dot(own, own)
        sums[256:512] = dot(own, other)
        sums[512:] = dot(other, other)

    @pl.when(meta[26] != 0)
    def _():
        sums[:256] = dot(other, other)
        sums[256:512] = dot(other, own)
        sums[512:] = dot(own, own)

    mine_ref[...] = sums[pl.ds(pl.multiple_of(meta[24] * 384, 128), 384), :]
    away_ref[...] = sums[pl.ds(pl.multiple_of((1 - meta[24]) * 384, 128), 384), :]


def leading_sums(meta, own, other):
    full = pl.BlockSpec(memory_space=pltpu.VMEM)
    return pl.pallas_call(
        sums_kernel,
        out_shape=(jax.ShapeDtypeStruct((384, 256), jnp.float32),) * 2,
        in_specs=[pl.BlockSpec(memory_space=pltpu.SMEM), full, full],
        out_specs=(full, full),
        scratch_shapes=[pltpu.VMEM((768, 256), jnp.float32)],
        compiler_params=pltpu.CompilerParams(vmem_limit_bytes=32 * 2**20),
        cost_estimate=pl.CostEstimate(flops=2**30, bytes_accessed=2**20, transcendentals=0),
    )(meta, own, other)


def factor_block(k, work, u_ref, inv_ref, block):
    n, nb, np_ = 512, 128, 16
    lo, hi = k * nb, (k + 1) * nb
    sub = lax.broadcasted_iota(jnp.int32, (np_, nb), 0)
    sub2 = lax.broadcasted_iota(jnp.int32, (np_, 2 * nb), 0)
    lane2 = lax.broadcasted_iota(jnp.int32, (np_, 2 * nb), 1)
    block[:, :nb] = work[lo:hi, lo:hi]
    block[:, nb:] = (
        lax.broadcasted_iota(jnp.int32, (nb, nb), 0) == lax.broadcasted_iota(jnp.int32, (nb, nb), 1)
    ).astype(jnp.float32)
    for base in range(0, nb, np_):
        end = base + np_
        v = block[base:end, :]
        pc = [jnp.broadcast_to(v[:, base + i:base + i + 1], (np_, nb)) for i in range(np_)]
        for i in range(np_):
            s = lax.rsqrt(pc[i][i:i + 1, :])
            below = jnp.where(sub > i, pc[i] * s, 0.0)
            for j in range(i + 1, np_):
                pc[j] = pc[j] - below * (pc[j][i:i + 1, :] * s)
            u = v[i:i + 1, :] * jnp.concatenate([s, s], 1)
            v = jnp.where(sub2 == i, u, v - jnp.concatenate([below, below], 1) * u)
        v = jnp.where(lane2 >= base + sub2, v, 0.0)
        block[base:end, :] = v
        if end < nb:
            block[end:, :] -= dot_t(v[:, :nb], v)[end:]
    x = block[:, nb:]
    u_ref[lo:hi, lo:hi] = block[:, :nb]
    inv_ref[lo:hi, lo:hi] = x
    if k:
        inner = dot_t(u_ref[0:lo, lo:hi], inv_ref[0:lo, 0:lo])
        inv_ref[lo:hi, 0:lo] = -dot_n(x, inner)
    if hi < n:
        right = dot_n(x, work[lo:hi, hi:n])
        u_ref[lo:hi, hi:n] = right
        work[hi:n, hi:n] -= dot_t(right, right)


def factor_first(scale, sums, work, u_ref, inv_ref, block):
    rid = lax.broadcasted_iota(jnp.int32, (256, 256), 0)
    cid = lax.broadcasted_iota(jnp.int32, (256, 256), 1)

    def regular(part):
        return jnp.where(rid == cid, part * scale, reg_alpha * (part * scale))

    work[...] = jnp.zeros((512, 512), jnp.float32)
    work[:256, :256] = regular(sums[:256])
    work[:256, 256:] = reg_alpha * (sums[256:512] * scale)
    work[256:, 256:] = regular(sums[512:])
    u_ref[...] = jnp.zeros((512, 512), jnp.float32)
    inv_ref[...] = jnp.zeros((512, 512), jnp.float32)
    for k in (0, 1):
        factor_block(k, work, u_ref, inv_ref, block)


def factor_second(work_ref, u_in, inv_in, u_ref, inv_ref, work, block):
    work[...] = work_ref[...]
    u_ref[...] = u_in[...]
    inv_ref[...] = inv_in[...]
    for k in (2, 3):
        factor_block(k, work, u_ref, inv_ref, block)


def factor_part(kernel, n_out, args):
    full = pl.BlockSpec(memory_space=pltpu.VMEM)
    shape = jax.ShapeDtypeStruct((512, 512), jnp.float32)
    small = pltpu.VMEM((128, 256), jnp.float32)
    return pl.pallas_call(
        kernel,
        out_shape=(shape,) * n_out,
        in_specs=[full] * len(args),
        out_specs=(full,) * n_out,
        scratch_shapes=[pltpu.VMEM((512, 512), jnp.float32)] * (3 - n_out) + [small],
        compiler_params=pltpu.CompilerParams(vmem_limit_bytes=32 * 2**20),
        cost_estimate=pl.CostEstimate(flops=2**20, bytes_accessed=2**20, transcendentals=512),
    )(*args)


def per_device(acts_one, acts_two):
    cal, row, z = (lax.axis_index(a) for a in AXES)
    low, core = cal // 2, cal % 2
    total_tokens = 8 * acts_one.shape[0]
    scale = 1.0 / total_tokens
    device = (cal * 8 + row) * 8 + z
    meta = lax.dynamic_index_in_dim(jnp.asarray(TABLE), device, 0, keepdims=False)
    after = lax.optimization_barrier
    root = lambda x, y, z: (x // 2, y) == (0, 0) and z < 2

    row_start = row * 2048 + cal * 512
    meta = meta.at[25].set(row_start).at[26].set(z * 256)

    piece = jnp.concatenate([acts_one.T, acts_two.T], 1)[None]
    other = move(piece, lambda x, y, z, c: (x, y, 1 - z, c) if root(x, y, z) else None)
    r0 = move(piece, row_home)
    a0, b0 = acts_one[None], acts_two[None]
    a01 = jnp.concatenate([a0, move(a0, x_step(0))], 0)
    b01 = jnp.concatenate([b0, move(b0, y_step(0))], 0)
    lead, away = leading_sums(meta, piece, other)
    lead = lead + move(away, lambda x, y, z, c: (x, y, z, 1 - c) if root(x, y, z) else None)
    r0, a01, b01, lead = after((r0, a01, b01, lead))

    r01 = jnp.concatenate([r0, move(r0, z_step(0))], 0)
    r2 = move(r01, z_step(1))
    first = jnp.concatenate([a01, move(a01, x_step(1))], 0)
    b23 = move(b01, y_step(1))
    first, b23 = after((first, b23))
    first1 = move(first, y_step(0))
    lead = lead + move(lead, lambda x, y, z, c: (x ^ 1, y, z, c) if root(x, y, z) else None)
    lead = jnp.where(row == 0, lead, 0.0)
    lead = lead + move(lead, lambda x, y, z, c: (x + 2, y, z, c) if root(x, y, z) else None)
    r01, r2, first, first1, b01, b23, lead = after((r01, r2, first, first1, b01, b23, lead))

    r3 = move(r2, z_step(2))
    second = jnp.concatenate([b01, b23], 0)
    second1 = move(second, x_step(0))
    lead = lead + move(lead, lambda x, y, z, c: (x, 1, z, c) if y == 0 and z < 2 else None)
    lead = lead + move(lead, lambda x, y, z, c: (x, 3 - y, z, c) if y < 2 and z < 2 else None)
    r01, r2, r3, first, first1, second, second1, lead = after(
        (r01, r2, r3, first, first1, second, second1, lead)
    )

    r4 = move(r3, z_step(3))
    first2 = move(first, y_step(1))
    second2 = move(second, x_step(1))
    theirs = move(lead, lambda x, y, z, c: (x, y, z, 1 - c) if z < 2 else None)
    lead = jnp.where(core == 0, jnp.stack([lead, theirs]), jnp.stack([theirs, lead]))
    state = factor_part(functools.partial(factor_first, scale), 3, (lead.reshape(768, 256),))
    r01, r2, r3, r4, first, first1, first2, second, second1, second2, state = after(
        (r01, r2, r3, r4, first, first1, first2, second, second1, second2, state)
    )

    first3 = move(first1, y_step(1))
    second3 = move(second1, x_step(1))
    upper, inverse = factor_part(factor_second, 2, state)
    pieces, upper, inverse = after(
        (
            (
                (r01, r2, r3, r4),
                (first, first1, first2, first3),
                (second, second1, second2, second3),
            ),
            upper,
            inverse,
        )
    )

    theirs, block, away = gram_part(scale, meta, *pieces)
    away = move(away, lambda x, y, z, c: (x, y, z, 1 - c) if z < 2 else None)
    away, theirs = after((away, theirs))
    theirs = move(theirs, core_swap)
    block = (block + away) * scale
    row_ids = row_start + jnp.arange(512, dtype=jnp.int32)[:, None]
    col_ids = z * 256 + jnp.arange(256, dtype=jnp.int32)[None, :]
    block = jnp.where(row_ids == col_ids, block, reg_alpha * block)

    edge = z == 0
    solved = lax.dot_general(
        jnp.where(edge, inverse[:, :256], inverse[:, 256:]), block, (((1,), (1,)), ((), ())),
        precision=HIGHEST, preferred_element_type=jnp.float32,
    )
    head = jnp.where(edge, upper, 0.0)
    solved = jnp.where((row == 0) & (cal == 0), head, solved).reshape(4, 128, 512)
    parts = [jnp.where(edge, solved[0], 0.0)]
    for i in range(3):
        def target(x, y, z, c, i=i):
            if z == 0:
                return x, y, 2 * i + 2, c
            return (x, y, 2 * i + 4, c) if z == 1 and i < 2 else None

        value = jnp.where(edge, solved[i + 1], solved[i + 2]) if i < 2 else solved[3]
        parts.append(move(value, target))
    (gram_reg,) = gram_part(scale, meta, *pieces, other=theirs)
    gram_reg, parts = after((gram_reg, parts))
    share = functools.reduce(jnp.add, parts)
    odd = move(share[64:], lambda x, y, z, c: (x, y, z + 1, c) if z % 2 == 0 else None)
    share = jnp.where(z % 2 == 0, share[:64], odd)
    return gram_reg.reshape(1, 512, 8, 1, 256), share.T.reshape(1, 512, 64)


def solution(mesh):
    return jax.shard_map(
        per_device,
        mesh=mesh,
        in_specs=(P("cal", ("row", "col")), P("cal", ("row", "col"))),
        out_specs=(P("row", "cal", None, "col", None), P("row", "cal", "col")),
        check_vma=False,
    )
```

```python
import functools

import jax
import jax.numpy as jnp
import numpy as np
from jax import lax
from jax.experimental import pallas as pl
from jax.experimental.pallas import tpu as pltpu
from jax.sharding import PartitionSpec as P

PANEL = 512
reg_alpha = 0.9
AXES = ("cal", "row", "col")
NX, NY, NZ = 4, 4, 8
HIGHEST = lax.Precision.HIGHEST


def flat(x, y, z, core):
    return (((x % 2) * 2 + core) * 8 + (x // 2) * 4 + y) * 8 + z


def devices():
    for x in range(NX):
        for y in range(NY):
            for z in range(NZ):
                for core in range(2):
                    yield x, y, z, core


def move(value, target):
    pairs = []
    for device in devices():
        to = target(*device)
        if to is not None:
            pairs.append((flat(*device), flat(*to)))
    return lax.ppermute(value, AXES, sorted(pairs))


def near(i, size, phase):
    return i ^ 1 if phase == 0 else (i + 1 if i % 2 else i - 1) % size


def x_step(s):
    return lambda x, y, z, c: (near(x, NX, (s + c) % 2), y, z, c)


def y_step(s):
    return lambda x, y, z, c: (x, near(y, NY, (s + c) % 2), z, c)


def z_step(s):
    return lambda x, y, z, c: (x, y, near(z, NZ, (s + c) % 2), c)


def core_swap(x, y, z, c):
    return x, y, z, 1 - c


def row_home(x, y, z, c):
    return (x, y, z, c) if z // 4 == x % 2 else (x ^ 1, y, 7 - z, c)


def tables():
    table = np.zeros((256, 32), np.int32)
    for x, y, z, c in devices():
        def ring4(i):
            p1 = lambda v: near(v, 4, c % 2)
            p2 = lambda v: near(v, 4, (1 + c) % 2)
            return [i, p1(i), p2(i), p1(p2(i))]

        step = lambda v, s: near(v, NZ, (s + c) % 2)
        first = lambda v: [v, step(v, 0)]
        third = lambda v: first(step(step(v, 2), 1))
        slots = first(z) + first(step(z, 1)) + third(z) + third(step(z, 3))
        assert sorted(slots) == list(range(8))
        low = x % 2
        blocks = [(p if p // 4 == low else 7 - p) - 4 * low for p in slots]
        halves = [low if p // 4 == low else 1 - low for p in slots]
        table[flat(x, y, z, c)] = ring4(x) + ring4(y) + blocks + halves + [c, low] + [0] * 6
    return table


TABLE = tables()


def column(meta, j, pair):
    x = jnp.where(meta[24] == 0, meta[2 * pair], meta[pair])
    return (x // 2) * 4 + meta[4 + j]


def column_copies(meta, first_refs, second_refs, cols, sem, j, late=False):
    half = first_refs[0].shape[1]
    copies = []
    for i in range(4):
        pair = jnp.where(meta[24] == 0, i // 2, i % 2)
        side = meta[i] % 2
        for which, ref in ((0, first_refs[j].at[i]), (1, second_refs[i].at[j])):
            dst = cols.at[
                2 * j + pair,
                pl.ds(pl.multiple_of(side * 2 * half + which * half, half), half),
            ]
            want = pair == 1 if late and j < 3 else True
            copies.append((want, pltpu.make_async_copy(ref, dst, sem.at[j, i, which])))
    return copies


def start_all(copies):
    for want, copy in copies:
        pl.when(want)(copy.start)


def wait_all(copies):
    for want, copy in copies:
        pl.when(want)(copy.wait)


def row_copies_of(meta, row_refs, rows, sem):
    tokens = row_refs[0].shape[2]
    wanted, refs = rows
    copies = []
    for slot in range(8):
        dst = refs.at[
            pl.ds(pl.multiple_of((meta[8 + slot] % 2) * 256, 256), 256),
            pl.ds(pl.multiple_of(meta[16 + slot] * tokens, tokens), tokens),
        ]
        copy = pltpu.make_async_copy(row_refs[slot // 2].at[slot % 2], dst, sem.at[slot])
        copies.append((meta[8 + slot] // 2 == wanted, copy))
    return copies


def early_kernel(*refs):
    meta, row_refs, first_refs, second_refs = refs[0], refs[1:5], refs[5:8], refs[8:11]
    own_ref, away_ref, rows, cols, acc, row_sem, col_sem, sem = refs[11:]
    tokens = row_refs[0].shape[2]
    half = tokens // 2
    core = meta[24]
    row_copies = []
    for h, wanted in ((0, core), (1, 1 - core)):
        place = rows.at[pl.ds(h * 512, 512)]
        row_copies += row_copies_of(meta, row_refs, (wanted, place), row_sem)
    start_all(row_copies)
    groups = []
    for j in range(3):
        group = []
        for i in range(3):
            want = (True, core == 0, core == 1)[i]
            side = meta[i] % 2
            for which, ref in ((0, first_refs[j].at[i]), (1, second_refs[i].at[j])):
                at = pl.ds(pl.multiple_of(side * tokens + which * half, half), half)
                copy = pltpu.make_async_copy(ref, cols.at[j, at], col_sem.at[j, i, which])
                group.append((want, copy))
        start_all(group)
        groups.append(group)
    wait_all(row_copies)
    copies = []
    for j in range(3):
        wait_all(groups[j])

        def part(h, _, j=j):
            at = pl.ds(pl.multiple_of(h * 512, 512), 512)
            acc[j, at, :] = jnp.dot(rows[at, :], cols[j], preferred_element_type=jnp.float32)
            return 0

        lax.fori_loop(0, 2, part, 0)
        for h, ref in ((0, own_ref), (1, away_ref)):
            copy = pltpu.make_async_copy(acc.at[j, pl.ds(h * 512, 512)], ref.at[j], sem.at[h, j])
            copy.start()
            copies.append(copy)
    for copy in copies:
        copy.wait()


def early_part(meta, row_bufs, first_bufs, second_bufs):
    tokens = row_bufs[0].shape[2]
    any_spec = pl.BlockSpec(memory_space=pl.ANY)
    return pl.pallas_call(
        early_kernel,
        out_shape=(jax.ShapeDtypeStruct((3, 512, 256), jnp.float32),) * 2,
        in_specs=[pl.BlockSpec(memory_space=pltpu.SMEM)] + [any_spec] * 10,
        out_specs=(any_spec, any_spec),
        scratch_shapes=[
            pltpu.VMEM((1024, 2 * tokens), jnp.bfloat16),
            pltpu.VMEM((3, 2 * tokens, 256), jnp.bfloat16),
            pltpu.VMEM((3, 1024, 256), jnp.float32),
            pltpu.SemaphoreType.DMA((8,)),
            pltpu.SemaphoreType.DMA((3, 3, 2)),
            pltpu.SemaphoreType.DMA((2, 3)),
        ],
        compiler_params=pltpu.CompilerParams(vmem_limit_bytes=40 * 2**20),
        cost_estimate=pl.CostEstimate(flops=2**20, bytes_accessed=2**20, transcendentals=0),
    )(meta, *row_bufs, *first_bufs, *second_bufs)


def gram_kernel(own, scale, *refs):
    meta, row_refs, first_refs, second_refs, refs = refs[0], refs[1:5], refs[5:9], refs[9:13], refs[13:]
    early_ref, refs = refs[0], refs[1:]
    if own:
        other_ref, out_ref, rows, cols, acc, row_sem, col_sem, sem, early, early_sem = refs
    else:
        out_ref, lead_ref, away_ref, rows, cols, acc, row_sem, col_sem, sem, lead_rows, lead_sem = refs
    wanted = meta[24] if own else 1 - meta[24]
    row_copies = row_copies_of(meta, row_refs, (wanted, rows), row_sem)
    lead_copies = [] if own else row_copies_of(meta, row_refs, (1 - wanted, lead_rows), lead_sem)
    groups = []
    for j in range(4):
        group = column_copies(meta, first_refs, second_refs, cols, col_sem, j, late=own)
        if j < 3:
            dst, at = (early.at[j], early_sem.at[j]) if own else (acc.at[2 * j], sem.at[2 * j])
            group.append((True, pltpu.make_async_copy(early_ref.at[j], dst, at)))
        if own:
            for pair in range(2):
                k = 2 * j + pair
                src = other_ref.at[column(meta, j, pair)]
                group.append((True, pltpu.make_async_copy(src, acc.at[k], sem.at[k])))
        groups.append(group)
    start_all(row_copies)
    start_all(groups[0])
    start_all(groups[1])
    start_all(lead_copies)
    row_ids = meta[25] + lax.broadcasted_iota(jnp.int32, (512, 128), 0)
    lane = meta[26] + lax.broadcasted_iota(jnp.int32, (512, 128), 1)
    wait_all(row_copies)
    out_copies = []
    for j in range(4):
        wait_all(groups[j])
        if j + 2 < 4:
            start_all(groups[j + 2])
        for pair in range(2):
            k, a = 2 * j + pair, column(meta, j, pair)
            done = pair == 0 and j < 3
            if done:
                total = early[j] if own else None
            else:
                total = jnp.dot(rows[...], cols[k], preferred_element_type=jnp.float32)
            if own:
                for h in range(2):
                    at = slice(h * 128, (h + 1) * 128)
                    part = (total[:, at] + acc[k, :, at]) * scale
                    same = row_ids == lane + (a * 2048 + h * 128)
                    out_ref[pl.ds(2 * a + h, 512, stride=16), :] = jnp.where(
                        same, part, reg_alpha * part
                    )
            else:
                if not done:
                    acc[k] = total
                copy = pltpu.make_async_copy(acc.at[k], out_ref.at[a], sem.at[k])
                copy.start()
                out_copies.append(copy)
    if not own:
        at = sum((2 * j + p) * (column(meta, j, p) == 0) for j in range(4) for p in range(2))
        away_ref[...] = acc[at]
        wait_all(lead_copies)
        lead_ref[...] = jnp.dot(lead_rows[...], cols[at], preferred_element_type=jnp.float32)
    for copy in out_copies:
        copy.wait()


def gram_part(scale, meta, row_bufs, first_bufs, second_bufs, early, other=None):
    own = other is not None
    tokens = row_bufs[0].shape[2]
    any_spec = pl.BlockSpec(memory_space=pl.ANY)
    vmem = pl.BlockSpec(memory_space=pltpu.VMEM)
    shapes = ((512 * 16, 128),) if own else ((8, 512, 256), (512, 256), (512, 256))
    rows = pltpu.VMEM((512, 2 * tokens), jnp.bfloat16)
    return pl.pallas_call(
        functools.partial(gram_kernel, own, scale),
        out_shape=tuple(jax.ShapeDtypeStruct(shape, jnp.float32) for shape in shapes),
        in_specs=[pl.BlockSpec(memory_space=pltpu.SMEM)] + [any_spec] * (13 + own),
        out_specs=(vmem,) if own else (any_spec, vmem, vmem),
        scratch_shapes=[
            rows,
            pltpu.VMEM((8, 2 * tokens, 256), jnp.bfloat16),
            pltpu.VMEM((8, 512, 256), jnp.float32),
            pltpu.SemaphoreType.DMA((8,)),
            pltpu.SemaphoreType.DMA((4, 4, 2)),
            pltpu.SemaphoreType.DMA((8,)),
        ]
        + [pltpu.VMEM((3, 512, 256), jnp.float32) if own else rows, pltpu.SemaphoreType.DMA((8,))],
        compiler_params=pltpu.CompilerParams(vmem_limit_bytes=62 * 2**20),
        cost_estimate=pl.CostEstimate(
            flops=2 * 512 * 2048 * 2 * tokens, bytes_accessed=24 * 2**20, transcendentals=0
        ),
    )(meta, *row_bufs, *first_bufs, *second_bufs, early, *([other] if own else []))


def dot_t(a, b):
    return lax.dot_general(
        a, b, (((0,), (0,)), ((), ())), precision=HIGHEST, preferred_element_type=jnp.float32
    )


def dot_n(a, b):
    return lax.dot_general(
        a, b, (((1,), (0,)), ((), ())), precision=HIGHEST, preferred_element_type=jnp.float32
    )


def sums_kernel(meta, own, other, mine_ref, away_ref, sums):
    def dot(p, q):
        return lax.dot_general(
            p[0], q[0], (((1,), (1,)), ((), ())), preferred_element_type=jnp.float32
        )

    @pl.when(meta[26] == 0)
    def _():
        sums[:256] = dot(own, own)
        sums[256:512] = dot(own, other)
        sums[512:] = dot(other, other)

    @pl.when(meta[26] != 0)
    def _():
        sums[:256] = dot(other, other)
        sums[256:512] = dot(other, own)
        sums[512:] = dot(own, own)

    mine_ref[...] = sums[pl.ds(pl.multiple_of(meta[24] * 384, 128), 384), :]
    away_ref[...] = sums[pl.ds(pl.multiple_of((1 - meta[24]) * 384, 128), 384), :]


def leading_sums(meta, own, other):
    full = pl.BlockSpec(memory_space=pltpu.VMEM)
    return pl.pallas_call(
        sums_kernel,
        out_shape=(jax.ShapeDtypeStruct((384, 256), jnp.float32),) * 2,
        in_specs=[pl.BlockSpec(memory_space=pltpu.SMEM), full, full],
        out_specs=(full, full),
        scratch_shapes=[pltpu.VMEM((768, 256), jnp.float32)],
        compiler_params=pltpu.CompilerParams(vmem_limit_bytes=32 * 2**20),
        cost_estimate=pl.CostEstimate(flops=2**30, bytes_accessed=2**20, transcendentals=0),
    )(meta, own, other)


def factor_block(k, work, u_ref, inv_ref, block):
    n, nb, np_ = 512, 128, 16
    lo, hi = k * nb, (k + 1) * nb
    sub = lax.broadcasted_iota(jnp.int32, (np_, nb), 0)
    sub2 = lax.broadcasted_iota(jnp.int32, (np_, 2 * nb), 0)
    lane2 = lax.broadcasted_iota(jnp.int32, (np_, 2 * nb), 1)
    block[:, :nb] = work[lo:hi, lo:hi]
    block[:, nb:] = (
        lax.broadcasted_iota(jnp.int32, (nb, nb), 0) == lax.broadcasted_iota(jnp.int32, (nb, nb), 1)
    ).astype(jnp.float32)
    for base in range(0, nb, np_):
        end = base + np_
        v = block[base:end, :]
        pc = [jnp.broadcast_to(v[:, base + i:base + i + 1], (np_, nb)) for i in range(np_)]
        for i in range(np_):
            s = lax.rsqrt(pc[i][i:i + 1, :])
            below = jnp.where(sub > i, pc[i] * s, 0.0)
            for j in range(i + 1, np_):
                pc[j] = pc[j] - below * (pc[j][i:i + 1, :] * s)
            u = v[i:i + 1, :] * jnp.concatenate([s, s], 1)
            v = jnp.where(sub2 == i, u, v - jnp.concatenate([below, below], 1) * u)
        v = jnp.where(lane2 >= base + sub2, v, 0.0)
        block[base:end, :] = v
        if end < nb:
            block[end:, :] -= dot_t(v[:, :nb], v)[end:]
    x = block[:, nb:]
    u_ref[lo:hi, lo:hi] = block[:, :nb]
    inv_ref[lo:hi, lo:hi] = x
    if k:
        inner = dot_t(u_ref[0:lo, lo:hi], inv_ref[0:lo, 0:lo])
        inv_ref[lo:hi, 0:lo] = -dot_n(x, inner)
    if hi < n:
        right = dot_n(x, work[lo:hi, hi:n])
        u_ref[lo:hi, hi:n] = right
        work[hi:n, hi:n] -= dot_t(right, right)


def factor_first(scale, sums, work, u_ref, inv_ref, block):
    rid = lax.broadcasted_iota(jnp.int32, (256, 256), 0)
    cid = lax.broadcasted_iota(jnp.int32, (256, 256), 1)

    def regular(part):
        return jnp.where(rid == cid, part * scale, reg_alpha * (part * scale))

    work[...] = jnp.zeros((512, 512), jnp.float32)
    work[:256, :256] = regular(sums[:256])
    work[:256, 256:] = reg_alpha * (sums[256:512] * scale)
    work[256:, 256:] = regular(sums[512:])
    u_ref[...] = jnp.zeros((512, 512), jnp.float32)
    inv_ref[...] = jnp.zeros((512, 512), jnp.float32)
    for k in (0, 1):
        factor_block(k, work, u_ref, inv_ref, block)


def factor_second(work_ref, u_in, inv_in, u_ref, inv_ref, work, block):
    work[...] = work_ref[...]
    u_ref[...] = u_in[...]
    inv_ref[...] = inv_in[...]
    for k in (2, 3):
        factor_block(k, work, u_ref, inv_ref, block)


def factor_part(kernel, n_out, args):
    full = pl.BlockSpec(memory_space=pltpu.VMEM)
    shape = jax.ShapeDtypeStruct((512, 512), jnp.float32)
    small = pltpu.VMEM((128, 256), jnp.float32)
    return pl.pallas_call(
        kernel,
        out_shape=(shape,) * n_out,
        in_specs=[full] * len(args),
        out_specs=(full,) * n_out,
        scratch_shapes=[pltpu.VMEM((512, 512), jnp.float32)] * (3 - n_out) + [small],
        compiler_params=pltpu.CompilerParams(vmem_limit_bytes=32 * 2**20),
        cost_estimate=pl.CostEstimate(flops=2**20, bytes_accessed=2**20, transcendentals=512),
    )(*args)


def per_device(acts_one, acts_two):
    cal, row, z = (lax.axis_index(a) for a in AXES)
    low, core = cal // 2, cal % 2
    total_tokens = 8 * acts_one.shape[0]
    scale = 1.0 / total_tokens
    device = (cal * 8 + row) * 8 + z
    meta = lax.dynamic_index_in_dim(jnp.asarray(TABLE), device, 0, keepdims=False)
    after = lax.optimization_barrier
    root = lambda x, y, z: (x // 2, y) == (0, 0) and z < 2

    row_start = row * 2048 + cal * 512
    meta = meta.at[25].set(row_start).at[26].set(z * 256)

    piece = jnp.concatenate([acts_one.T, acts_two.T], 1)[None]
    other = move(piece, lambda x, y, z, c: (x, y, 1 - z, c) if root(x, y, z) else None)
    r0 = move(piece, row_home)
    a0, b0 = acts_one[None], acts_two[None]
    a01 = jnp.concatenate([a0, move(a0, x_step(0))], 0)
    b01 = jnp.concatenate([b0, move(b0, y_step(0))], 0)
    a23 = move(a01, x_step(1))
    b23 = move(b01, y_step(1))
    r1 = move(r0, z_step(0))
    lead, away = leading_sums(meta, piece, other)
    lead = lead + move(away, lambda x, y, z, c: (x, y, z, 1 - c) if root(x, y, z) else None)
    r0, r1, a01, a23, b01, b23, lead = after((r0, r1, a01, a23, b01, b23, lead))

    r01 = jnp.concatenate([r0, r1], 0)
    r2 = move(r01, z_step(1))
    first = jnp.concatenate([a01, a23], 0)
    first1 = move(first, y_step(0))
    lead = lead + move(lead, lambda x, y, z, c: (x ^ 1, y, z, c) if root(x, y, z) else None)
    lead = jnp.where(row == 0, lead, 0.0)
    lead = lead + move(lead, lambda x, y, z, c: (x + 2, y, z, c) if root(x, y, z) else None)
    r01, r2, first, first1, b01, b23, lead = after((r01, r2, first, first1, b01, b23, lead))

    r3 = move(r2, z_step(2))
    second = jnp.concatenate([b01, b23], 0)
    second1 = move(second, x_step(0))
    lead = lead + move(lead, lambda x, y, z, c: (x, 1, z, c) if y == 0 and z < 2 else None)
    lead = lead + move(lead, lambda x, y, z, c: (x, 3 - y, z, c) if y < 2 and z < 2 else None)
    theirs = move(lead, lambda x, y, z, c: (x, y, z, 1 - c) if z < 2 else None)
    lead = jnp.where(core == 0, jnp.stack([lead, theirs]), jnp.stack([theirs, lead]))
    r01, r2, r3, first, first1, second, second1, lead = after(
        (r01, r2, r3, first, first1, second, second1, lead)
    )

    r4 = move(r3, z_step(3))
    first2 = move(first, y_step(1))
    second2 = move(second, x_step(1))
    state = factor_part(functools.partial(factor_first, scale), 3, (lead.reshape(768, 256),))
    r01, r2, r3, r4, first, first1, first2, second, second1, second2, state = after(
        (r01, r2, r3, r4, first, first1, first2, second, second1, second2, state)
    )

    first3 = move(first1, y_step(1))
    second3 = move(second1, x_step(1))
    upper, inverse = factor_part(factor_second, 2, state)
    early_own, early_away = early_part(
        meta, (r01, r2, r3, r4), (first, first1, first2), (second, second1, second2)
    )
    pieces, upper, inverse, early_own, early_away = after(
        (
            (
                (r01, r2, r3, r4),
                (first, first1, first2, first3),
                (second, second1, second2, second3),
            ),
            upper,
            inverse,
            early_own,
            early_away,
        )
    )

    theirs, block, away = gram_part(scale, meta, *pieces, early_away)
    away = move(away, lambda x, y, z, c: (x, y, z, 1 - c) if z < 2 else None)
    away, theirs = after((away, theirs))
    theirs = move(theirs, core_swap)
    block = (block + away) * scale
    row_ids = row_start + jnp.arange(512, dtype=jnp.int32)[:, None]
    col_ids = z * 256 + jnp.arange(256, dtype=jnp.int32)[None, :]
    block = jnp.where(row_ids == col_ids, block, reg_alpha * block)

    edge = z == 0
    solved = lax.dot_general(
        jnp.where(edge, inverse[:, :256], inverse[:, 256:]), block, (((1,), (1,)), ((), ())),
        precision=HIGHEST, preferred_element_type=jnp.float32,
    )
    head = jnp.where(edge, upper, 0.0)
    solved = jnp.where((row == 0) & (cal == 0), head, solved).reshape(4, 128, 512)
    parts = [jnp.where(edge, solved[0], 0.0)]
    for i in range(3):
        def target(x, y, z, c, i=i):
            if z == 0:
                return x, y, 2 * i + 2, c
            return (x, y, 2 * i + 4, c) if z == 1 and i < 2 else None

        value = jnp.where(edge, solved[i + 1], solved[i + 2]) if i < 2 else solved[3]
        parts.append(move(value, target))
    (gram_reg,) = gram_part(scale, meta, *pieces, early_own, other=theirs)
    gram_reg, parts = after((gram_reg, parts))
    share = functools.reduce(jnp.add, parts)
    odd = move(share[64:], lambda x, y, z, c: (x, y, z + 1, c) if z % 2 == 0 else None)
    share = jnp.where(z % 2 == 0, share[:64], odd)
    return gram_reg.reshape(1, 512, 8, 1, 256), share.T.reshape(1, 512, 64)


def solution(mesh):
    return jax.shard_map(
        per_device,
        mesh=mesh,
        in_specs=(P("cal", ("row", "col")), P("cal", ("row", "col"))),
        out_specs=(P("row", "cal", None, "col", None), P("row", "cal", "col")),
        check_vma=False,
    )
```

```python
import functools

import jax
import jax.numpy as jnp
import numpy as np
from jax import lax
from jax.experimental import pallas as pl
from jax.experimental.pallas import tpu as pltpu
from jax.sharding import PartitionSpec as P

PANEL = 512
reg_alpha = 0.9
AXES = ("cal", "row", "col")
NX, NY, NZ = 4, 4, 8
HIGHEST = lax.Precision.HIGHEST


def flat(x, y, z, core):
    return (((x % 2) * 2 + core) * 8 + (x // 2) * 4 + y) * 8 + z


def devices():
    for x in range(NX):
        for y in range(NY):
            for z in range(NZ):
                for core in range(2):
                    yield x, y, z, core


def move(value, target):
    pairs = []
    for device in devices():
        to = target(*device)
        if to is not None:
            pairs.append((flat(*device), flat(*to)))
    return lax.ppermute(value, AXES, sorted(pairs))


def near(i, size, phase):
    return i ^ 1 if phase == 0 else (i + 1 if i % 2 else i - 1) % size


def x_step(s):
    return lambda x, y, z, c: (near(x, NX, (s + c) % 2), y, z, c)


def y_step(s):
    return lambda x, y, z, c: (x, near(y, NY, (s + c) % 2), z, c)


def z_step(s):
    return lambda x, y, z, c: (x, y, near(z, NZ, (s + c) % 2), c)


def core_swap(x, y, z, c):
    return x, y, z, 1 - c


def row_home(x, y, z, c):
    return (x, y, z, c) if z // 4 == x % 2 else (x ^ 1, y, 7 - z, c)


def tables():
    table = np.zeros((256, 32), np.int32)
    for x, y, z, c in devices():
        def ring4(i):
            p1 = lambda v: near(v, 4, c % 2)
            p2 = lambda v: near(v, 4, (1 + c) % 2)
            return [i, p1(i), p2(i), p1(p2(i))]

        step = lambda v, s: near(v, NZ, (s + c) % 2)
        first = lambda v: [v, step(v, 0)]
        third = lambda v: first(step(step(v, 2), 1))
        slots = first(z) + first(step(z, 1)) + third(z) + third(step(z, 3))
        assert sorted(slots) == list(range(8))
        low = x % 2
        blocks = [(p if p // 4 == low else 7 - p) - 4 * low for p in slots]
        halves = [low if p // 4 == low else 1 - low for p in slots]
        table[flat(x, y, z, c)] = ring4(x) + ring4(y) + blocks + halves + [c, low] + [0] * 6
    return table


TABLE = tables()


def column(meta, j, pair):
    x = jnp.where(meta[24] == 0, meta[2 * pair], meta[pair])
    return (x // 2) * 4 + meta[4 + j]


def column_copies(meta, first_refs, second_refs, cols, sem, j):
    half = first_refs[0].shape[1]
    copies = []
    for i in range(4):
        pair = jnp.where(meta[24] == 0, i // 2, i % 2)
        side = meta[i] % 2
        for which, ref in ((0, first_refs[j].at[i]), (1, second_refs[i].at[j])):
            dst = cols.at[
                2 * j + pair,
                pl.ds(pl.multiple_of(side * 2 * half + which * half, half), half),
            ]
            copies.append((True, pltpu.make_async_copy(ref, dst, sem.at[j, i, which])))
    return copies


def start_all(copies):
    for want, copy in copies:
        pl.when(want)(copy.start)


def wait_all(copies):
    for want, copy in copies:
        pl.when(want)(copy.wait)


def row_copies_of(meta, row_refs, rows, sem):
    tokens = row_refs[0].shape[2]
    wanted, refs = rows
    copies = []
    for slot in range(8):
        dst = refs.at[
            pl.ds(pl.multiple_of((meta[8 + slot] % 2) * 256, 256), 256),
            pl.ds(pl.multiple_of(meta[16 + slot] * tokens, tokens), tokens),
        ]
        copy = pltpu.make_async_copy(row_refs[slot // 2].at[slot % 2], dst, sem.at[slot])
        copies.append((meta[8 + slot] // 2 == wanted, copy))
    return copies


def gram_kernel(own, scale, *refs):
    meta, row_refs, first_refs, second_refs, refs = refs[0], refs[1:5], refs[5:9], refs[9:13], refs[13:]
    if own:
        other_ref, out_ref, rows, cols, acc, row_sem, col_sem, sem = refs
    else:
        out_ref, lead_ref, away_ref, rows, cols, acc, row_sem, col_sem, sem, lead_rows, lead_sem = refs
    wanted = meta[24] if own else 1 - meta[24]
    row_copies = row_copies_of(meta, row_refs, (wanted, rows), row_sem)
    lead_copies = [] if own else row_copies_of(meta, row_refs, (1 - wanted, lead_rows), lead_sem)
    groups = []
    for j in range(4):
        group = column_copies(meta, first_refs, second_refs, cols, col_sem, j)
        if own:
            for pair in range(2):
                k = 2 * j + pair
                src = other_ref.at[column(meta, j, pair)]
                group.append((True, pltpu.make_async_copy(src, acc.at[k], sem.at[k])))
        groups.append(group)
    start_all(row_copies)
    start_all(groups[0])
    start_all(groups[1])
    start_all(lead_copies)
    row_ids = meta[25] + lax.broadcasted_iota(jnp.int32, (512, 128), 0)
    lane = meta[26] + lax.broadcasted_iota(jnp.int32, (512, 128), 1)
    wait_all(row_copies)
    out_copies = []
    for j in range(4):
        wait_all(groups[j])
        if j + 2 < 4:
            start_all(groups[j + 2])
        for pair in range(2):
            k, a = 2 * j + pair, column(meta, j, pair)
            total = jnp.dot(rows[...], cols[k], preferred_element_type=jnp.float32)
            if own:
                for h in range(2):
                    at = slice(h * 128, (h + 1) * 128)
                    part = (total[:, at] + acc[k, :, at]) * scale
                    same = row_ids == lane + (a * 2048 + h * 128)
                    out_ref[pl.ds(2 * a + h, 512, stride=16), :] = jnp.where(
                        same, part, reg_alpha * part
                    )
            else:
                acc[k] = total
                copy = pltpu.make_async_copy(acc.at[k], out_ref.at[a], sem.at[k])
                copy.start()
                out_copies.append(copy)
    if not own:
        at = sum((2 * j + p) * (column(meta, j, p) == 0) for j in range(4) for p in range(2))
        away_ref[...] = acc[at]
        wait_all(lead_copies)
        lead_ref[...] = jnp.dot(lead_rows[...], cols[at], preferred_element_type=jnp.float32)
    for copy in out_copies:
        copy.wait()


def gram_part(scale, meta, row_bufs, first_bufs, second_bufs, other=None):
    own = other is not None
    tokens = row_bufs[0].shape[2]
    any_spec = pl.BlockSpec(memory_space=pl.ANY)
    vmem = pl.BlockSpec(memory_space=pltpu.VMEM)
    shapes = ((512 * 16, 128),) if own else ((8, 512, 256), (512, 256), (512, 256))
    rows = pltpu.VMEM((512, 2 * tokens), jnp.bfloat16)
    return pl.pallas_call(
        functools.partial(gram_kernel, own, scale),
        out_shape=tuple(jax.ShapeDtypeStruct(shape, jnp.float32) for shape in shapes),
        in_specs=[pl.BlockSpec(memory_space=pltpu.SMEM)] + [any_spec] * (12 + own),
        out_specs=(vmem,) if own else (any_spec, vmem, vmem),
        scratch_shapes=[
            rows,
            pltpu.VMEM((8, 2 * tokens, 256), jnp.bfloat16),
            pltpu.VMEM((8, 512, 256), jnp.float32),
            pltpu.SemaphoreType.DMA((8,)),
            pltpu.SemaphoreType.DMA((4, 4, 2)),
            pltpu.SemaphoreType.DMA((8,)),
        ]
        + ([] if own else [rows, pltpu.SemaphoreType.DMA((8,))]),
        compiler_params=pltpu.CompilerParams(vmem_limit_bytes=62 * 2**20),
        cost_estimate=pl.CostEstimate(
            flops=2 * 512 * 2048 * 2 * tokens, bytes_accessed=24 * 2**20, transcendentals=0
        ),
    )(meta, *row_bufs, *first_bufs, *second_bufs, *([other] if own else []))


def dot_t(a, b):
    return lax.dot_general(
        a, b, (((0,), (0,)), ((), ())), precision=HIGHEST, preferred_element_type=jnp.float32
    )


def dot_n(a, b):
    return lax.dot_general(
        a, b, (((1,), (0,)), ((), ())), precision=HIGHEST, preferred_element_type=jnp.float32
    )


def sums_kernel(meta, own, other, mine_ref, away_ref, sums):
    def dot(p, q):
        return lax.dot_general(
            p[0], q[0], (((1,), (1,)), ((), ())), preferred_element_type=jnp.float32
        )

    @pl.when(meta[26] == 0)
    def _():
        sums[:256] = dot(own, own)
        sums[256:512] = dot(own, other)
        sums[512:] = dot(other, other)

    @pl.when(meta[26] != 0)
    def _():
        sums[:256] = dot(other, other)
        sums[256:512] = dot(other, own)
        sums[512:] = dot(own, own)

    mine_ref[...] = sums[pl.ds(pl.multiple_of(meta[24] * 384, 128), 384), :]
    away_ref[...] = sums[pl.ds(pl.multiple_of((1 - meta[24]) * 384, 128), 384), :]


def leading_sums(meta, own, other):
    full = pl.BlockSpec(memory_space=pltpu.VMEM)
    return pl.pallas_call(
        sums_kernel,
        out_shape=(jax.ShapeDtypeStruct((384, 256), jnp.float32),) * 2,
        in_specs=[pl.BlockSpec(memory_space=pltpu.SMEM), full, full],
        out_specs=(full, full),
        scratch_shapes=[pltpu.VMEM((768, 256), jnp.float32)],
        compiler_params=pltpu.CompilerParams(vmem_limit_bytes=32 * 2**20),
        cost_estimate=pl.CostEstimate(flops=2**30, bytes_accessed=2**20, transcendentals=0),
    )(meta, own, other)


def factor_block(k, work, u_ref, inv_ref, block):
    n, nb, np_ = 512, 128, 16
    lo, hi = k * nb, (k + 1) * nb
    sub = lax.broadcasted_iota(jnp.int32, (np_, nb), 0)
    sub2 = lax.broadcasted_iota(jnp.int32, (np_, 2 * nb), 0)
    lane2 = lax.broadcasted_iota(jnp.int32, (np_, 2 * nb), 1)
    block[:, :nb] = work[lo:hi, lo:hi]
    block[:, nb:] = (
        lax.broadcasted_iota(jnp.int32, (nb, nb), 0) == lax.broadcasted_iota(jnp.int32, (nb, nb), 1)
    ).astype(jnp.float32)
    for base in range(0, nb, np_):
        end = base + np_
        v = block[base:end, :]
        pc = [jnp.broadcast_to(v[:, base + i:base + i + 1], (np_, nb)) for i in range(np_)]
        for i in range(np_):
            s = lax.rsqrt(pc[i][i:i + 1, :])
            below = jnp.where(sub > i, pc[i] * s, 0.0)
            for j in range(i + 1, np_):
                pc[j] = pc[j] - below * (pc[j][i:i + 1, :] * s)
            u = v[i:i + 1, :] * jnp.concatenate([s, s], 1)
            v = jnp.where(sub2 == i, u, v - jnp.concatenate([below, below], 1) * u)
        v = jnp.where(lane2 >= base + sub2, v, 0.0)
        block[base:end, :] = v
        if end < nb:
            block[end:, :] -= dot_t(v[:, :nb], v)[end:]
    x = block[:, nb:]
    u_ref[lo:hi, lo:hi] = block[:, :nb]
    inv_ref[lo:hi, lo:hi] = x
    if k:
        inner = dot_t(u_ref[0:lo, lo:hi], inv_ref[0:lo, 0:lo])
        inv_ref[lo:hi, 0:lo] = -dot_n(x, inner)
    if hi < n:
        right = dot_n(x, work[lo:hi, hi:n])
        u_ref[lo:hi, hi:n] = right
        work[hi:n, hi:n] -= dot_t(right, right)


def factor_first(scale, sums, work, u_ref, inv_ref, block):
    rid = lax.broadcasted_iota(jnp.int32, (256, 256), 0)
    cid = lax.broadcasted_iota(jnp.int32, (256, 256), 1)

    def regular(part):
        return jnp.where(rid == cid, part * scale, reg_alpha * (part * scale))

    work[...] = jnp.zeros((512, 512), jnp.float32)
    work[:256, :256] = regular(sums[:256])
    work[:256, 256:] = reg_alpha * (sums[256:512] * scale)
    work[256:, 256:] = regular(sums[512:])
    u_ref[...] = jnp.zeros((512, 512), jnp.float32)
    inv_ref[...] = jnp.zeros((512, 512), jnp.float32)
    for k in (0, 1):
        factor_block(k, work, u_ref, inv_ref, block)


def factor_second(work_ref, u_in, inv_in, u_ref, inv_ref, work, block):
    work[...] = work_ref[...]
    u_ref[...] = u_in[...]
    inv_ref[...] = inv_in[...]
    for k in (2, 3):
        factor_block(k, work, u_ref, inv_ref, block)


def factor_part(kernel, n_out, args):
    full = pl.BlockSpec(memory_space=pltpu.VMEM)
    shape = jax.ShapeDtypeStruct((512, 512), jnp.float32)
    small = pltpu.VMEM((128, 256), jnp.float32)
    return pl.pallas_call(
        kernel,
        out_shape=(shape,) * n_out,
        in_specs=[full] * len(args),
        out_specs=(full,) * n_out,
        scratch_shapes=[pltpu.VMEM((512, 512), jnp.float32)] * (3 - n_out) + [small],
        compiler_params=pltpu.CompilerParams(vmem_limit_bytes=32 * 2**20),
        cost_estimate=pl.CostEstimate(flops=2**20, bytes_accessed=2**20, transcendentals=512),
    )(*args)


def per_device(acts_one, acts_two):
    cal, row, z = (lax.axis_index(a) for a in AXES)
    low, core = cal // 2, cal % 2
    total_tokens = 8 * acts_one.shape[0]
    scale = 1.0 / total_tokens
    device = (cal * 8 + row) * 8 + z
    meta = lax.dynamic_index_in_dim(jnp.asarray(TABLE), device, 0, keepdims=False)
    after = lax.optimization_barrier
    root = lambda x, y, z: (x // 2, y) == (0, 0) and z < 2

    row_start = row * 2048 + cal * 512
    meta = meta.at[25].set(row_start).at[26].set(z * 256)

    piece = jnp.concatenate([acts_one.T, acts_two.T], 1)[None]
    other = move(piece, lambda x, y, z, c: (x, y, 1 - z, c) if root(x, y, z) else None)
    r0 = move(piece, row_home)
    r01 = jnp.concatenate([r0, move(r0, z_step(0))], 0)
    a0, b0 = acts_one[None], acts_two[None]
    a01 = jnp.concatenate([a0, move(a0, x_step(0))], 0)
    b01 = jnp.concatenate([b0, move(b0, y_step(0))], 0)
    first = jnp.concatenate([a01, move(a01, x_step(1))], 0)
    second = jnp.concatenate([b01, move(b01, y_step(1))], 0)
    lead, away = leading_sums(meta, piece, other)
    lead = lead + move(away, lambda x, y, z, c: (x, y, z, 1 - c) if root(x, y, z) else None)
    r01, first, second, lead = after((r01, first, second, lead))

    r2 = move(r01, z_step(1))
    first1 = move(first, y_step(0))
    lead = lead + move(lead, lambda x, y, z, c: (x ^ 1, y, z, c) if root(x, y, z) else None)
    lead = jnp.where(row == 0, lead, 0.0)
    lead = lead + move(lead, lambda x, y, z, c: (x + 2, y, z, c) if root(x, y, z) else None)
    r01, r2, first, first1, second, lead = after((r01, r2, first, first1, second, lead))

    r3 = move(r2, z_step(2))
    second1 = move(second, x_step(0))
    lead = lead + move(lead, lambda x, y, z, c: (x, 1, z, c) if y == 0 and z < 2 else None)
    lead = lead + move(lead, lambda x, y, z, c: (x, 3 - y, z, c) if y < 2 and z < 2 else None)
    theirs = move(lead, lambda x, y, z, c: (x, y, z, 1 - c) if z < 2 else None)
    lead = jnp.where(core == 0, jnp.stack([lead, theirs]), jnp.stack([theirs, lead]))
    r01, r2, r3, first, first1, second, second1, lead = after(
        (r01, r2, r3, first, first1, second, second1, lead)
    )

    r4 = move(r3, z_step(3))
    first2 = move(first, y_step(1))
    second2 = move(second, x_step(1))
    first3 = move(first1, y_step(1))
    second3 = move(second1, x_step(1))
    state = factor_part(functools.partial(factor_first, scale), 3, (lead.reshape(768, 256),))
    upper, inverse = factor_part(factor_second, 2, state)
    pieces, upper, inverse = after(
        (
            (
                (r01, r2, r3, r4),
                (first, first1, first2, first3),
                (second, second1, second2, second3),
            ),
            upper,
            inverse,
        )
    )

    theirs, block, away = gram_part(scale, meta, *pieces)
    away = move(away, lambda x, y, z, c: (x, y, z, 1 - c) if z < 2 else None)
    away, theirs = after((away, theirs))
    theirs = move(theirs, core_swap)
    block = (block + away) * scale
    row_ids = row_start + jnp.arange(512, dtype=jnp.int32)[:, None]
    col_ids = z * 256 + jnp.arange(256, dtype=jnp.int32)[None, :]
    block = jnp.where(row_ids == col_ids, block, reg_alpha * block)

    edge = z == 0
    solved = lax.dot_general(
        jnp.where(edge, inverse[:, :256], inverse[:, 256:]), block, (((1,), (1,)), ((), ())),
        precision=HIGHEST, preferred_element_type=jnp.float32,
    )
    head = jnp.where(edge, upper, 0.0)
    solved = jnp.where((row == 0) & (cal == 0), head, solved).reshape(4, 128, 512)
    parts = [jnp.where(edge, solved[0], 0.0)]
    for i in range(3):
        def target(x, y, z, c, i=i):
            if z == 0:
                return x, y, 2 * i + 2, c
            return (x, y, 2 * i + 4, c) if z == 1 and i < 2 else None

        value = jnp.where(edge, solved[i + 1], solved[i + 2]) if i < 2 else solved[3]
        parts.append(move(value, target))
    (gram_reg,) = gram_part(scale, meta, *pieces, other=theirs)
    gram_reg, parts = after((gram_reg, parts))
    share = functools.reduce(jnp.add, parts)
    odd = move(share[64:], lambda x, y, z, c: (x, y, z + 1, c) if z % 2 == 0 else None)
    share = jnp.where(z % 2 == 0, share[:64], odd)
    return gram_reg.reshape(1, 512, 8, 1, 256), share.T.reshape(1, 512, 64)


def solution(mesh):
    return jax.shard_map(
        per_device,
        mesh=mesh,
        in_specs=(P("cal", ("row", "col")), P("cal", ("row", "col"))),
        out_specs=(P("row", "cal", None, "col", None), P("row", "cal", "col")),
        check_vma=False,
    )
```

```python
import functools

import jax
import jax.numpy as jnp
import numpy as np
from jax import lax
from jax.experimental import pallas as pl
from jax.experimental.pallas import tpu as pltpu
from jax.sharding import PartitionSpec as P

PANEL = 512
reg_alpha = 0.9
AXES = ("cal", "row", "col")
NX, NY, NZ = 4, 4, 8
HIGHEST = lax.Precision.HIGHEST


def flat(x, y, z, core):
    return (((x % 2) * 2 + core) * 8 + (x // 2) * 4 + y) * 8 + z


def devices():
    for x in range(NX):
        for y in range(NY):
            for z in range(NZ):
                for core in range(2):
                    yield x, y, z, core


def move(value, target):
    pairs = []
    for device in devices():
        to = target(*device)
        if to is not None:
            pairs.append((flat(*device), flat(*to)))
    return lax.ppermute(value, AXES, sorted(pairs))


def near(i, size, phase):
    return i ^ 1 if phase == 0 else (i + 1 if i % 2 else i - 1) % size


def x_step(s):
    return lambda x, y, z, c: (near(x, NX, (s + c) % 2), y, z, c)


def y_step(s):
    return lambda x, y, z, c: (x, near(y, NY, (s + c) % 2), z, c)


def z_step(s):
    return lambda x, y, z, c: (x, y, near(z, NZ, (s + c) % 2), c)


def core_swap(x, y, z, c):
    return x, y, z, 1 - c


def row_home(x, y, z, c):
    return (x, y, z, c) if z // 4 == x % 2 else (x ^ 1, y, 7 - z, c)


def tables():
    table = np.zeros((256, 32), np.int32)
    for x, y, z, c in devices():
        def ring4(i):
            p1 = lambda v: near(v, 4, c % 2)
            p2 = lambda v: near(v, 4, (1 + c) % 2)
            return [i, p1(i), p2(i), p1(p2(i))]

        step = lambda v, s: near(v, NZ, (s + c) % 2)
        first = lambda v: [v, step(v, 0)]
        third = lambda v: first(step(step(v, 2), 1))
        slots = first(z) + first(step(z, 1)) + third(z) + third(step(z, 3))
        assert sorted(slots) == list(range(8))
        low = x % 2
        blocks = [(p if p // 4 == low else 7 - p) - 4 * low for p in slots]
        halves = [low if p // 4 == low else 1 - low for p in slots]
        table[flat(x, y, z, c)] = ring4(x) + ring4(y) + blocks + halves + [c, low] + [0] * 6
    return table


TABLE = tables()


def column(meta, j, pair):
    x = jnp.where(meta[24] == 0, meta[2 * pair], meta[pair])
    return (x // 2) * 4 + meta[4 + j]


def column_copies(meta, first_refs, second_refs, cols, sem, j):
    half = first_refs[0].shape[1]
    copies = []
    for i in range(4):
        pair = jnp.where(meta[24] == 0, i // 2, i % 2)
        side = meta[i] % 2
        for which, ref in ((0, first_refs[j].at[i]), (1, second_refs[i].at[j])):
            dst = cols.at[
                2 * j + pair,
                pl.ds(pl.multiple_of(side * 2 * half + which * half, half), half),
            ]
            copies.append((True, pltpu.make_async_copy(ref, dst, sem.at[j, i, which])))
    return copies


def start_all(copies):
    for want, copy in copies:
        pl.when(want)(copy.start)


def wait_all(copies):
    for want, copy in copies:
        pl.when(want)(copy.wait)


def row_copies_of(meta, row_refs, rows, sem):
    tokens = row_refs[0].shape[2]
    wanted, refs = rows
    copies = []
    for slot in range(8):
        dst = refs.at[
            pl.ds(pl.multiple_of((meta[8 + slot] % 2) * 256, 256), 256),
            pl.ds(pl.multiple_of(meta[16 + slot] * tokens, tokens), tokens),
        ]
        copy = pltpu.make_async_copy(row_refs[slot // 2].at[slot % 2], dst, sem.at[slot])
        copies.append((meta[8 + slot] // 2 == wanted, copy))
    return copies


def gram_kernel(own, scale, *refs):
    meta, row_refs, first_refs, second_refs, refs = refs[0], refs[1:5], refs[5:9], refs[9:13], refs[13:]
    if own:
        other_ref, out_ref, rows, cols, acc, row_sem, col_sem, sem = refs
    else:
        out_ref, lead_ref, away_ref, rows, cols, acc, row_sem, col_sem, sem, lead_rows, lead_sem = refs
    wanted = meta[24] if own else 1 - meta[24]
    row_copies = row_copies_of(meta, row_refs, (wanted, rows), row_sem)
    lead_copies = [] if own else row_copies_of(meta, row_refs, (1 - wanted, lead_rows), lead_sem)
    groups = []
    for j in range(4):
        group = column_copies(meta, first_refs, second_refs, cols, col_sem, j)
        if own:
            for pair in range(2):
                k = 2 * j + pair
                src = other_ref.at[column(meta, j, pair)]
                group.append((True, pltpu.make_async_copy(src, acc.at[k], sem.at[k])))
        groups.append(group)
    start_all(row_copies)
    start_all(groups[0])
    row_ids = meta[25] + lax.broadcasted_iota(jnp.int32, (512, 128), 0)
    lane = meta[26] + lax.broadcasted_iota(jnp.int32, (512, 128), 1)
    wait_all(row_copies)
    start_all(groups[1])
    out_copies = []
    for j in range(4):
        wait_all(groups[j])
        if 0 < j < 3:
            start_all(groups[j + 1])
        elif j == 3:
            start_all(lead_copies)
        for pair in range(2):
            k, a = 2 * j + pair, column(meta, j, pair)
            total = jnp.dot(rows[...], cols[k], preferred_element_type=jnp.float32)
            if own:
                for h in range(2):
                    at = slice(h * 128, (h + 1) * 128)
                    part = (total[:, at] + acc[k, :, at]) * scale
                    same = row_ids == lane + (a * 2048 + h * 128)
                    out_ref[pl.ds(2 * a + h, 512, stride=16), :] = jnp.where(
                        same, part, reg_alpha * part
                    )
            else:
                acc[k] = total
                copy = pltpu.make_async_copy(acc.at[k], out_ref.at[a], sem.at[k])
                copy.start()
                out_copies.append(copy)
    if not own:
        at = sum((2 * j + p) * (column(meta, j, p) == 0) for j in range(4) for p in range(2))
        away_ref[...] = acc[at]
        wait_all(lead_copies)
        lead_ref[...] = jnp.dot(lead_rows[...], cols[at], preferred_element_type=jnp.float32)
    for copy in out_copies:
        copy.wait()


def gram_part(scale, meta, row_bufs, first_bufs, second_bufs, other=None):
    own = other is not None
    tokens = row_bufs[0].shape[2]
    any_spec = pl.BlockSpec(memory_space=pl.ANY)
    vmem = pl.BlockSpec(memory_space=pltpu.VMEM)
    shapes = ((512 * 16, 128),) if own else ((8, 512, 256), (512, 256), (512, 256))
    rows = pltpu.VMEM((512, 2 * tokens), jnp.bfloat16)
    return pl.pallas_call(
        functools.partial(gram_kernel, own, scale),
        out_shape=tuple(jax.ShapeDtypeStruct(shape, jnp.float32) for shape in shapes),
        in_specs=[pl.BlockSpec(memory_space=pltpu.SMEM)] + [any_spec] * (12 + own),
        out_specs=(vmem,) if own else (any_spec, vmem, vmem),
        scratch_shapes=[
            rows,
            pltpu.VMEM((8, 2 * tokens, 256), jnp.bfloat16),
            pltpu.VMEM((8, 512, 256), jnp.float32),
            pltpu.SemaphoreType.DMA((8,)),
            pltpu.SemaphoreType.DMA((4, 4, 2)),
            pltpu.SemaphoreType.DMA((8,)),
        ]
        + ([] if own else [rows, pltpu.SemaphoreType.DMA((8,))]),
        compiler_params=pltpu.CompilerParams(vmem_limit_bytes=62 * 2**20),
        cost_estimate=pl.CostEstimate(
            flops=2 * 512 * 2048 * 2 * tokens, bytes_accessed=24 * 2**20, transcendentals=0
        ),
    )(meta, *row_bufs, *first_bufs, *second_bufs, *([other] if own else []))


def dot_t(a, b):
    return lax.dot_general(
        a, b, (((0,), (0,)), ((), ())), precision=HIGHEST, preferred_element_type=jnp.float32
    )


def dot_n(a, b):
    return lax.dot_general(
        a, b, (((1,), (0,)), ((), ())), precision=HIGHEST, preferred_element_type=jnp.float32
    )


def sums_kernel(meta, own, other, mine_ref, away_ref, sums):
    def dot(p, q):
        return lax.dot_general(
            p[0], q[0], (((1,), (1,)), ((), ())), preferred_element_type=jnp.float32
        )

    @pl.when(meta[26] == 0)
    def _():
        sums[:256] = dot(own, own)
        sums[256:512] = dot(own, other)
        sums[512:] = dot(other, other)

    @pl.when(meta[26] != 0)
    def _():
        sums[:256] = dot(other, other)
        sums[256:512] = dot(other, own)
        sums[512:] = dot(own, own)

    mine_ref[...] = sums[pl.ds(pl.multiple_of(meta[24] * 384, 128), 384), :]
    away_ref[...] = sums[pl.ds(pl.multiple_of((1 - meta[24]) * 384, 128), 384), :]


def leading_sums(meta, own, other):
    full = pl.BlockSpec(memory_space=pltpu.VMEM)
    return pl.pallas_call(
        sums_kernel,
        out_shape=(jax.ShapeDtypeStruct((384, 256), jnp.float32),) * 2,
        in_specs=[pl.BlockSpec(memory_space=pltpu.SMEM), full, full],
        out_specs=(full, full),
        scratch_shapes=[pltpu.VMEM((768, 256), jnp.float32)],
        compiler_params=pltpu.CompilerParams(vmem_limit_bytes=32 * 2**20),
        cost_estimate=pl.CostEstimate(flops=2**30, bytes_accessed=2**20, transcendentals=0),
    )(meta, own, other)


def factor_block(k, work, u_ref, inv_ref, block):
    n, nb, np_ = 512, 128, 16
    lo, hi = k * nb, (k + 1) * nb
    sub = lax.broadcasted_iota(jnp.int32, (np_, nb), 0)
    sub2 = lax.broadcasted_iota(jnp.int32, (np_, 2 * nb), 0)
    lane2 = lax.broadcasted_iota(jnp.int32, (np_, 2 * nb), 1)
    block[:, :nb] = work[lo:hi, lo:hi]
    block[:, nb:] = (
        lax.broadcasted_iota(jnp.int32, (nb, nb), 0) == lax.broadcasted_iota(jnp.int32, (nb, nb), 1)
    ).astype(jnp.float32)
    for base in range(0, nb, np_):
        end = base + np_
        v = block[base:end, :]
        pc = [jnp.broadcast_to(v[:, base + i:base + i + 1], (np_, nb)) for i in range(np_)]
        for i in range(np_):
            s = lax.rsqrt(pc[i][i:i + 1, :])
            below = jnp.where(sub > i, pc[i] * s, 0.0)
            for j in range(i + 1, np_):
                pc[j] = pc[j] - below * (pc[j][i:i + 1, :] * s)
            u = v[i:i + 1, :] * jnp.concatenate([s, s], 1)
            v = jnp.where(sub2 == i, u, v - jnp.concatenate([below, below], 1) * u)
        v = jnp.where(lane2 >= base + sub2, v, 0.0)
        block[base:end, :] = v
        if end < nb:
            block[end:, :] -= dot_t(v[:, :nb], v)[end:]
    x = block[:, nb:]
    u_ref[lo:hi, lo:hi] = block[:, :nb]
    inv_ref[lo:hi, lo:hi] = x
    if k:
        inner = dot_t(u_ref[0:lo, lo:hi], inv_ref[0:lo, 0:lo])
        inv_ref[lo:hi, 0:lo] = -dot_n(x, inner)
    if hi < n:
        right = dot_n(x, work[lo:hi, hi:n])
        u_ref[lo:hi, hi:n] = right
        work[hi:n, hi:n] -= dot_t(right, right)


def factor_first(scale, sums, work, u_ref, inv_ref, block):
    rid = lax.broadcasted_iota(jnp.int32, (256, 256), 0)
    cid = lax.broadcasted_iota(jnp.int32, (256, 256), 1)

    def regular(part):
        return jnp.where(rid == cid, part * scale, reg_alpha * (part * scale))

    work[...] = jnp.zeros((512, 512), jnp.float32)
    work[:256, :256] = regular(sums[:256])
    work[:256, 256:] = reg_alpha * (sums[256:512] * scale)
    work[256:, 256:] = regular(sums[512:])
    u_ref[...] = jnp.zeros((512, 512), jnp.float32)
    inv_ref[...] = jnp.zeros((512, 512), jnp.float32)
    for k in (0, 1):
        factor_block(k, work, u_ref, inv_ref, block)


def factor_second(work_ref, u_in, inv_in, u_ref, inv_ref, work, block):
    work[...] = work_ref[...]
    u_ref[...] = u_in[...]
    inv_ref[...] = inv_in[...]
    for k in (2, 3):
        factor_block(k, work, u_ref, inv_ref, block)


def factor_part(kernel, n_out, args):
    full = pl.BlockSpec(memory_space=pltpu.VMEM)
    shape = jax.ShapeDtypeStruct((512, 512), jnp.float32)
    small = pltpu.VMEM((128, 256), jnp.float32)
    return pl.pallas_call(
        kernel,
        out_shape=(shape,) * n_out,
        in_specs=[full] * len(args),
        out_specs=(full,) * n_out,
        scratch_shapes=[pltpu.VMEM((512, 512), jnp.float32)] * (3 - n_out) + [small],
        compiler_params=pltpu.CompilerParams(vmem_limit_bytes=32 * 2**20),
        cost_estimate=pl.CostEstimate(flops=2**20, bytes_accessed=2**20, transcendentals=512),
    )(*args)


def per_device(acts_one, acts_two):
    cal, row, z = (lax.axis_index(a) for a in AXES)
    low, core = cal // 2, cal % 2
    total_tokens = 8 * acts_one.shape[0]
    scale = 1.0 / total_tokens
    device = (cal * 8 + row) * 8 + z
    meta = lax.dynamic_index_in_dim(jnp.asarray(TABLE), device, 0, keepdims=False)
    after = lax.optimization_barrier
    root = lambda x, y, z: (x // 2, y) == (0, 0) and z < 2

    row_start = row * 2048 + cal * 512
    meta = meta.at[25].set(row_start).at[26].set(z * 256)

    piece = jnp.concatenate([acts_one.T, acts_two.T], 1)[None]
    other = move(piece, lambda x, y, z, c: (x, y, 1 - z, c) if root(x, y, z) else None)
    r0 = move(piece, row_home)
    r01 = jnp.concatenate([r0, move(r0, z_step(0))], 0)
    a0, b0 = acts_one[None], acts_two[None]
    a01 = jnp.concatenate([a0, move(a0, x_step(0))], 0)
    b01 = jnp.concatenate([b0, move(b0, y_step(0))], 0)
    first = jnp.concatenate([a01, move(a01, x_step(1))], 0)
    second = jnp.concatenate([b01, move(b01, y_step(1))], 0)
    lead, away = leading_sums(meta, piece, other)
    lead = lead + move(away, lambda x, y, z, c: (x, y, z, 1 - c) if root(x, y, z) else None)
    r01, first, second, lead = after((r01, first, second, lead))

    r2 = move(r01, z_step(1))
    first1 = move(first, y_step(0))
    lead = lead + move(lead, lambda x, y, z, c: (x ^ 1, y, z, c) if root(x, y, z) else None)
    lead = jnp.where(row == 0, lead, 0.0)
    lead = lead + move(lead, lambda x, y, z, c: (x + 2, y, z, c) if root(x, y, z) else None)
    lead, second = after((lead, second))
    second1 = move(second, x_step(0))
    lead, first1 = after((lead, first1))

    r3 = move(r2, z_step(2))
    lead = lead + move(lead, lambda x, y, z, c: (x, 1, z, c) if y == 0 and z < 2 else None)
    lead = lead + move(lead, lambda x, y, z, c: (x, 3 - y, z, c) if y < 2 and z < 2 else None)
    theirs = move(lead, lambda x, y, z, c: (x, y, z, 1 - c) if z < 2 else None)
    lead = jnp.where(core == 0, jnp.stack([lead, theirs]), jnp.stack([theirs, lead]))
    r01, r2, r3, first, first1, second, second1, lead = after(
        (r01, r2, r3, first, first1, second, second1, lead)
    )

    r4 = move(r3, z_step(3))
    first2 = move(first, y_step(1))
    second2 = move(second, x_step(1))
    first3 = move(first1, y_step(1))
    second3 = move(second1, x_step(1))
    state = factor_part(functools.partial(factor_first, scale), 3, (lead.reshape(768, 256),))
    upper, inverse = factor_part(factor_second, 2, state)
    pieces, upper, inverse = after(
        (
            (
                (r01, r2, r3, r4),
                (first, first1, first2, first3),
                (second, second1, second2, second3),
            ),
            upper,
            inverse,
        )
    )

    theirs, block, away = gram_part(scale, meta, *pieces)
    away = move(away, lambda x, y, z, c: (x, y, z, 1 - c) if z < 2 else None)
    away, theirs = after((away, theirs))
    theirs = move(theirs, core_swap)
    block = (block + away) * scale
    row_ids = row_start + jnp.arange(512, dtype=jnp.int32)[:, None]
    col_ids = z * 256 + jnp.arange(256, dtype=jnp.int32)[None, :]
    block = jnp.where(row_ids == col_ids, block, reg_alpha * block)

    edge = z == 0
    solved = lax.dot_general(
        jnp.where(edge, inverse[:, :256], inverse[:, 256:]), block, (((1,), (1,)), ((), ())),
        precision=HIGHEST, preferred_element_type=jnp.float32,
    )
    head = jnp.where(edge, upper, 0.0)
    solved = jnp.where((row == 0) & (cal == 0), head, solved).reshape(4, 128, 512)
    parts = [jnp.where(edge, solved[0], 0.0)]
    for i in range(3):
        def target(x, y, z, c, i=i):
            if z == 0:
                return x, y, 2 * i + 2, c
            return (x, y, 2 * i + 4, c) if z == 1 and i < 2 else None

        value = jnp.where(edge, solved[i + 1], solved[i + 2]) if i < 2 else solved[3]
        parts.append(move(value, target))
    (gram_reg,) = gram_part(scale, meta, *pieces, other=theirs)
    gram_reg, parts = after((gram_reg, parts))
    share = functools.reduce(jnp.add, parts)
    odd = move(share[64:], lambda x, y, z, c: (x, y, z + 1, c) if z % 2 == 0 else None)
    share = jnp.where(z % 2 == 0, share[:64], odd)
    return gram_reg.reshape(1, 512, 8, 1, 256), share.T.reshape(1, 512, 64)


def solution(mesh):
    return jax.shard_map(
        per_device,
        mesh=mesh,
        in_specs=(P("cal", ("row", "col")), P("cal", ("row", "col"))),
        out_specs=(P("row", "cal", None, "col", None), P("row", "cal", "col")),
        check_vma=False,
    )
```

```python
import functools

import jax
import jax.numpy as jnp
import numpy as np
from jax import lax
from jax.experimental import pallas as pl
from jax.experimental.pallas import tpu as pltpu
from jax.sharding import PartitionSpec as P

PANEL = 512
reg_alpha = 0.9
AXES = ("cal", "row", "col")
NX, NY, NZ = 4, 4, 8
HIGHEST = lax.Precision.HIGHEST


def flat(x, y, z, core):
    return (((x % 2) * 2 + core) * 8 + (x // 2) * 4 + y) * 8 + z


def devices():
    for x in range(NX):
        for y in range(NY):
            for z in range(NZ):
                for core in range(2):
                    yield x, y, z, core


def move(value, target):
    pairs = []
    for device in devices():
        to = target(*device)
        if to is not None:
            pairs.append((flat(*device), flat(*to)))
    return lax.ppermute(value, AXES, sorted(pairs))


def near(i, size, phase):
    return i ^ 1 if phase == 0 else (i + 1 if i % 2 else i - 1) % size


def x_step(s):
    return lambda x, y, z, c: (near(x, NX, (s + c) % 2), y, z, c)


def y_step(s):
    return lambda x, y, z, c: (x, near(y, NY, (s + c) % 2), z, c)


def z_step(s):
    return lambda x, y, z, c: (x, y, near(z, NZ, (s + c) % 2), c)


def core_swap(x, y, z, c):
    return x, y, z, 1 - c


def row_home(x, y, z, c):
    return (x, y, z, c) if z // 4 == x % 2 else (x ^ 1, y, 7 - z, c)


def tables():
    table = np.zeros((256, 32), np.int32)
    for x, y, z, c in devices():
        def ring4(i):
            p1 = lambda v: near(v, 4, c % 2)
            p2 = lambda v: near(v, 4, (1 + c) % 2)
            return [i, p1(i), p2(i), p1(p2(i))]

        step = lambda v, s: near(v, NZ, (s + c) % 2)
        first = lambda v: [v, step(v, 0)]
        third = lambda v: first(step(step(v, 2), 1))
        slots = first(z) + first(step(z, 1)) + third(z) + third(step(z, 3))
        assert sorted(slots) == list(range(8))
        low = x % 2
        blocks = [(p if p // 4 == low else 7 - p) - 4 * low for p in slots]
        halves = [low if p // 4 == low else 1 - low for p in slots]
        table[flat(x, y, z, c)] = ring4(x) + ring4(y) + blocks + halves + [c, low] + [0] * 6
    return table


TABLE = tables()


def column(meta, j, pair):
    x = jnp.where(meta[24] == 0, meta[2 * pair], meta[pair])
    return (x // 2) * 4 + meta[4 + j]


def column_copies(meta, first_refs, second_refs, cols, sem, j):
    half = first_refs[0].shape[1]
    copies = []
    for i in range(4):
        pair = jnp.where(meta[24] == 0, i // 2, i % 2)
        side = meta[i] % 2
        for which, ref in ((0, first_refs[j].at[i]), (1, second_refs[i].at[j])):
            dst = cols.at[
                2 * j + pair,
                pl.ds(pl.multiple_of(side * 2 * half + which * half, half), half),
            ]
            copies.append((True, pltpu.make_async_copy(ref, dst, sem.at[j, i, which])))
    return copies


def start_all(copies):
    for want, copy in copies:
        pl.when(want)(copy.start)


def wait_all(copies):
    for want, copy in copies:
        pl.when(want)(copy.wait)


def row_copies_of(meta, row_refs, rows, sem):
    tokens = row_refs[0].shape[2]
    wanted, refs = rows
    copies = []
    for slot in range(8):
        dst = refs.at[
            pl.ds(pl.multiple_of((meta[8 + slot] % 2) * 256, 256), 256),
            pl.ds(pl.multiple_of(meta[16 + slot] * tokens, tokens), tokens),
        ]
        copy = pltpu.make_async_copy(row_refs[slot // 2].at[slot % 2], dst, sem.at[slot])
        copies.append((meta[8 + slot] // 2 == wanted, copy))
    return copies


def gram_kernel(own, scale, *refs):
    meta, row_refs, first_refs, second_refs, refs = refs[0], refs[1:5], refs[5:9], refs[9:13], refs[13:]
    if own:
        other_ref, out_ref, rows, cols, acc, row_sem, col_sem, sem = refs
    else:
        out_ref, lead_ref, away_ref, rows, cols, acc, row_sem, col_sem, sem, lead_rows, lead_sem = refs
    wanted = meta[24] if own else 1 - meta[24]
    row_copies = row_copies_of(meta, row_refs, (wanted, rows), row_sem)
    lead_copies = [] if own else row_copies_of(meta, row_refs, (1 - wanted, lead_rows), lead_sem)
    groups = []
    for j in range(4):
        group = column_copies(meta, first_refs, second_refs, cols, col_sem, j)
        if own:
            for pair in range(2):
                k = 2 * j + pair
                src = other_ref.at[column(meta, j, pair)]
                group.append((True, pltpu.make_async_copy(src, acc.at[k], sem.at[k])))
        groups.append(group)
    start_all(row_copies)
    start_all(groups[0])
    row_ids = meta[25] + lax.broadcasted_iota(jnp.int32, (512, 128), 0)
    lane = meta[26] + lax.broadcasted_iota(jnp.int32, (512, 128), 1)
    wait_all(row_copies)
    start_all(groups[1])
    out_copies = []
    for j in range(4):
        wait_all(groups[j])
        if 0 < j < 3:
            start_all(groups[j + 1])
        elif j == 3:
            start_all(lead_copies)
        for pair in range(2):
            k, a = 2 * j + pair, column(meta, j, pair)
            total = jnp.dot(rows[...], cols[k], preferred_element_type=jnp.float32)
            if own:
                for h in range(2):
                    at = slice(h * 128, (h + 1) * 128)
                    part = (total[:, at] + acc[k, :, at]) * scale
                    same = row_ids == lane + (a * 2048 + h * 128)
                    out_ref[pl.ds(2 * a + h, 512, stride=16), :] = jnp.where(
                        same, part, reg_alpha * part
                    )
            else:
                acc[k] = total
                copy = pltpu.make_async_copy(acc.at[k], out_ref.at[a], sem.at[k])
                copy.start()
                out_copies.append(copy)
    if not own:
        at = sum((2 * j + p) * (column(meta, j, p) == 0) for j in range(4) for p in range(2))
        away_ref[...] = acc[at]
        wait_all(lead_copies)
        lead_ref[...] = jnp.dot(lead_rows[...], cols[at], preferred_element_type=jnp.float32)
    for copy in out_copies:
        copy.wait()


def gram_part(scale, meta, row_bufs, first_bufs, second_bufs, other=None):
    own = other is not None
    tokens = row_bufs[0].shape[2]
    any_spec = pl.BlockSpec(memory_space=pl.ANY)
    vmem = pl.BlockSpec(memory_space=pltpu.VMEM)
    shapes = ((512 * 16, 128),) if own else ((8, 512, 256), (512, 256), (512, 256))
    rows = pltpu.VMEM((512, 2 * tokens), jnp.bfloat16)
    return pl.pallas_call(
        functools.partial(gram_kernel, own, scale),
        out_shape=tuple(jax.ShapeDtypeStruct(shape, jnp.float32) for shape in shapes),
        in_specs=[pl.BlockSpec(memory_space=pltpu.SMEM)] + [any_spec] * (12 + own),
        out_specs=(vmem,) if own else (any_spec, vmem, vmem),
        scratch_shapes=[
            rows,
            pltpu.VMEM((8, 2 * tokens, 256), jnp.bfloat16),
            pltpu.VMEM((8, 512, 256), jnp.float32),
            pltpu.SemaphoreType.DMA((8,)),
            pltpu.SemaphoreType.DMA((4, 4, 2)),
            pltpu.SemaphoreType.DMA((8,)),
        ]
        + ([] if own else [rows, pltpu.SemaphoreType.DMA((8,))]),
        compiler_params=pltpu.CompilerParams(vmem_limit_bytes=62 * 2**20),
        cost_estimate=pl.CostEstimate(
            flops=2 * 512 * 2048 * 2 * tokens, bytes_accessed=24 * 2**20, transcendentals=0
        ),
    )(meta, *row_bufs, *first_bufs, *second_bufs, *([other] if own else []))


def dot_t(a, b):
    return lax.dot_general(
        a, b, (((0,), (0,)), ((), ())), precision=HIGHEST, preferred_element_type=jnp.float32
    )


def dot_n(a, b):
    return lax.dot_general(
        a, b, (((1,), (0,)), ((), ())), precision=HIGHEST, preferred_element_type=jnp.float32
    )


def sums_kernel(meta, own, other, mine_ref, away_ref, sums):
    def dot(p, q):
        return lax.dot_general(
            p[0], q[0], (((1,), (1,)), ((), ())), preferred_element_type=jnp.float32
        )

    @pl.when(meta[26] == 0)
    def _():
        sums[:256] = dot(own, own)
        sums[256:512] = dot(own, other)
        sums[512:] = dot(other, other)

    @pl.when(meta[26] != 0)
    def _():
        sums[:256] = dot(other, other)
        sums[256:512] = dot(other, own)
        sums[512:] = dot(own, own)

    mine_ref[...] = sums[pl.ds(pl.multiple_of(meta[24] * 384, 128), 384), :]
    away_ref[...] = sums[pl.ds(pl.multiple_of((1 - meta[24]) * 384, 128), 384), :]


def leading_sums(meta, own, other):
    full = pl.BlockSpec(memory_space=pltpu.VMEM)
    return pl.pallas_call(
        sums_kernel,
        out_shape=(jax.ShapeDtypeStruct((384, 256), jnp.float32),) * 2,
        in_specs=[pl.BlockSpec(memory_space=pltpu.SMEM), full, full],
        out_specs=(full, full),
        scratch_shapes=[pltpu.VMEM((768, 256), jnp.float32)],
        compiler_params=pltpu.CompilerParams(vmem_limit_bytes=32 * 2**20),
        cost_estimate=pl.CostEstimate(flops=2**30, bytes_accessed=2**20, transcendentals=0),
    )(meta, own, other)


def factor_block(k, work, u_ref, inv_ref, block):
    n, nb, np_ = 512, 128, 16
    lo, hi = k * nb, (k + 1) * nb
    sub = lax.broadcasted_iota(jnp.int32, (np_, nb), 0)
    sub2 = lax.broadcasted_iota(jnp.int32, (np_, 2 * nb), 0)
    lane2 = lax.broadcasted_iota(jnp.int32, (np_, 2 * nb), 1)
    block[:, :nb] = work[lo:hi, lo:hi]
    block[:, nb:] = (
        lax.broadcasted_iota(jnp.int32, (nb, nb), 0) == lax.broadcasted_iota(jnp.int32, (nb, nb), 1)
    ).astype(jnp.float32)
    for base in range(0, nb, np_):
        end = base + np_
        v = block[base:end, :]
        pc = [jnp.broadcast_to(v[:, base + i:base + i + 1], (np_, nb)) for i in range(np_)]
        for i in range(np_):
            s = lax.rsqrt(pc[i][i:i + 1, :])
            below = jnp.where(sub > i, pc[i] * s, 0.0)
            for j in range(i + 1, np_):
                pc[j] = pc[j] - below * (pc[j][i:i + 1, :] * s)
            u = v[i:i + 1, :] * jnp.concatenate([s, s], 1)
            v = jnp.where(sub2 == i, u, v - jnp.concatenate([below, below], 1) * u)
        v = jnp.where(lane2 >= base + sub2, v, 0.0)
        block[base:end, :] = v
        if end < nb:
            block[end:, :] -= dot_t(v[:, :nb], v)[end:]
    x = block[:, nb:]
    u_ref[lo:hi, lo:hi] = block[:, :nb]
    inv_ref[lo:hi, lo:hi] = x
    if k:
        inner = dot_t(u_ref[0:lo, lo:hi], inv_ref[0:lo, 0:lo])
        inv_ref[lo:hi, 0:lo] = -dot_n(x, inner)
    if hi < n:
        right = dot_n(x, work[lo:hi, hi:n])
        u_ref[lo:hi, hi:n] = right
        work[hi:n, hi:n] -= dot_t(right, right)


def factor_first(scale, sums, work, u_ref, inv_ref, block):
    rid = lax.broadcasted_iota(jnp.int32, (256, 256), 0)
    cid = lax.broadcasted_iota(jnp.int32, (256, 256), 1)

    def regular(part):
        return jnp.where(rid == cid, part * scale, reg_alpha * (part * scale))

    work[...] = jnp.zeros((512, 512), jnp.float32)
    work[:256, :256] = regular(sums[:256])
    work[:256, 256:] = reg_alpha * (sums[256:512] * scale)
    work[256:, 256:] = regular(sums[512:])
    u_ref[...] = jnp.zeros((512, 512), jnp.float32)
    inv_ref[...] = jnp.zeros((512, 512), jnp.float32)
    for k in (0, 1):
        factor_block(k, work, u_ref, inv_ref, block)


def factor_second(work_ref, u_in, inv_in, u_ref, inv_ref, work, block):
    work[...] = work_ref[...]
    u_ref[...] = u_in[...]
    inv_ref[...] = inv_in[...]
    for k in (2, 3):
        factor_block(k, work, u_ref, inv_ref, block)


def factor_part(kernel, n_out, args):
    full = pl.BlockSpec(memory_space=pltpu.VMEM)
    shape = jax.ShapeDtypeStruct((512, 512), jnp.float32)
    small = pltpu.VMEM((128, 256), jnp.float32)
    return pl.pallas_call(
        kernel,
        out_shape=(shape,) * n_out,
        in_specs=[full] * len(args),
        out_specs=(full,) * n_out,
        scratch_shapes=[pltpu.VMEM((512, 512), jnp.float32)] * (3 - n_out) + [small],
        compiler_params=pltpu.CompilerParams(vmem_limit_bytes=32 * 2**20),
        cost_estimate=pl.CostEstimate(flops=2**20, bytes_accessed=2**20, transcendentals=512),
    )(*args)


def per_device(acts_one, acts_two):
    cal, row, z = (lax.axis_index(a) for a in AXES)
    low, core = cal // 2, cal % 2
    total_tokens = 8 * acts_one.shape[0]
    scale = 1.0 / total_tokens
    device = (cal * 8 + row) * 8 + z
    meta = lax.dynamic_index_in_dim(jnp.asarray(TABLE), device, 0, keepdims=False)
    after = lax.optimization_barrier
    root = lambda x, y, z: (x // 2, y) == (0, 0) and z < 2

    row_start = row * 2048 + cal * 512
    meta = meta.at[25].set(row_start).at[26].set(z * 256)

    piece = jnp.concatenate([acts_one.T, acts_two.T], 1)[None]
    other = move(piece, lambda x, y, z, c: (x, y, 1 - z, c) if root(x, y, z) else None)
    r0 = move(piece, row_home)
    r01 = jnp.concatenate([r0, move(r0, z_step(0))], 0)
    a0, b0 = acts_one[None], acts_two[None]
    a01 = jnp.concatenate([a0, move(a0, x_step(0))], 0)
    b01 = jnp.concatenate([b0, move(b0, y_step(0))], 0)
    first = jnp.concatenate([a01, move(a01, x_step(1))], 0)
    second = jnp.concatenate([b01, move(b01, y_step(1))], 0)
    lead, away = leading_sums(meta, piece, other)
    lead = lead + move(away, lambda x, y, z, c: (x, y, z, 1 - c) if root(x, y, z) else None)
    r01, first, second, lead = after((r01, first, second, lead))

    r2 = move(r01, z_step(1))
    first1 = move(first, y_step(0))
    lead = lead + move(lead, lambda x, y, z, c: (x ^ 1, y, z, c) if root(x, y, z) else None)
    lead = jnp.where(row == 0, lead, 0.0)
    lead = lead + move(lead, lambda x, y, z, c: (x + 2, y, z, c) if root(x, y, z) else None)
    lead, second = after((lead, second))
    second1 = move(second, x_step(0))
    lead, first1 = after((lead, first1))

    r3 = move(r2, z_step(2))
    r4 = move(r3, z_step(3))
    lead = lead + move(lead, lambda x, y, z, c: (x, 1, z, c) if y == 0 and z < 2 else None)
    lead = lead + move(lead, lambda x, y, z, c: (x, 3 - y, z, c) if y < 2 and z < 2 else None)
    lead, first = after((lead, first))
    first2 = move(first, y_step(1))
    second, second1 = after((second, second1))
    second2 = move(second, x_step(1))
    theirs = move(lead, lambda x, y, z, c: (x, y, z, 1 - c) if z < 2 else None)
    lead = jnp.where(core == 0, jnp.stack([lead, theirs]), jnp.stack([theirs, lead]))
    state = factor_part(functools.partial(factor_first, scale), 3, (lead.reshape(768, 256),))
    r01, r2, r3, r4, first, first1, first2, second, second1, second2, state = after(
        (r01, r2, r3, r4, first, first1, first2, second, second1, second2, state)
    )

    first3 = move(first1, y_step(1))
    second3 = move(second1, x_step(1))
    upper, inverse = factor_part(factor_second, 2, state)
    pieces, upper, inverse = after(
        (
            (
                (r01, r2, r3, r4),
                (first, first1, first2, first3),
                (second, second1, second2, second3),
            ),
            upper,
            inverse,
        )
    )

    theirs, block, away = gram_part(scale, meta, *pieces)
    away = move(away, lambda x, y, z, c: (x, y, z, 1 - c) if z < 2 else None)
    away, theirs = after((away, theirs))
    theirs = move(theirs, core_swap)
    block = (block + away) * scale
    row_ids = row_start + jnp.arange(512, dtype=jnp.int32)[:, None]
    col_ids = z * 256 + jnp.arange(256, dtype=jnp.int32)[None, :]
    block = jnp.where(row_ids == col_ids, block, reg_alpha * block)

    edge = z == 0
    solved = lax.dot_general(
        jnp.where(edge, inverse[:, :256], inverse[:, 256:]), block, (((1,), (1,)), ((), ())),
        precision=HIGHEST, preferred_element_type=jnp.float32,
    )
    head = jnp.where(edge, upper, 0.0)
    solved = jnp.where((row == 0) & (cal == 0), head, solved).reshape(4, 128, 512)
    parts = [jnp.where(edge, solved[0], 0.0)]
    for i in range(3):
        def target(x, y, z, c, i=i):
            if z == 0:
                return x, y, 2 * i + 2, c
            return (x, y, 2 * i + 4, c) if z == 1 and i < 2 else None

        value = jnp.where(edge, solved[i + 1], solved[i + 2]) if i < 2 else solved[3]
        parts.append(move(value, target))
    (gram_reg,) = gram_part(scale, meta, *pieces, other=theirs)
    gram_reg, parts = after((gram_reg, parts))
    share = functools.reduce(jnp.add, parts)
    odd = move(share[64:], lambda x, y, z, c: (x, y, z + 1, c) if z % 2 == 0 else None)
    share = jnp.where(z % 2 == 0, share[:64], odd)
    return gram_reg.reshape(1, 512, 8, 1, 256), share.T.reshape(1, 512, 64)


def solution(mesh):
    return jax.shard_map(
        per_device,
        mesh=mesh,
        in_specs=(P("cal", ("row", "col")), P("cal", ("row", "col"))),
        out_specs=(P("row", "cal", None, "col", None), P("row", "cal", "col")),
        check_vma=False,
    )
```

```python
import functools

import jax
import jax.numpy as jnp
import numpy as np
from jax import lax
from jax.experimental import pallas as pl
from jax.experimental.pallas import tpu as pltpu
from jax.sharding import PartitionSpec as P

PANEL = 512
reg_alpha = 0.9
AXES = ("cal", "row", "col")
NX, NY, NZ = 4, 4, 8
HIGHEST = lax.Precision.HIGHEST


def flat(x, y, z, core):
    return (((x % 2) * 2 + core) * 8 + (x // 2) * 4 + y) * 8 + z


def devices():
    for x in range(NX):
        for y in range(NY):
            for z in range(NZ):
                for core in range(2):
                    yield x, y, z, core


def move(value, target):
    pairs = []
    for device in devices():
        to = target(*device)
        if to is not None:
            pairs.append((flat(*device), flat(*to)))
    return lax.ppermute(value, AXES, sorted(pairs))


def near(i, size, phase):
    return i ^ 1 if phase == 0 else (i + 1 if i % 2 else i - 1) % size


def x_step(s):
    return lambda x, y, z, c: (near(x, NX, (s + c) % 2), y, z, c)


def y_step(s):
    return lambda x, y, z, c: (x, near(y, NY, (s + c) % 2), z, c)


def z_step(s):
    return lambda x, y, z, c: (x, y, near(z, NZ, (s + c) % 2), c)


def core_swap(x, y, z, c):
    return x, y, z, 1 - c


def row_home(x, y, z, c):
    return (x, y, z, c) if z // 4 == x % 2 else (x ^ 1, y, 7 - z, c)


def tables():
    table = np.zeros((256, 32), np.int32)
    for x, y, z, c in devices():
        def ring4(i):
            p1 = lambda v: near(v, 4, c % 2)
            p2 = lambda v: near(v, 4, (1 + c) % 2)
            return [i, p1(i), p2(i), p1(p2(i))]

        step = lambda v, s: near(v, NZ, (s + c) % 2)
        first = lambda v: [v, step(v, 0)]
        third = lambda v: first(step(step(v, 2), 1))
        slots = first(z) + first(step(z, 1)) + third(z) + third(step(z, 3))
        assert sorted(slots) == list(range(8))
        low = x % 2
        blocks = [(p if p // 4 == low else 7 - p) - 4 * low for p in slots]
        halves = [low if p // 4 == low else 1 - low for p in slots]
        table[flat(x, y, z, c)] = ring4(x) + ring4(y) + blocks + halves + [c, low] + [0] * 6
    return table


TABLE = tables()


def column(meta, j, pair):
    x = jnp.where(meta[24] == 0, meta[2 * pair], meta[pair])
    return (x // 2) * 4 + meta[4 + j]


def column_copies(meta, first_refs, second_refs, cols, sem, j):
    half = first_refs[0].shape[1]
    copies = []
    for i in range(4):
        pair = jnp.where(meta[24] == 0, i // 2, i % 2)
        side = meta[i] % 2
        for which, ref in ((0, first_refs[j].at[i]), (1, second_refs[i].at[j])):
            dst = cols.at[
                2 * j + pair,
                pl.ds(pl.multiple_of(side * 2 * half + which * half, half), half),
            ]
            copies.append((True, pltpu.make_async_copy(ref, dst, sem.at[j, i, which])))
    return copies


def start_all(copies):
    for want, copy in copies:
        pl.when(want)(copy.start)


def wait_all(copies):
    for want, copy in copies:
        pl.when(want)(copy.wait)


def row_copies_of(meta, row_refs, rows, sem):
    tokens = row_refs[0].shape[2]
    wanted, refs = rows
    copies = []
    for slot in range(8):
        dst = refs.at[
            pl.ds(pl.multiple_of((meta[8 + slot] % 2) * 256, 256), 256),
            pl.ds(pl.multiple_of(meta[16 + slot] * tokens, tokens), tokens),
        ]
        copy = pltpu.make_async_copy(row_refs[slot // 2].at[slot % 2], dst, sem.at[slot])
        copies.append((meta[8 + slot] // 2 == wanted, copy))
    return copies


def gram_kernel(own, scale, *refs):
    meta, row_refs, first_refs, second_refs, refs = refs[0], refs[1:5], refs[5:9], refs[9:13], refs[13:]
    if own:
        other_ref, out_ref, rows, cols, acc, row_sem, col_sem, sem = refs
    else:
        out_ref, lead_ref, away_ref, rows, cols, acc, row_sem, col_sem, sem, lead_rows, lead_sem = refs
    wanted = meta[24] if own else 1 - meta[24]
    row_copies = row_copies_of(meta, row_refs, (wanted, rows), row_sem)
    lead_copies = [] if own else row_copies_of(meta, row_refs, (1 - wanted, lead_rows), lead_sem)
    groups = []
    for j in range(4):
        group = column_copies(meta, first_refs, second_refs, cols, col_sem, j)
        if own:
            for pair in range(2):
                k = 2 * j + pair
                src = other_ref.at[column(meta, j, pair)]
                group.append((True, pltpu.make_async_copy(src, acc.at[k], sem.at[k])))
        groups.append(group)
    start_all(row_copies)
    start_all(groups[0])
    row_ids = meta[25] + lax.broadcasted_iota(jnp.int32, (512, 128), 0)
    lane = meta[26] + lax.broadcasted_iota(jnp.int32, (512, 128), 1)
    wait_all(row_copies)
    start_all(groups[1])
    out_copies = []
    for j in range(4):
        wait_all(groups[j])
        if 0 < j < 3:
            start_all(groups[j + 1])
        elif j == 3:
            start_all(lead_copies)
        for pair in range(2):
            k, a = 2 * j + pair, column(meta, j, pair)
            total = jnp.dot(rows[...], cols[k], preferred_element_type=jnp.float32)
            if own:
                for h in range(2):
                    at = slice(h * 128, (h + 1) * 128)
                    part = (total[:, at] + acc[k, :, at]) * scale
                    same = row_ids == lane + (a * 2048 + h * 128)
                    out_ref[pl.ds(2 * a + h, 512, stride=16), :] = jnp.where(
                        same, part, reg_alpha * part
                    )
            else:
                acc[k] = total
                copy = pltpu.make_async_copy(acc.at[k], out_ref.at[a], sem.at[k])
                copy.start()
                out_copies.append(copy)
    if not own:
        at = sum((2 * j + p) * (column(meta, j, p) == 0) for j in range(4) for p in range(2))
        away_ref[...] = acc[at]
        wait_all(lead_copies)
        lead_ref[...] = jnp.dot(lead_rows[...], cols[at], preferred_element_type=jnp.float32)
    for copy in out_copies:
        copy.wait()


def gram_part(scale, meta, row_bufs, first_bufs, second_bufs, other=None):
    own = other is not None
    tokens = row_bufs[0].shape[2]
    any_spec = pl.BlockSpec(memory_space=pl.ANY)
    vmem = pl.BlockSpec(memory_space=pltpu.VMEM)
    shapes = ((512 * 16, 128),) if own else ((8, 512, 256), (512, 256), (512, 256))
    rows = pltpu.VMEM((512, 2 * tokens), jnp.bfloat16)
    return pl.pallas_call(
        functools.partial(gram_kernel, own, scale),
        out_shape=tuple(jax.ShapeDtypeStruct(shape, jnp.float32) for shape in shapes),
        in_specs=[pl.BlockSpec(memory_space=pltpu.SMEM)] + [any_spec] * (12 + own),
        out_specs=(vmem,) if own else (any_spec, vmem, vmem),
        scratch_shapes=[
            rows,
            pltpu.VMEM((8, 2 * tokens, 256), jnp.bfloat16),
            pltpu.VMEM((8, 512, 256), jnp.float32),
            pltpu.SemaphoreType.DMA((8,)),
            pltpu.SemaphoreType.DMA((4, 4, 2)),
            pltpu.SemaphoreType.DMA((8,)),
        ]
        + ([] if own else [rows, pltpu.SemaphoreType.DMA((8,))]),
        compiler_params=pltpu.CompilerParams(vmem_limit_bytes=62 * 2**20),
        cost_estimate=pl.CostEstimate(
            flops=2 * 512 * 2048 * 2 * tokens, bytes_accessed=24 * 2**20, transcendentals=0
        ),
    )(meta, *row_bufs, *first_bufs, *second_bufs, *([other] if own else []))


def dot_t(a, b):
    return lax.dot_general(
        a, b, (((0,), (0,)), ((), ())), precision=HIGHEST, preferred_element_type=jnp.float32
    )


def dot_n(a, b):
    return lax.dot_general(
        a, b, (((1,), (0,)), ((), ())), precision=HIGHEST, preferred_element_type=jnp.float32
    )


def sums_kernel(meta, own, other, mine_ref, away_ref, sums):
    def dot(p, q):
        return lax.dot_general(
            p[0], q[0], (((1,), (1,)), ((), ())), preferred_element_type=jnp.float32
        )

    @pl.when(meta[26] == 0)
    def _():
        sums[:256] = dot(own, own)
        sums[256:512] = dot(own, other)
        sums[512:] = dot(other, other)

    @pl.when(meta[26] != 0)
    def _():
        sums[:256] = dot(other, other)
        sums[256:512] = dot(other, own)
        sums[512:] = dot(own, own)

    mine_ref[...] = sums[pl.ds(pl.multiple_of(meta[24] * 384, 128), 384), :]
    away_ref[...] = sums[pl.ds(pl.multiple_of((1 - meta[24]) * 384, 128), 384), :]


def leading_sums(meta, own, other):
    full = pl.BlockSpec(memory_space=pltpu.VMEM)
    return pl.pallas_call(
        sums_kernel,
        out_shape=(jax.ShapeDtypeStruct((384, 256), jnp.float32),) * 2,
        in_specs=[pl.BlockSpec(memory_space=pltpu.SMEM), full, full],
        out_specs=(full, full),
        scratch_shapes=[pltpu.VMEM((768, 256), jnp.float32)],
        compiler_params=pltpu.CompilerParams(vmem_limit_bytes=32 * 2**20),
        cost_estimate=pl.CostEstimate(flops=2**30, bytes_accessed=2**20, transcendentals=0),
    )(meta, own, other)


def factor_block(k, work, u_ref, inv_ref, block):
    n, nb, np_ = 512, 128, 16
    lo, hi = k * nb, (k + 1) * nb
    sub = lax.broadcasted_iota(jnp.int32, (np_, nb), 0)
    sub2 = lax.broadcasted_iota(jnp.int32, (np_, 2 * nb), 0)
    lane2 = lax.broadcasted_iota(jnp.int32, (np_, 2 * nb), 1)
    block[:, :nb] = work[lo:hi, lo:hi]
    block[:, nb:] = (
        lax.broadcasted_iota(jnp.int32, (nb, nb), 0) == lax.broadcasted_iota(jnp.int32, (nb, nb), 1)
    ).astype(jnp.float32)
    for base in range(0, nb, np_):
        end = base + np_
        v = block[base:end, :]
        pc = [jnp.broadcast_to(v[:, base + i:base + i + 1], (np_, nb)) for i in range(np_)]
        for i in range(np_):
            s = lax.rsqrt(pc[i][i:i + 1, :])
            below = jnp.where(sub > i, pc[i] * s, 0.0)
            for j in range(i + 1, np_):
                pc[j] = pc[j] - below * (pc[j][i:i + 1, :] * s)
            u = v[i:i + 1, :] * jnp.concatenate([s, s], 1)
            v = jnp.where(sub2 == i, u, v - jnp.concatenate([below, below], 1) * u)
        v = jnp.where(lane2 >= base + sub2, v, 0.0)
        block[base:end, :] = v
        if end < nb:
            block[end:, :] -= dot_t(v[:, :nb], v)[end:]
    x = block[:, nb:]
    u_ref[lo:hi, lo:hi] = block[:, :nb]
    inv_ref[lo:hi, lo:hi] = x
    if k:
        inner = dot_t(u_ref[0:lo, lo:hi], inv_ref[0:lo, 0:lo])
        inv_ref[lo:hi, 0:lo] = -dot_n(x, inner)
    if hi < n:
        right = dot_n(x, work[lo:hi, hi:n])
        u_ref[lo:hi, hi:n] = right
        work[hi:n, hi:n] -= dot_t(right, right)


def factor_first(scale, sums, work, u_ref, inv_ref, block):
    rid = lax.broadcasted_iota(jnp.int32, (256, 256), 0)
    cid = lax.broadcasted_iota(jnp.int32, (256, 256), 1)

    def regular(part):
        return jnp.where(rid == cid, part * scale, reg_alpha * (part * scale))

    work[...] = jnp.zeros((512, 512), jnp.float32)
    work[:256, :256] = regular(sums[:256])
    work[:256, 256:] = reg_alpha * (sums[256:512] * scale)
    work[256:, 256:] = regular(sums[512:])
    u_ref[...] = jnp.zeros((512, 512), jnp.float32)
    inv_ref[...] = jnp.zeros((512, 512), jnp.float32)
    for k in (0, 1):
        factor_block(k, work, u_ref, inv_ref, block)


def factor_second(work_ref, u_in, inv_in, u_ref, inv_ref, work, block):
    work[...] = work_ref[...]
    u_ref[...] = u_in[...]
    inv_ref[...] = inv_in[...]
    for k in (2, 3):
        factor_block(k, work, u_ref, inv_ref, block)


def factor_part(kernel, n_out, args):
    full = pl.BlockSpec(memory_space=pltpu.VMEM)
    shape = jax.ShapeDtypeStruct((512, 512), jnp.float32)
    small = pltpu.VMEM((128, 256), jnp.float32)
    return pl.pallas_call(
        kernel,
        out_shape=(shape,) * n_out,
        in_specs=[full] * len(args),
        out_specs=(full,) * n_out,
        scratch_shapes=[pltpu.VMEM((512, 512), jnp.float32)] * (3 - n_out) + [small],
        compiler_params=pltpu.CompilerParams(vmem_limit_bytes=32 * 2**20),
        cost_estimate=pl.CostEstimate(flops=2**20, bytes_accessed=2**20, transcendentals=512),
    )(*args)


def per_device(acts_one, acts_two):
    cal, row, z = (lax.axis_index(a) for a in AXES)
    low, core = cal // 2, cal % 2
    total_tokens = 8 * acts_one.shape[0]
    scale = 1.0 / total_tokens
    device = (cal * 8 + row) * 8 + z
    meta = lax.dynamic_index_in_dim(jnp.asarray(TABLE), device, 0, keepdims=False)
    after = lax.optimization_barrier
    root = lambda x, y, z: (x // 2, y) == (0, 0) and z < 2

    row_start = row * 2048 + cal * 512
    meta = meta.at[25].set(row_start).at[26].set(z * 256)

    piece = jnp.concatenate([acts_one.T, acts_two.T], 1)[None]
    other = move(piece, lambda x, y, z, c: (x, y, 1 - z, c) if root(x, y, z) else None)
    r0 = move(piece, row_home)
    r01 = jnp.concatenate([r0, move(r0, z_step(0))], 0)
    a0, b0 = acts_one[None], acts_two[None]
    a01 = jnp.concatenate([a0, move(a0, x_step(0))], 0)
    b01 = jnp.concatenate([b0, move(b0, y_step(0))], 0)
    first = jnp.concatenate([a01, move(a01, x_step(1))], 0)
    second = jnp.concatenate([b01, move(b01, y_step(1))], 0)
    lead, away = leading_sums(meta, piece, other)
    lead = lead + move(away, lambda x, y, z, c: (x, y, z, 1 - c) if root(x, y, z) else None)
    r01, first, second, lead = after((r01, first, second, lead))

    r2 = move(r01, z_step(1))
    first1 = move(first, y_step(0))
    lead = lead + move(lead, lambda x, y, z, c: (x ^ 1, y, z, c) if root(x, y, z) else None)
    lead = jnp.where(row == 0, lead, 0.0)
    lead = lead + move(lead, lambda x, y, z, c: (x + 2, y, z, c) if root(x, y, z) else None)
    lead, second = after((lead, second))
    second1 = move(second, x_step(0))
    lead, first1 = after((lead, first1))

    r3 = move(r2, z_step(2))
    r4 = move(r3, z_step(3))
    lead = lead + move(lead, lambda x, y, z, c: (x, 1, z, c) if y == 0 and z < 2 else None)
    lead = lead + move(lead, lambda x, y, z, c: (x, 3 - y, z, c) if y < 2 and z < 2 else None)
    lead, first = after((lead, first))
    first2 = move(first, y_step(1))
    second, second1 = after((second, second1))
    second2 = move(second, x_step(1))
    theirs = move(lead, lambda x, y, z, c: (x, y, z, 1 - c) if z < 2 else None)
    lead = jnp.where(core == 0, jnp.stack([lead, theirs]), jnp.stack([theirs, lead]))
    state = factor_part(functools.partial(factor_first, scale), 3, (lead.reshape(768, 256),))

    first1, first2 = after((first1, first2))
    first3 = move(first1, y_step(1))
    second1, second2 = after((second1, second2))
    second3 = move(second1, x_step(1))
    upper, inverse = factor_part(factor_second, 2, state)
    pieces, upper, inverse = after(
        (
            (
                (r01, r2, r3, r4),
                (first, first1, first2, first3),
                (second, second1, second2, second3),
            ),
            upper,
            inverse,
        )
    )

    theirs, block, away = gram_part(scale, meta, *pieces)
    away = move(away, lambda x, y, z, c: (x, y, z, 1 - c) if z < 2 else None)
    away, theirs = after((away, theirs))
    theirs = move(theirs, core_swap)
    block = (block + away) * scale
    row_ids = row_start + jnp.arange(512, dtype=jnp.int32)[:, None]
    col_ids = z * 256 + jnp.arange(256, dtype=jnp.int32)[None, :]
    block = jnp.where(row_ids == col_ids, block, reg_alpha * block)

    edge = z == 0
    solved = lax.dot_general(
        jnp.where(edge, inverse[:, :256], inverse[:, 256:]), block, (((1,), (1,)), ((), ())),
        precision=HIGHEST, preferred_element_type=jnp.float32,
    )
    head = jnp.where(edge, upper, 0.0)
    solved = jnp.where((row == 0) & (cal == 0), head, solved).reshape(4, 128, 512)
    parts = [jnp.where(edge, solved[0], 0.0)]
    for i in range(3):
        def target(x, y, z, c, i=i):
            if z == 0:
                return x, y, 2 * i + 2, c
            return (x, y, 2 * i + 4, c) if z == 1 and i < 2 else None

        value = jnp.where(edge, solved[i + 1], solved[i + 2]) if i < 2 else solved[3]
        parts.append(move(value, target))
    (gram_reg,) = gram_part(scale, meta, *pieces, other=theirs)
    gram_reg, parts = after((gram_reg, parts))
    share = functools.reduce(jnp.add, parts)
    odd = move(share[64:], lambda x, y, z, c: (x, y, z + 1, c) if z % 2 == 0 else None)
    share = jnp.where(z % 2 == 0, share[:64], odd)
    return gram_reg.reshape(1, 512, 8, 1, 256), share.T.reshape(1, 512, 64)


def solution(mesh):
    return jax.shard_map(
        per_device,
        mesh=mesh,
        in_specs=(P("cal", ("row", "col")), P("cal", ("row", "col"))),
        out_specs=(P("row", "cal", None, "col", None), P("row", "cal", "col")),
        check_vma=False,
    )
```
